32 devices in a mesh: dp: 4 (over y, x), fsdp: 8 (over z, core).
Axes of the slice: x: 2, y: 2, z: 4, core: 2. Of those that a mesh axis runs over, the one named last changes fastest.
Arguments:
- latents: float32 [2, 96, 4096], P(None, ('dp', 'fsdp')), may hold values from -6 to 6
- noise: float32 [2, 96, 4096], P(None, ('dp', 'fsdp')), may hold values from -6 to 6
- timesteps: int32 [2, 96], P(None, ('dp', 'fsdp')), may hold values from 1 to 999
- labels: int32 [2, 96], P(None, ('dp', 'fsdp')), may hold values from 0 to 999
- patch_mask: int32 [2, 96, 256], P(None, ('dp', 'fsdp')), may hold values from 0 to 1, as said below
- counts: int32 [2, 32], P(None, ('dp', 'fsdp')), may hold values from 0 to 3, as said below
- owners: int32 [3], replicated, may hold values from 0 to 3, as said below
- tables_w: float32 [384, 1273], P('fsdp')
- tables_m: float32 [384, 1273], P('fsdp'), may hold values from -1.1920929e-06 to 1.1920929e-06
- tables_v: float32 [384, 1273], P('fsdp'), may hold values from 2.807061e-15 to 1.1228244e-14
- rows_w: float32 [384, 17312], P('fsdp')
- rows_m: float32 [384, 17312], P('fsdp'), may hold values from -1.1920929e-06 to 1.1920929e-06
- rows_v: float32 [384, 17312], P('fsdp'), may hold values from 2.807061e-15 to 8.9825953e-14
- down_w: float32 [384, 4608], P('fsdp'), may hold values from -0.15625 to 0.15625
- down_m: float32 [384, 4608], P('fsdp'), may hold values from -1.1920929e-06 to 1.1920929e-06
- down_v: float32 [384, 4608], P('fsdp'), may hold values from 2.807061e-15 to 1.1228244e-14
Outputs:
- loss: float32 [], replicated
- grad_norm: float32 [], replicated
- tables_w_new: float32 [384, 1273], P('fsdp')
- tables_m_new: float32 [384, 1273], P('fsdp')
- tables_v_new: float32 [384, 1273], P('fsdp')
- rows_w_new: float32 [384, 17312], P('fsdp', 'dp')
- rows_m_new: float32 [384, 17312], P('fsdp', 'dp')
- rows_v_new: float32 [384, 17312], P('fsdp', 'dp')
- down_w_new: float32 [384, 4608], P('fsdp', 'dp')
- down_m_new: float32 [384, 4608], P('fsdp', 'dp')
- down_v_new: float32 [384, 4608], P('fsdp', 'dp')
The draws below stay inside these ranges and needn't reach their ends.
Inputs may be any that keep to these rules, and one draw needn't show every extreme that they name: `counts`: A device uses the first entries of its 3 slots; in each micro-batch some device uses all 3. `owners`: three distinct dp indices, for the groups tables, rows and down in that order. `patch_mask`: each latent has exactly 76 masked tokens.
All inputs are finite; a program needn't handle non-finite values.
Results may differ from the reference program's by a relative error of at most 0.019.
Values may be sent and summed in bfloat16 or wider, within the bound.
No kernel may reach another device: no remote copies, remote signals or barrier semaphores. Data moves between devices by JAX's collectives and lax.ppermute only.
A program may use at most 216 MiB of HBM per device.

```python
import math
import jax
import jax.numpy as jnp
from jax import lax

D = 384
HEADS = 6
HDIM = 64
FF = 1536
NTOK = 256
PIN = 16
FREQ = 256
CLASSES = 1000
TSTEPS = 1000
STEP = 10
MICRO = 2
SLOTS = 3
MASKED = 76
POUT = 32
RANKS = 32
COPIES = 4
LATS = 96
TABROWS = 1273
WIDE = 17312
NPARAM = 8906112


def scaled_noise(key, shape_in):
    return jax.random.normal(key, shape_in, jnp.float32)


def draw_counts(key, part):
    base_counts = jax.random.randint(key, (MICRO, RANKS), 0, SLOTS + 1)
    picked = jax.random.randint(jax.random.fold_in(key, 7), (MICRO,), 0, RANKS)
    is_full = jnp.arange(RANKS)[None, :] == picked[:, None]
    return jnp.where(is_full, SLOTS, base_counts).astype(jnp.int32)


def draw_owners(key, part):
    return jax.random.permutation(key, COPIES)[:3].astype(jnp.int32)


def draw_patch_mask(key, part):
    row_keys = jax.random.split(key, MICRO * LATS)
    orders = jax.vmap(lambda row_key: jax.random.permutation(row_key, NTOK))(row_keys)
    return (orders < MASKED).astype(jnp.int32).reshape(MICRO, LATS, NTOK)


def draw_tables_w(key, part):
    col_ids = jnp.arange(TABROWS)[None, :]
    col_scale = jnp.where(col_ids < PIN, PIN ** (-0.5), jnp.where(col_ids == PIN, 1.0, jnp.where(col_ids < PIN + 1 + FREQ, FREQ ** (-0.5), 0.02)))
    return scaled_noise(key, (D, TABROWS)) * col_scale.astype(jnp.float32)


def draw_rows_w(key, part):
    col_ids = jnp.arange(WIDE)[None, :]
    stride = 10 * D + FF
    offset = (col_ids - D) % stride
    in_blocks = (col_ids >= D) & (col_ids < D + 3 * stride)
    is_out = in_blocks & (offset >= 3 * D) & (offset < 4 * D)
    col_scale = jnp.where(col_ids < D, 2.0, jnp.where(is_out, 4.0, 1.0)) * D ** (-0.5)
    return scaled_noise(key, (D, WIDE)) * col_scale.astype(jnp.float32)


def draw_rows_v(key, part):
    key = jax.random.fold_in(key, 11)
    low_end = 2.5e-08 / NPARAM
    high_end = 1e-07 / NPARAM
    expo = jax.random.uniform(key, (D, WIDE), jnp.float32, jnp.log(low_end), jnp.log(high_end))
    return jnp.clip(jnp.exp(expo), low_end, high_end).astype(jnp.float32)


def touch_ends(result, rng, least, largest):
    extent = result.shape
    spot = [jax.random.randint(jax.random.fold_in(rng, axis), (), 0, extent[axis]) for axis in range(len(extent))]
    result = result.at[tuple(spot)].set(least)
    longest = extent.index(max(extent))
    spot[longest] = (spot[longest] + 1) % extent[longest]
    return result.at[tuple(spot)].set(largest)


def steps_of(own_key, shape, shards, least, high):
    gain = 1.0
    for axis_at, shards_of in shards:
        draws = jax.random.uniform(jax.random.fold_in(jax.random.fold_in(own_key, 6), axis_at), (shards_of,), jnp.float32, least / len(shards), high / len(shards))
        gain = gain * jnp.repeat(jnp.exp(draws), shape[axis_at] // shards_of).reshape((-1,) + (1,) * (len(shape) - 1 - axis_at))
    return gain


def bell_draw(stream_key, dims, deviation, limit, cuts=(), kind=jnp.bfloat16):
    drawn = deviation * jax.random.normal(stream_key, dims, jnp.float32)
    if cuts:
        drawn = drawn * steps_of(stream_key, dims, cuts, -0.22, 0.18)
    return jnp.clip(drawn, -limit, limit).astype(kind)


def setup_inputs(seed: int = 0) -> dict:
    splits = jax.random.split(jax.random.key(seed), 17)
    return {
        "latents": bell_draw(splits[0], (MICRO, LATS, NTOK * PIN), 1.0, 6.0, ((1, 32),), jnp.float32),
        "noise": bell_draw(splits[1], (MICRO, LATS, NTOK * PIN), 1.0, 6.0, ((1, 32),), jnp.float32),
        "timesteps": touch_ends(jax.random.randint(splits[2], (MICRO, LATS), 1, TSTEPS), jax.random.fold_in(splits[2], 1), 1, TSTEPS - 1).astype(jnp.int32),
        "labels": touch_ends(jax.random.randint(splits[3], (MICRO, LATS), 0, CLASSES), jax.random.fold_in(splits[3], 1), 0, CLASSES - 1).astype(jnp.int32),
        "patch_mask": draw_patch_mask(jax.random.fold_in(splits[16], 71), 0),
        "counts": draw_counts(jax.random.fold_in(splits[16], 71), 0),
        "owners": draw_owners(jax.random.fold_in(splits[16], 71), 0),
        "tables_w": draw_tables_w(jax.random.fold_in(splits[16], 71), 0),
        "tables_m": bell_draw(splits[8], (D, TABROWS), (0.000555 / NPARAM ** 0.5), 1.1920928955078125e-06, ((0, 8),), jnp.float32),
        "tables_v": jnp.clip(jnp.exp(math.log(1.1228244184847535e-14) - 1.3862944 * jax.random.uniform(splits[9], (D, TABROWS), jnp.float32) ** steps_of(splits[9], (D, TABROWS), ((0, 8),), -0.2, 0.2)), 2.8070610462118837e-15, 1.1228244184847535e-14),
        "rows_w": draw_rows_w(jax.random.fold_in(splits[16], 71), 0),
        "rows_m": bell_draw(splits[11], (D, WIDE), (0.000555 / NPARAM ** 0.5), 1.1920928955078125e-06, ((0, 8),), jnp.float32),
        "rows_v": draw_rows_v(jax.random.fold_in(splits[16], 71), 0),
        "down_w": bell_draw(splits[13], (D, 3 * FF), FF ** -0.5, 0.15625, ((0, 8),), jnp.float32),
        "down_m": bell_draw(splits[14], (D, 3 * FF), (0.000555 / NPARAM ** 0.5), 1.1920928955078125e-06, ((0, 8),), jnp.float32),
        "down_v": jnp.clip(jnp.exp(math.log(1.1228244184847535e-14) - 1.3862944 * jax.random.uniform(splits[15], (D, 3 * FF), jnp.float32) ** steps_of(splits[15], (D, 3 * FF), ((0, 8),), -0.2, 0.2)), 2.8070610462118837e-15, 1.1228244184847535e-14),
    }


@jax.custom_vjp
def low(v):
    return lax.optimization_barrier(v.astype(jnp.bfloat16)).astype(jnp.float32)

@jax.custom_vjp
def low_back(v):
    return v

def low_keep(v):
    return (low(v), None)

def low_pass(kept, grad):
    return (grad,)

def back_keep(v):
    return (v, None)

def back_low(kept, grad):
    return (low(grad),)
low.defvjp(low_keep, low_pass)
low_back.defvjp(back_keep, back_low)
beta_one = 0.9
beta_two = 0.999
adam_eps = 1e-08
learn_rate = 0.05
weight_decay = 0.1
clip_level = 0.005
ln_eps = 1e-06
highest = lax.Precision.HIGHEST

def plan():
    t_steps = jnp.arange(TSTEPS).astype(jnp.float32)
    beta_all = 0.0001 + (0.02 - 0.0001) * t_steps / (TSTEPS - 1)
    return (beta_all, jnp.cumprod(1.0 - beta_all))

def position_table():
    half_width = D // 2
    rates_t = jnp.exp(-math.log(10000.0) * 2.0 * jnp.arange(half_width).astype(jnp.float32) / D)
    angles = jnp.arange(NTOK).astype(jnp.float32)[:, None] * rates_t[None, :]
    return jnp.concatenate([jnp.sin(angles), jnp.cos(angles)], axis=1)

def time_features(t_steps):
    half_width = FREQ // 2
    rates_t = jnp.exp(-math.log(10000.0) * jnp.arange(half_width).astype(jnp.float32) / half_width)
    angles = t_steps.astype(jnp.float32)[:, None] * rates_t[None, :]
    return jnp.concatenate([jnp.cos(angles), jnp.sin(angles)], axis=1)

def modulate(hidden, shift_v, scale_v):
    mean_v = lax.optimization_barrier(jnp.mean(hidden, axis=-1, keepdims=True))
    centred = hidden - mean_v
    var_v = lax.optimization_barrier(jnp.mean(centred * centred, axis=-1, keepdims=True))
    normed = centred * lax.rsqrt(var_v + ln_eps)
    return normed * (1.0 + scale_v[:, None, :]) + shift_v[:, None, :]

def loss_terms(head_out, noise, t_steps, weight, beta_all, abar_all):
    abar_t = abar_all[t_steps][:, None, None]
    abar_prev = abar_all[t_steps - 1][:, None, None]
    beta_t = beta_all[t_steps][:, None, None]
    post_log = jnp.log(beta_t * (1.0 - abar_prev) / (1.0 - abar_t))
    mean_w = abar_prev * beta_t * beta_t / ((1.0 - abar_t) * abar_t)
    eps_diff = head_out[..., :PIN] - noise
    var_frac = (head_out[..., PIN:] + 1.0) / 2.0
    log_var = var_frac * jnp.log(beta_t) + (1.0 - var_frac) * post_log
    kl_term = 0.5 * (-1.0 + log_var - post_log + jnp.exp(post_log - log_var) + mean_w * eps_diff * eps_diff * jnp.exp(-log_var)) / math.log(2.0)
    per_sample = lax.optimization_barrier(jnp.sum(eps_diff * eps_diff + kl_term, axis=(1, 2)))
    return jnp.sum(per_sample * weight)

def split_weights(tables, row_block, down_block):
    tab_rows = tables.T
    w_patch = tab_rows[:PIN]
    mask_token = tab_rows[PIN]
    w_tone = tab_rows[PIN + 1:PIN + 1 + FREQ]
    class_tab = tab_rows[PIN + 1 + FREQ:]
    w_ttwo = row_block[:, :D]
    col_start = D
    block_list = []
    for block_idx in range(3):
        w_qkv = row_block[:, col_start:col_start + 3 * D]
        w_out = row_block[:, col_start + 3 * D:col_start + 4 * D]
        w_up = row_block[:, col_start + 4 * D:col_start + 4 * D + FF]
        w_ada = row_block[:, col_start + 4 * D + FF:col_start + 10 * D + FF]
        w_down = down_block[:, block_idx * FF:(block_idx + 1) * FF].T
        block_list.append((w_qkv, w_out, w_up, w_ada, w_down))
        col_start = col_start + 10 * D + FF
    w_fin = row_block[:, col_start:col_start + 2 * D]
    w_head = row_block[:, col_start + 2 * D:col_start + 2 * D + POUT]
    return (w_patch, mask_token, w_tone, class_tab, w_ttwo, block_list, w_fin, w_head)

def dense_mul(left_op, right_op):
    return jnp.dot(left_op, right_op, precision=highest)

def ref_block(hidden, s_cond, block_w, key_bias):
    w_qkv, w_out, w_up, w_ada, w_down = block_w
    samples = hidden.shape[0]
    ada_mod = low_back(dense_mul(s_cond, w_ada))
    shift_one, scale_one, gate_one, shift_two, scale_two, gate_two = jnp.split(ada_mod, 6, axis=1)
    n_one = low(modulate(hidden, shift_one, scale_one)).reshape(-1, D)
    qkv_all = low(low_back(dense_mul(n_one, w_qkv))).reshape(samples, NTOK, 3, HEADS, HDIM)
    scores = low_back(jnp.einsum('snhd,smhd->shnm', qkv_all[:, :, 0], qkv_all[:, :, 1], precision=highest) / math.sqrt(HDIM)) + key_bias
    row_top = lax.optimization_barrier(jnp.max(scores, axis=-1, keepdims=True))
    expo_vals = jnp.exp(scores - row_top)
    attn_prob = low(expo_vals / lax.optimization_barrier(jnp.sum(expo_vals, axis=-1, keepdims=True)))
    attn_out = low(low_back(jnp.einsum('shnm,smhd->snhd', attn_prob, qkv_all[:, :, 2], precision=highest))).reshape(-1, D)
    attn_res = low_back(dense_mul(attn_out, w_out)).reshape(samples, NTOK, D)
    h_two = hidden + gate_one[:, None, :] * attn_res
    n_two = low(modulate(h_two, shift_two, scale_two)).reshape(-1, D)
    up_act = low(jax.nn.gelu(low_back(dense_mul(n_two, w_up)), approximate=True))
    mlp_out = low_back(dense_mul(up_act, w_down)).reshape(samples, NTOK, D)
    return h_two + gate_two[:, None, :] * mlp_out

def group_loss(pieces, pos_table, beta_all, abar_all, batch_data):
    w_patch, mask_token, w_tone, class_tab, w_ttwo, block_list, w_fin, w_head = pieces
    x_zero, noise, t_steps, label_ids, mask_ids, weight = batch_data
    samples = x_zero.shape[0]
    abar_t = abar_all[t_steps][:, None]
    x_in = low(jnp.sqrt(abar_t) * x_zero + jnp.sqrt(1.0 - abar_t) * noise).reshape(samples * NTOK, PIN)
    h_patch = low_back(dense_mul(x_in, w_patch)).reshape(samples, NTOK, D)
    mask_f = mask_ids.astype(jnp.float32)[:, :, None]
    key_bias = (-1000000000.0 * mask_ids.astype(jnp.float32))[:, None, None, :]
    h_zero = h_patch + pos_table[None]
    t_feat = low(time_features(t_steps))
    a_act = low(jax.nn.silu(low_back(dense_mul(t_feat, w_tone))))
    cond_vec = low_back(dense_mul(a_act, w_ttwo)) + class_tab[label_ids]
    s_cond = low(jax.nn.silu(cond_vec))
    fin_mod = low_back(dense_mul(s_cond, w_fin))
    h_enc = ref_block(h_zero, s_cond, block_list[0], key_bias)
    h_side_in = h_enc * (1.0 - mask_f) + mask_f * (mask_token[None, None, :] + pos_table[None])
    h_side = ref_block(h_side_in, s_cond, block_list[1], 0.0)
    h_dec = ref_block(h_side, s_cond, block_list[2], 0.0)
    shift_fin, scale_fin = jnp.split(fin_mod, 2, axis=1)
    n_fin = low(modulate(h_dec, shift_fin, scale_fin)).reshape(-1, D)
    head_out = low_back(dense_mul(n_fin, w_head)).reshape(samples, NTOK, POUT)
    return loss_terms(head_out, noise.reshape(samples, NTOK, PIN), t_steps, weight, beta_all, abar_all)

def adam_step(master, first_m, second, grad_in):
    first_new = beta_one * first_m + (1.0 - beta_one) * grad_in
    second_new = beta_two * second + (1.0 - beta_two) * grad_in * grad_in
    first_hat = first_new / (1.0 - beta_one ** STEP)
    second_hat = second_new / (1.0 - beta_two ** STEP)
    master_new = master - learn_rate * (first_hat / (jnp.sqrt(second_hat) + adam_eps) + weight_decay * master)
    return (master_new, first_new, second_new)

def reference(latents, noise, timesteps, labels, patch_mask, counts, owners, tables_w, tables_m, tables_v, rows_w, rows_m, rows_v, down_w, down_m, down_v):
    beta_all, abar_all = plan()
    pos_table = position_table()
    count_total = jnp.sum(counts.astype(jnp.float32))
    valid_slot = (jnp.arange(LATS)[None, :] % SLOTS < jnp.repeat(counts, SLOTS, axis=1)).astype(jnp.float32)
    weight = valid_slot / (count_total * NTOK * PIN)
    group_size = math.gcd(MICRO * LATS, 16)
    blocks = MICRO * LATS // group_size

    def regroup(array_in):
        return array_in.reshape((blocks, group_size) + array_in.shape[2:])
    batch_data = (regroup(latents), regroup(noise), regroup(timesteps), regroup(labels), regroup(patch_mask), regroup(weight))
    checked = jax.checkpoint(group_loss)

    def total_loss(tables, row_block, down_block):
        pieces = split_weights(low(tables), low(row_block), low(down_block))

        def scan_step(carry_sum, batch_part):
            return (carry_sum + checked(pieces, pos_table, beta_all, abar_all, batch_part), None)
        loss_sum, _ = lax.scan(scan_step, jnp.zeros((), jnp.float32), batch_data)
        return loss_sum
    loss_sum, loss_pull = jax.vjp(total_loss, tables_w, rows_w, down_w)
    gradients = loss_pull(jnp.ones((), jnp.float32))
    grad_norm = jnp.sqrt(jnp.sum(gradients[0] ** 2) + jnp.sum(gradients[1] ** 2) + jnp.sum(gradients[2] ** 2))
    factor = jnp.minimum(1.0, clip_level / (grad_norm + 1e-06))
    tab_new = adam_step(tables_w, tables_m, tables_v, factor * gradients[0])
    row_new = adam_step(rows_w, rows_m, rows_v, factor * gradients[1])
    down_new = adam_step(down_w, down_m, down_v, factor * gradients[2])
    return (loss_sum, grad_norm, tab_new[0], tab_new[1], tab_new[2], row_new[0], row_new[1], row_new[2], down_new[0], down_new[1], down_new[2])
```

```python
import functools
import math

import jax
import jax.numpy as jnp
import numpy as np
from jax import lax
from jax.experimental import pallas as pl
from jax.experimental.pallas import tpu as pltpu
from jax.sharding import PartitionSpec as P

D = 384
HEADS = 6
HDIM = 64
FF = 1536
NTOK = 256
PIN = 16
FREQ = 256
CLASSES = 1000
TSTEPS = 1000
STEP = 10
POUT = 32

beta_one = 0.9
beta_two = 0.999
adam_eps = 1e-08
learn_rate = 0.05
weight_decay = 0.1
clip_level = 0.005
ln_eps = 1e-06

F32 = jnp.float32
BF16 = jnp.bfloat16
STRIDE = 10 * D + FF
TOKW = 3 * D + D + FF + FF
CHUNKS = 4
CW = TOKW // CHUNKS
GELU_C = math.sqrt(2.0 / math.pi)
VMEM_LIMIT = 60 * 1024 * 1024


def plan_table():
    j = np.arange(TSTEPS, dtype=np.float64)
    beta = 0.0001 + (0.02 - 0.0001) * j / (TSTEPS - 1)
    abar = np.cumprod(1.0 - beta)
    prev = np.concatenate([[1.0], abar[:-1]])
    out = np.zeros((TSTEPS, 8), np.float64)
    out[:, 0] = np.sqrt(abar)
    out[:, 1] = np.sqrt(1.0 - abar)
    out[1:, 2] = np.log(beta[1:])
    out[1:, 3] = np.log(beta[1:] * (1.0 - prev[1:]) / (1.0 - abar[1:]))
    out[1:, 4] = prev[1:] * beta[1:] ** 2 / ((1.0 - abar[1:]) * abar[1:])
    return out.astype(np.float32)


def position_table():
    half = D // 2
    rates = np.exp(-math.log(10000.0) * 2.0 * np.arange(half) / D)
    angles = np.arange(NTOK)[:, None] * rates[None, :]
    return np.concatenate([np.sin(angles), np.cos(angles)], axis=1).astype(np.float32)


def time_features(steps):
    half = FREQ // 2
    rates = jnp.exp(-math.log(10000.0) * jnp.arange(half).astype(F32) / half)
    angles = steps.astype(F32)[:, None] * rates[None, :]
    return jnp.concatenate([jnp.cos(angles), jnp.sin(angles)], axis=1)


def stages(size, pair_first):
    out, stride = [], 1
    if pair_first and size % 2 == 0:
        out.append((1, 2))
        stride, size = 2, size // 2
    while size > 1:
        step = 4 if size % 4 == 0 else 2
        out.append((stride, step))
        stride, size = stride * step, size // step
    return out


def axis_stages(axis):
    return stages(lax.axis_size(axis), axis == "fsdp")


def swap(val, axis, mask):
    size = lax.axis_size(axis)
    return lax.ppermute(val, axis, [(i, i ^ mask) for i in range(size)])


def place(axis, stride, size):
    return (lax.axis_index(axis) // stride) % size


def in_order(parts, pos):
    size = len(parts)
    return jnp.stack([lax.select_n(pos, *[parts[j ^ p] for p in range(size)]) if size > 2 else lax.select(pos == 1, parts[j ^ 1], parts[j]) for j in range(size)])


def gather(val, axis):
    plan = axis_stages(axis)
    shape = val.shape
    for stride, size in reversed(plan):
        parts = [val] + [swap(val, axis, k * stride) for k in range(1, size)]
        val = in_order(parts, place(axis, stride, size))
    n = len(plan)
    order = tuple(reversed(range(n))) + tuple(range(n, n + len(shape)))
    return val.transpose(order).reshape((lax.axis_size(axis),) + shape)


def reduce_parts(val, axis, send_type):
    plan = axis_stages(axis)
    sizes = [s for _, s in reversed(plan)]
    val = val.reshape(tuple(sizes) + val.shape[1:])
    dim = len(sizes)
    for stride, size in plan:
        dim -= 1
        pos = place(axis, stride, size)
        total = lax.dynamic_index_in_dim(val, pos, dim, keepdims=False).astype(F32)
        for k in range(1, size):
            piece = lax.dynamic_index_in_dim(val, pos ^ k, dim, keepdims=False)
            total = total + swap(piece.astype(send_type), axis, k * stride).astype(F32)
        val = total
    return val


def sum_all(val):
    for axis in ("fsdp", "dp"):
        for stride, size in axis_stages(axis):
            parts = [val] + [swap(val, axis, k * stride) for k in range(1, size)]
            while len(parts) > 1:
                parts = [parts[i] + parts[i + 1] for i in range(0, len(parts), 2)]
            val = parts[0]
    return val


def gather_block(chunk, whole):
    rows = chunk.shape[0]
    if rows % 16 or lax.axis_size("dp") != CHUNKS or lax.axis_size("fsdp") != 8:
        full = lax.all_gather(whole, "fsdp", axis=0, tiled=True)
        full = full.reshape(D, CHUNKS, CW).transpose(1, 0, 2)
        return [full.reshape(CHUNKS, 4, 2, D // 8, CW)]
    parts = [chunk] + [swap(chunk, "fsdp", 2 * k) for k in (1, 2, 3)]
    mine = in_order(parts, place("fsdp", 2, 4))
    mine = [mine] + [swap(mine, "dp", k) for k in (1, 2, 3)]
    other = [swap(v, "fsdp", 1) for v in mine]
    return mine + other


def dot(a, b):
    return jnp.dot(a, b, preferred_element_type=F32)


def dot_nt(a, b):
    return lax.dot_general(a, b, (((1,), (1,)), ((), ())), preferred_element_type=F32)


def dot_tn(a, b):
    return lax.dot_general(a, b, (((0,), (0,)), ((), ())), preferred_element_type=F32)


def layer_norm(v):
    c = v - jnp.mean(v, axis=-1, keepdims=True)
    r = lax.rsqrt(jnp.mean(c * c, axis=-1, keepdims=True) + ln_eps)
    return c * r, r


def norm_grad(dm, y, r, scale):
    dy = dm * (1.0 + scale)
    dv = r * (dy - jnp.mean(dy, axis=-1, keepdims=True) - y * jnp.mean(dy * y, axis=-1, keepdims=True))
    return dv, jnp.sum(dm, axis=0, keepdims=True), jnp.sum(dm * y, axis=0, keepdims=True)


def wpart(w, j, lo, hi):
    return w[j, :, :, :, lo:hi].reshape(D, hi - lo)


def head_masks():
    lane = lax.broadcasted_iota(jnp.int32, (1, 2 * HDIM), 1)
    low = (lane < HDIM).astype(F32)
    return low, 1.0 - low


def block_forward(h, mod, w, bias, sv):
    qkv_ref, p_ref, o_ref, g_ref, gp_ref, att_ref, mlp_ref, h2_ref = sv
    y1, _ = layer_norm(h)
    n1 = (y1 * (1.0 + mod(1)) + mod(0)).astype(BF16)
    qkv_ref[...] = dot(n1, wpart(w, 0, 0, CW)).astype(BF16)
    masks = head_masks()
    for j in range(3):
        q2 = qkv_ref[:, 128 * j : 128 * j + 128]
        k2 = qkv_ref[:, D + 128 * j : D + 128 * j + 128]
        v2 = qkv_ref[:, 2 * D + 128 * j : 2 * D + 128 * j + 128]
        o2 = None
        for a in range(2):
            s = dot_nt(q2, k2 * (masks[a] * 0.125).astype(BF16))
            if bias is not None:
                s = s + bias
            e = jnp.exp(s - jnp.max(s, axis=-1, keepdims=True))
            p = (e * (1.0 / jnp.sum(e, axis=-1, keepdims=True))).astype(BF16)
            p_ref[2 * j + a] = p
            part = dot(p, v2 * masks[a].astype(BF16))
            o2 = part if o2 is None else o2 + part
        o_ref[:, 128 * j : 128 * j + 128] = o2.astype(BF16)
    att = dot(o_ref[...], wpart(w, 1, 0, D))
    att_ref[...] = att.astype(BF16)
    h2 = h + mod(2) * att
    h2_ref[...] = h2
    y2, _ = layer_norm(h2)
    n2 = (y2 * (1.0 + mod(4)) + mod(3)).astype(BF16)
    for j, lo, hi, at in ((1, D, CW, 0), (2, 0, 2 * D, 2 * D)):
        u = dot(n2, wpart(w, j, lo, hi))
        u2 = u * u
        t = jnp.tanh(u * (GELU_C + (GELU_C * 0.044715) * u2))
        half = 0.5 * t + 0.5
        g_ref[:, at : at + 2 * D] = (u * half).astype(BF16)
        gp = half + (u * (0.5 - 0.5 * t * t)) * (GELU_C + (3.0 * GELU_C * 0.044715) * u2)
        gp_ref[:, at : at + 2 * D] = gp.astype(BF16)
    mlp = dot_nt(g_ref[:, 0:D], wpart(w, 2, 2 * D, CW)) + dot_nt(g_ref[:, D:], wpart(w, 3, 0, CW))
    mlp_ref[...] = mlp.astype(BF16)
    return h2 + mod(5) * mlp


def block_backward(d3, h, mod, w, sv, dw, du_ref, dqkv_ref, dmod_ref):
    qkv_ref, p_ref, o_ref, g_ref, gp_ref, att_ref, mlp_ref, h2_ref = sv
    dmlp = (d3 * mod(5)).astype(BF16)
    dmod_ref[5:6, :] = jnp.sum(d3 * mlp_ref[...].astype(F32), axis=0, keepdims=True)
    du_ref[:, 0:D] = (dot(dmlp, wpart(w, 2, 2 * D, CW)) * gp_ref[:, 0:D].astype(F32)).astype(BF16)
    du_ref[:, D:] = (dot(dmlp, wpart(w, 3, 0, CW)) * gp_ref[:, D:].astype(F32)).astype(BF16)
    dw[2, :, 2 * D : CW] += dot_tn(dmlp, g_ref[:, 0:D])
    dw[3] += dot_tn(dmlp, g_ref[:, D:])
    dn2 = dot_nt(du_ref[:, 0 : 2 * D], wpart(w, 1, D, CW)) + dot_nt(du_ref[:, 2 * D :], wpart(w, 2, 0, 2 * D))
    y2, r2 = layer_norm(h2_ref[...])
    n2 = (y2 * (1.0 + mod(4)) + mod(3)).astype(BF16)
    dw[1, :, D:CW] += dot_tn(n2, du_ref[:, 0 : 2 * D])
    dw[2, :, 0 : 2 * D] += dot_tn(n2, du_ref[:, 2 * D :])
    dv, dshift, dscale = norm_grad(dn2, y2, r2, mod(4))
    dmod_ref[3:4, :] = dshift
    dmod_ref[4:5, :] = dscale
    d2 = d3 + dv
    datt = (d2 * mod(2)).astype(BF16)
    dmod_ref[2:3, :] = jnp.sum(d2 * att_ref[...].astype(F32), axis=0, keepdims=True)
    do = dot_nt(datt, wpart(w, 1, 0, D)).astype(BF16)
    dw[1, :, 0:D] += dot_tn(o_ref[...], datt)
    masks = head_masks()
    for j in range(3):
        q2 = qkv_ref[:, 128 * j : 128 * j + 128]
        k2 = qkv_ref[:, D + 128 * j : D + 128 * j + 128]
        v2 = qkv_ref[:, 2 * D + 128 * j : 2 * D + 128 * j + 128]
        do2 = do[:, 128 * j : 128 * j + 128]
        dq2, dk2, dv2 = 0.0, 0.0, 0.0
        for a in range(2):
            one = masks[a].astype(BF16)
            eighth = (masks[a] * 0.125).astype(BF16)
            pb = p_ref[2 * j + a]
            p = pb.astype(F32)
            dp = dot_nt(do2, v2 * one)
            ds = (p * (dp - jnp.sum(p * dp, axis=-1, keepdims=True))).astype(BF16)
            dq2 += dot(ds, k2 * eighth)
            dk2 += dot_tn(ds, q2 * eighth)
            dv2 += dot_tn(pb, do2 * one)
        dqkv_ref[:, 128 * j : 128 * j + 128] = dq2.astype(BF16)
        dqkv_ref[:, D + 128 * j : D + 128 * j + 128] = dk2.astype(BF16)
        dqkv_ref[:, 2 * D + 128 * j : 2 * D + 128 * j + 128] = dv2.astype(BF16)
    dn1 = dot_nt(dqkv_ref[...], wpart(w, 0, 0, CW))
    y1, r1 = layer_norm(h)
    n1 = (y1 * (1.0 + mod(1)) + mod(0)).astype(BF16)
    dw[0] += dot_tn(n1, dqkv_ref[...])
    dv, dshift, dscale = norm_grad(dn1, y1, r1, mod(1))
    dmod_ref[0:1, :] = dshift
    dmod_ref[1:2, :] = dscale
    return d2 + dv


def load_weights(ids, pieces, w, sems):
    @pl.when(pl.program_id(0) == 0)
    def _():
        copies = []
        if len(pieces) == 1:
            copies.append(pltpu.make_async_copy(pieces[0], w, sems.at[0]))
        else:
            for c in range(2):
                for k in range(4):
                    target = w.at[ids[0] ^ k, :, ids[1] ^ c]
                    copies.append(pltpu.make_async_copy(pieces[4 * c + k], target, sems.at[4 * c + k]))
        for copy in copies:
            copy.start()
        for copy in copies:
            copy.wait()


def mod_row(mod_ref):
    return lambda i: mod_ref[i : i + 1, :]


def enc_forward_kernel(n, ids, valid, xin, pe, misc, mod, bias, *rest):
    pieces, (h0, h3), sv, (w, sems) = rest[:n], rest[n : n + 2], rest[n + 2 : n + 10], rest[n + 10 :]
    load_weights(ids, pieces, w, sems)

    @pl.when(valid[pl.program_id(0)] > 0)
    def _():
        h = dot_nt(xin[...], misc[...]) + pe[...]
        h0[...] = h
        h3[...] = block_forward(h, mod_row(mod), w, bias[...], sv)


def token_row(misc):
    lane = lax.broadcasted_iota(jnp.int32, (8, 128), 1)
    return dot_nt((lane == PIN).astype(BF16), misc[...])[0:1, :]


def side_forward_kernel(n, ids, valid, h_in, mask, pe, misc, mod, *rest):
    pieces, (hs, h3), sv, (w, sems) = rest[:n], rest[n : n + 2], rest[n + 2 : n + 10], rest[n + 10 :]
    load_weights(ids, pieces, w, sems)

    @pl.when(valid[pl.program_id(0)] > 0)
    def _():
        m = mask[...]
        h = h_in[...] * (1.0 - m) + m * (token_row(misc) + pe[...])
        hs[...] = h
        h3[...] = block_forward(h, mod_row(mod), w, None, sv)


def store_grads(dw, out):
    for j in range(CHUNKS):
        out[j] = dw[j].astype(BF16)


def dec_kernel(n, ids, valid, coef, h_in, noise, misc, mod, *rest):
    pieces = rest[:n]
    d_in, dmod, dw_out, dmisc, loss = rest[n : n + 5]
    w, sems, dw, du, dqkv = rest[n + 5 : n + 10]
    sv = rest[n + 10 :]
    load_weights(ids, pieces, w, sems)
    step = pl.program_id(0)

    @pl.when(step == 0)
    def _():
        dw[...] = jnp.zeros_like(dw)
        dmisc[...] = jnp.zeros_like(dmisc)
        loss[...] = jnp.zeros_like(loss)

    @pl.when(valid[step] <= 0)
    def _():
        dmod[...] = jnp.zeros_like(dmod)

    @pl.when(valid[step] > 0)
    def _():
        row = mod_row(mod)
        h = h_in[...]
        h_dec = block_forward(h, row, w, None, sv)
        yf, rf = layer_norm(h_dec)
        nf = (yf * (1.0 + row(7)) + row(6)).astype(BF16)
        out = dot(nf, misc[...])
        ln_b, ln_pv, wmean = coef[step, 2], coef[step, 3], coef[step, 4]
        lane = lax.broadcasted_iota(jnp.int32, (1, 128), 1)
        live = (lane >= 32) & (lane < 32 + PIN)
        d = jnp.where(live, out - noise[...], 0.0)
        vf = (pltpu.roll(out, 128 - 32, 1) + 1.0) * 0.5
        vf = jnp.where(live, vf, 0.0)
        lv = vf * ln_b + (1.0 - vf) * ln_pv
        first = jnp.exp(ln_pv - lv)
        second = wmean * jnp.exp(-lv)
        inv = 0.5 / math.log(2.0)
        dd = d * d
        kl = inv * (-1.0 + lv - ln_pv + first + dd * second)
        term = jnp.where(live, dd + kl, 0.0)
        loss[...] += jnp.sum(term.reshape(NTOK // 8, 8, 128), axis=0)
        deps = d * (2.0 + (2.0 * inv) * second)
        dlog = inv * (1.0 - first - dd * second) * (0.5 * (ln_b - ln_pv))
        dlog = jnp.where(live, dlog, 0.0)
        dout = (deps + pltpu.roll(dlog, 32, 1)).astype(BF16)
        dmisc[...] += dot_tn(nf, dout)
        dnf = dot_nt(dout, misc[...])
        d3, dshift, dscale = norm_grad(dnf, yf, rf, row(7))
        dmod[6:7, :] = dshift
        dmod[7:8, :] = dscale
        d_in[...] = block_backward(d3, h, row, w, sv, dw, du, dqkv, dmod)

    @pl.when(step == pl.num_programs(0) - 1)
    def _():
        store_grads(dw, dw_out)


def side_backward_kernel(n, ids, valid, d_out, h_in, mask, mod, *rest):
    sv, pieces, rest = rest[:8], rest[8 : 8 + n], rest[8 + n :]
    d_enc, dmod, dw_out, dtok, w, sems, dw, du, dqkv = rest
    load_weights(ids, pieces, w, sems)
    step = pl.program_id(0)

    @pl.when(step == 0)
    def _():
        dw[...] = jnp.zeros_like(dw)
        dtok[...] = jnp.zeros_like(dtok)

    @pl.when(valid[step] <= 0)
    def _():
        dmod[...] = jnp.zeros_like(dmod)

    @pl.when(valid[step] > 0)
    def _():
        m = mask[...]
        dh = block_backward(d_out[...], h_in[...], mod_row(mod), w, sv, dw, du, dqkv, dmod)
        dm = dh * m
        dtok[...] += jnp.sum(dm.reshape(NTOK // 8, 8, D), axis=0)
        d_enc[...] = dh - dm

    @pl.when(step == pl.num_programs(0) - 1)
    def _():
        store_grads(dw, dw_out)


def enc_backward_kernel(n, ids, valid, d_out, h_in, xin, mod, *rest):
    sv, pieces, rest = rest[:8], rest[8 : 8 + n], rest[8 + n :]
    dmod, dw_out, dmisc, w, sems, dw, du, dqkv = rest
    load_weights(ids, pieces, w, sems)
    step = pl.program_id(0)

    @pl.when(step == 0)
    def _():
        dw[...] = jnp.zeros_like(dw)
        dmisc[...] = jnp.zeros_like(dmisc)

    @pl.when(valid[step] <= 0)
    def _():
        dmod[...] = jnp.zeros_like(dmod)

    @pl.when(valid[step] > 0)
    def _():
        dh = block_backward(d_out[...], h_in[...], mod_row(mod), w, sv, dw, du, dqkv, dmod)
        dmisc[...] += dot_tn(dh.astype(BF16), xin[...])

    @pl.when(step == pl.num_programs(0) - 1)
    def _():
        store_grads(dw, dw_out)


SMEM = pl.BlockSpec(memory_space=pltpu.SMEM)
ANY = pl.BlockSpec(memory_space=pl.ANY)


def slot_spec(*shape):
    return pl.BlockSpec((None,) + shape, lambda s: (s,) + (0,) * len(shape))


def fixed_spec(*shape):
    return pl.BlockSpec(shape, lambda s: (0,) * len(shape))


SAVES = (
    ((NTOK, 3 * D), BF16),
    ((HEADS, NTOK, NTOK), BF16),
    ((NTOK, D), BF16),
    ((NTOK, FF), BF16),
    ((NTOK, FF), BF16),
    ((NTOK, D), BF16),
    ((NTOK, D), BF16),
    ((NTOK, D), F32),
)


def weight_scratch():
    return [pltpu.VMEM((CHUNKS, 4, 2, D // 8, CW), BF16), pltpu.SemaphoreType.DMA((8,))]


def grad_scratch():
    return [
        pltpu.VMEM((CHUNKS, D, CW), F32),
        pltpu.VMEM((NTOK, FF), BF16),
        pltpu.VMEM((NTOK, 3 * D), BF16),
    ]


def call(kernel, slots, in_specs, args, pieces, outs, scratch, macs):
    specs = list(in_specs) + [ANY] * len(pieces)
    return pl.pallas_call(
        functools.partial(kernel, len(pieces)),
        grid=(slots,),
        in_specs=specs,
        out_specs=[o[0] for o in outs],
        out_shape=[jax.ShapeDtypeStruct(o[1], o[2]) for o in outs],
        scratch_shapes=scratch,
        compiler_params=pltpu.CompilerParams(vmem_limit_bytes=VMEM_LIMIT, dimension_semantics=("arbitrary",)),
        cost_estimate=pl.CostEstimate(flops=int(2 * macs * slots), bytes_accessed=int(8e6), transcendentals=0),
    )(*args, *pieces)


def slot_out(slots, shape, kind):
    return (slot_spec(*shape), (slots,) + shape, kind)


def fixed_out(shape, kind):
    return (fixed_spec(*shape), shape, kind)


BLOCK_MACS = NTOK * (D * TOKW + 2 * NTOK * D)


def enc_forward(slots, ids, valid, xin, pe, misc, mod, bias, pieces):
    return call(
        enc_forward_kernel,
        slots,
        [SMEM, SMEM, slot_spec(NTOK, 128), fixed_spec(NTOK, D), fixed_spec(D, 128), slot_spec(6, D), slot_spec(1, NTOK)],
        [ids, valid, xin, pe, misc, mod, bias],
        pieces,
        [slot_out(slots, (NTOK, D), F32)] * 2 + [slot_out(slots, s, k) for s, k in SAVES],
        weight_scratch(),
        BLOCK_MACS,
    )


def side_forward(slots, ids, valid, h_in, mask, pe, misc, mod, pieces):
    return call(
        side_forward_kernel,
        slots,
        [SMEM, SMEM, slot_spec(NTOK, D), slot_spec(NTOK, 1), fixed_spec(NTOK, D), fixed_spec(D, 128), slot_spec(6, D)],
        [ids, valid, h_in, mask, pe, misc, mod],
        pieces,
        [slot_out(slots, (NTOK, D), F32)] * 2 + [slot_out(slots, s, k) for s, k in SAVES],
        weight_scratch(),
        BLOCK_MACS,
    )


def dec_both(slots, ids, valid, coef, h_in, noise, misc, mod, pieces):
    return call(
        dec_kernel,
        slots,
        [SMEM, SMEM, SMEM, slot_spec(NTOK, D), slot_spec(NTOK, 128), fixed_spec(D, 128), slot_spec(8, D)],
        [ids, valid, coef, h_in, noise, misc, mod],
        pieces,
        [
            slot_out(slots, (NTOK, D), F32),
            slot_out(slots, (8, D), F32),
            fixed_out((CHUNKS, D, CW), BF16),
            fixed_out((D, 128), F32),
            fixed_out((8, 128), F32),
        ],
        weight_scratch() + grad_scratch() + [pltpu.VMEM(s, k) for s, k in SAVES],
        3 * BLOCK_MACS,
    )


def side_backward(slots, ids, valid, d_out, h_in, mask, mod, saves, pieces):
    return call(
        side_backward_kernel,
        slots,
        [SMEM, SMEM, slot_spec(NTOK, D), slot_spec(NTOK, D), slot_spec(NTOK, 1), slot_spec(6, D)] + [slot_spec(*s) for s, _ in SAVES],
        [ids, valid, d_out, h_in, mask, mod] + list(saves),
        pieces,
        [
            slot_out(slots, (NTOK, D), F32),
            slot_out(slots, (8, D), F32),
            fixed_out((CHUNKS, D, CW), BF16),
            fixed_out((8, D), F32),
        ],
        weight_scratch() + grad_scratch(),
        2 * BLOCK_MACS,
    )


def enc_backward(slots, ids, valid, d_out, h_in, xin, mod, saves, pieces):
    return call(
        enc_backward_kernel,
        slots,
        [SMEM, SMEM, slot_spec(NTOK, D), slot_spec(NTOK, D), slot_spec(NTOK, 128), slot_spec(6, D)] + [slot_spec(*s) for s, _ in SAVES],
        [ids, valid, d_out, h_in, xin, mod] + list(saves),
        pieces,
        [
            slot_out(slots, (8, D), F32),
            fixed_out((CHUNKS, D, CW), BF16),
            fixed_out((D, 128), F32),
        ],
        weight_scratch() + grad_scratch(),
        2 * BLOCK_MACS,
    )


def silu_slope(val):
    s = jax.nn.sigmoid(val)
    return s * (1.0 + val * (1.0 - s))


def adam(master, first_m, second, grad_in):
    first_new = beta_one * first_m + (1.0 - beta_one) * grad_in
    second_new = beta_two * second + (1.0 - beta_two) * grad_in * grad_in
    first_hat = first_new / (1.0 - beta_one**STEP)
    second_hat = second_new / (1.0 - beta_two**STEP)
    master_new = master - learn_rate * (first_hat / (jnp.sqrt(second_hat) + adam_eps) + weight_decay * master)
    return [master_new, first_new, second_new]


def block_grad(dw):
    mine = lax.psum_scatter(dw, "fsdp", scatter_dimension=1, tiled=True)
    if lax.axis_size("dp") == CHUNKS:
        return reduce_parts(mine, "dp", BF16).astype(BF16)
    mine = mine.transpose(1, 0, 2).reshape(mine.shape[1], TOKW)
    return reduce_parts(mine.reshape(mine.shape[0], lax.axis_size("dp"), -1).transpose(1, 0, 2), "dp", BF16).astype(BF16)


def all_columns(part):
    full = gather(part, "dp")
    return full.transpose(1, 0, 2).reshape(part.shape[0], -1)


def on_device(latents, noise, timesteps, labels, patch_mask, counts, owners, tables_w, tables_m, tables_v, rows_w, rows_m, rows_v, down_w, down_m, down_v):
    nd, nf = lax.axis_size("dp"), lax.axis_size("fsdp")
    me_d, me_f = lax.axis_index("dp"), lax.axis_index("fsdp")
    rows = tables_w.shape[0]
    micro, per = latents.shape[0], latents.shape[1]
    slots = micro * per
    lats = nf * slots

    rows_b, down_b, tables_b = rows_w.astype(BF16), down_w.astype(BF16), tables_w.astype(BF16)
    pieces = []
    for b in range(3):
        at = D + b * STRIDE
        whole = jnp.concatenate([rows_b[:, at : at + 4 * D + FF], down_b[:, b * FF : (b + 1) * FF]], axis=1)
        chunk = lax.dynamic_slice_in_dim(whole, me_d * (TOKW // nd), TOKW // nd, 1)
        pieces.append(gather_block(chunk, whole))
    head_at = D + 3 * STRIDE + 2 * D
    gap = jnp.zeros((rows, 16), BF16)
    misc_own = jnp.concatenate(
        [
            tables_b[:, : PIN + 1],
            gap[:, :15],
            rows_b[:, head_at : head_at + PIN],
            gap,
            rows_b[:, head_at + PIN : head_at + 2 * PIN],
            gap,
            gap,
            gap,
        ],
        axis=1,
    )
    misc = gather(misc_own, "fsdp").reshape(D, 128)

    steps = timesteps.reshape(slots)
    plan = jnp.take(jnp.asarray(plan_table()), steps, axis=0)
    info = gather(jnp.stack([steps, labels.reshape(slots)]), "fsdp")
    steps_g, labels_g = info[:, 0].reshape(lats), info[:, 1].reshape(lats)
    feat = time_features(steps_g).astype(BF16)
    w_tone = tables_b[:, PIN + 1 : PIN + 1 + FREQ]
    class_tab = tables_b[:, PIN + 1 + FREQ :]
    w_ttwo = rows_b[:, :D]
    ada_at = [D + b * STRIDE + 4 * D + FF for b in range(3)]
    fin_at = D + 3 * STRIDE
    w_ada = jnp.concatenate([rows_b[:, a : a + 6 * D] for a in ada_at] + [rows_b[:, fin_at : fin_at + 2 * D]], axis=1)
    a_pre = dot_nt(feat, w_tone)
    a_act = jax.nn.silu(a_pre).astype(BF16)
    hot = (labels_g[:, None] == jnp.arange(CLASSES)[None, :]).astype(BF16)
    c_part = dot(a_act, w_ttwo).reshape(lats, nf, rows).transpose(1, 0, 2)
    cond = reduce_parts(c_part, "fsdp", F32) + dot_nt(hot, class_tab)
    s_cond = jax.nn.silu(cond).astype(BF16)
    mod_part = dot(s_cond, w_ada).reshape(nf, slots, 20 * D)
    mods = reduce_parts(mod_part, "fsdp", F32).reshape(slots, 20, D)
    mod_e, mod_s, mod_d = mods[:, 0:6], mods[:, 6:12], mods[:, 12:20]

    x_zero, eps = latents.reshape(slots, NTOK * PIN), noise.reshape(slots, NTOK * PIN)
    x_in = (plan[:, 0:1] * x_zero + plan[:, 1:2] * eps).astype(BF16).reshape(slots, NTOK, PIN)
    x_in = jnp.pad(x_in, ((0, 0), (0, 0), (0, 128 - PIN)))
    eps = jnp.pad(eps.reshape(slots, NTOK, PIN), ((0, 0), (0, 0), (32, 96 - PIN)))
    masked = patch_mask.reshape(slots, NTOK).astype(F32)
    bias = (-1e9 * masked)[:, None, :]
    mask_col = masked[:, :, None]
    pe = jnp.asarray(position_table())
    valid = (jnp.arange(per)[None, :] < counts).astype(jnp.int32).reshape(slots)
    ids = jnp.stack([me_d, me_f % 2]).astype(jnp.int32)

    h0, h_enc, *save_e = enc_forward(slots, ids, valid, x_in, pe, misc, mod_e, bias, pieces[0])
    hs, h_side, *save_s = side_forward(slots, ids, valid, h_enc, mask_col, pe, misc, mod_s, pieces[1])
    d_side, dmod_d, dw_d, dmisc_d, loss = dec_both(slots, ids, valid, plan, h_side, eps, misc, mod_d, pieces[2])
    g_dec = block_grad(dw_d)
    d_enc, dmod_s, dw_s, dtok = side_backward(slots, ids, valid, d_side, hs, mask_col, mod_s, save_s, pieces[1])
    g_side = block_grad(dw_s)
    dmod_e, dw_e, dmisc_e = enc_backward(slots, ids, valid, d_enc, h0, x_in, mod_e, save_e, pieces[0])
    g_enc = block_grad(dw_e)

    def group(val):
        return gather(val.astype(BF16).reshape(slots, -1), "fsdp").reshape(lats, -1)

    dm_all = jnp.concatenate([group(dmod_e[:, :6]), group(dmod_s[:, :6]), group(dmod_d)], axis=1)
    d_cond = dot_nt(dm_all, w_ada) * silu_slope(cond)
    d_cond_all = gather(d_cond.astype(BF16), "fsdp").transpose(1, 0, 2).reshape(lats, D)
    d_apre = (dot_nt(d_cond_all, w_ttwo) * silu_slope(a_pre)).astype(BF16)
    g_ada = dot_tn(s_cond, dm_all)
    g_ttwo = dot_tn(a_act, d_cond_all)
    g_tone = dot_tn(d_apre, feat)
    g_class = lax.dot_general(d_cond, hot.astype(F32), (((0,), (0,)), ((), ())), precision=lax.Precision.HIGHEST, preferred_element_type=F32)
    dmisc = dmisc_e + dmisc_d
    tok = jnp.sum(dtok, axis=0)[:, None]
    dmisc = jnp.concatenate([dmisc[:, :PIN], tok, dmisc[:, PIN + 1 :]], axis=1)
    g_misc = reduce_parts(dmisc.reshape(nf, rows, 128), "fsdp", F32)
    cond_grad = jnp.concatenate([g_ada, g_ttwo, g_tone, g_class, g_misc, jnp.zeros((rows, 24), F32)], axis=1)
    width = cond_grad.shape[1]
    g_cond = reduce_parts(cond_grad.reshape(rows, nd, width // nd).transpose(1, 0, 2), "dp", BF16).astype(BF16)

    parts = [g_enc, g_side, g_dec, g_cond]
    squares = sum(jnp.sum(jnp.square(p.astype(F32))) for p in parts)
    used = jnp.sum(valid).astype(F32)
    norm_sq, loss_sum, count = sum_all(jnp.stack([squares, jnp.sum(loss), used]))
    scale = 1.0 / (count * (NTOK * PIN))
    loss_out = loss_sum * scale
    grad_norm = jnp.sqrt(norm_sq) * scale
    factor = scale * jnp.minimum(1.0, clip_level / (grad_norm + 1e-06))

    f_enc, f_side, f_dec, f_cond = [all_columns(p) for p in parts]
    ada = [f_cond[:, i * 6 * D : (i + 1) * 6 * D] for i in range(3)]
    at = 18 * D
    fin, at = f_cond[:, at : at + 2 * D], at + 2 * D
    ttwo, at = f_cond[:, at : at + D], at + D
    tone, at = f_cond[:, at : at + FREQ], at + FREQ
    klass, at = f_cond[:, at : at + CLASSES], at + CLASSES
    small = f_cond[:, at : at + 128]
    heads = jnp.concatenate([small[:, 32 : 32 + PIN], small[:, 64 : 64 + PIN]], axis=1)
    up_to = 4 * D + FF
    rows_g = [ttwo]
    for blk, a in zip((f_enc, f_side, f_dec), ada):
        rows_g += [blk[:, :up_to], a]
    rows_g = jnp.concatenate(rows_g + [fin, heads], axis=1)
    down_g = jnp.concatenate([blk[:, up_to:] for blk in (f_enc, f_side, f_dec)], axis=1)
    tables_g = jnp.concatenate([small[:, : PIN + 1], tone, klass], axis=1)
    results = adam(tables_w, tables_m, tables_v, factor * tables_g.astype(F32))

    def own(val):
        size = val.shape[1] // nd
        return lax.dynamic_slice_in_dim(val, me_d * size, size, 1)

    results += adam(own(rows_w), own(rows_m), own(rows_v), factor * own(rows_g).astype(F32))
    results += adam(own(down_w), own(down_m), own(down_v), factor * own(down_g).astype(F32))
    return tuple([loss_out, grad_norm] + results)


def solution(mesh):
    lat = P(None, ("dp", "fsdp"), None)
    num = P(None, ("dp", "fsdp"))
    row = P("fsdp", None)
    both = P("fsdp", "dp")
    return jax.shard_map(
        on_device,
        mesh=mesh,
        in_specs=(lat, lat, num, num, lat, num, P()) + (row,) * 9,
        out_specs=(P(), P()) + (row,) * 3 + (both,) * 6,
        check_vma=False,
    )
```

```python
import functools
import math

import jax
import jax.numpy as jnp
import numpy as np
from jax import lax
from jax.experimental import pallas as pl
from jax.experimental.pallas import tpu as pltpu
from jax.sharding import PartitionSpec as P

D = 384
HEADS = 6
HDIM = 64
FF = 1536
NTOK = 256
PIN = 16
FREQ = 256
CLASSES = 1000
TSTEPS = 1000
STEP = 10
POUT = 32

beta_one = 0.9
beta_two = 0.999
adam_eps = 1e-08
learn_rate = 0.05
weight_decay = 0.1
clip_level = 0.005
ln_eps = 1e-06

F32 = jnp.float32
BF16 = jnp.bfloat16
STRIDE = 10 * D + FF
TOKW = 3 * D + D + FF + FF
CHUNKS = 4
CW = TOKW // CHUNKS
GELU_C = math.sqrt(2.0 / math.pi)
VMEM_LIMIT = 60 * 1024 * 1024


def plan_table():
    j = np.arange(TSTEPS, dtype=np.float64)
    beta = 0.0001 + (0.02 - 0.0001) * j / (TSTEPS - 1)
    abar = np.cumprod(1.0 - beta)
    prev = np.concatenate([[1.0], abar[:-1]])
    out = np.zeros((TSTEPS, 5), np.float64)
    out[:, 0] = np.sqrt(abar)
    out[:, 1] = np.sqrt(1.0 - abar)
    out[1:, 2] = np.log(beta[1:])
    out[1:, 3] = np.log(beta[1:] * (1.0 - prev[1:]) / (1.0 - abar[1:]))
    out[1:, 4] = prev[1:] * beta[1:] ** 2 / ((1.0 - abar[1:]) * abar[1:])
    full = np.zeros((TSTEPS, 128), np.float32)
    full[:, 0:2] = out[:, 0:2]
    for k in range(3):
        left = out[:, 2 + k].astype(np.float32)
        for part in range(3):
            full[:, 8 + 3 * k + part] = bf16_of(left)
            left = left - full[:, 8 + 3 * k + part]
    return full


def bf16_of(val):
    return val.astype(jnp.bfloat16).astype(np.float32)


def feature_table():
    half = FREQ // 2
    rates = np.exp(-math.log(10000.0) * np.arange(half) / half)
    angles = np.arange(1024)[:, None] * rates[None, :]
    return np.concatenate([np.cos(angles), np.sin(angles)], axis=1).astype(jnp.bfloat16)


def position_table():
    half = D // 2
    rates = np.exp(-math.log(10000.0) * 2.0 * np.arange(half) / D)
    angles = np.arange(NTOK)[:, None] * rates[None, :]
    return np.concatenate([np.sin(angles), np.cos(angles)], axis=1).astype(np.float32)


def stages(size, pair_first):
    out, stride = [], 1
    if pair_first and size % 2 == 0:
        out.append((1, 2))
        stride, size = 2, size // 2
    while size > 1:
        step = 4 if size % 4 == 0 else 2
        out.append((stride, step))
        stride, size = stride * step, size // step
    return out


def axis_stages(axis):
    return stages(lax.axis_size(axis), axis == "fsdp")


def swap(val, axis, mask):
    size = lax.axis_size(axis)
    return lax.ppermute(val, axis, [(i, i ^ mask) for i in range(size)])


def place(axis, stride, size):
    return (lax.axis_index(axis) // stride) % size


def in_order(parts, pos):
    size = len(parts)
    if size == 2:
        return jnp.stack([lax.select(pos == 1, parts[1 - j], parts[j]) for j in range(2)])
    return jnp.stack([lax.select_n(pos, *[parts[j ^ p] for p in range(size)]) for j in range(size)])


def gather_open(val, axis, level):
    stride, size = list(reversed(axis_stages(axis)))[level]
    return [val] + [swap(val, axis, k * stride) for k in range(1, size)]


def gather_close(parts, axis, level):
    stride, size = list(reversed(axis_stages(axis)))[level]
    return in_order(parts, place(axis, stride, size))


def gather_shape(val, axis, shape):
    n = len(axis_stages(axis))
    order = tuple(reversed(range(n))) + tuple(range(n, n + len(shape)))
    return val.transpose(order).reshape((lax.axis_size(axis),) + shape)


def gather(val, axis):
    shape = val.shape
    for level in range(len(axis_stages(axis))):
        val = gather_close(gather_open(val, axis, level), axis, level)
    return gather_shape(val, axis, shape)


def reduce_stage(val, dim, axis, stride, size, send_type):
    pos = place(axis, stride, size)
    total = lax.dynamic_index_in_dim(val, pos, dim, keepdims=False).astype(F32)
    for k in range(1, size):
        piece = lax.dynamic_index_in_dim(val, pos ^ k, dim, keepdims=False)
        total = total + swap(piece.astype(send_type), axis, k * stride).astype(F32)
    return total


def reduce_open(val, axis, send_type):
    plan = axis_stages(axis)
    sizes = [s for _, s in reversed(plan)]
    val = val.reshape(tuple(sizes) + val.shape[1:])
    for dim in range(len(sizes) - 1, 0, -1):
        stride, size = plan[len(sizes) - 1 - dim]
        val = reduce_stage(val, dim, axis, stride, size, send_type)
    stride, size = plan[-1]
    pos = place(axis, stride, size)
    out = [lax.dynamic_index_in_dim(val, pos ^ k, 0, keepdims=False) for k in range(size)]
    return [out[0]] + [swap(out[k].astype(send_type), axis, k * stride) for k in range(1, size)]


def total_of(parts):
    return sum(p.astype(F32) for p in parts)


def reduce_parts(val, axis, send_type):
    return total_of(reduce_open(val, axis, send_type))


def after(val, *deps):
    return lax.optimization_barrier((val,) + deps)[0]


def tie(parts, *deps):
    return list(lax.optimization_barrier(tuple(parts) + deps)[: len(parts)])


def sum_all(val, axes):
    for axis in axes:
        for stride, size in axis_stages(axis):
            parts = [val] + [swap(val, axis, k * stride) for k in range(1, size)]
            while len(parts) > 1:
                parts = [parts[i] + parts[i + 1] for i in range(0, len(parts), 2)]
            val = parts[0]
    return val


def small_mesh(rows):
    return rows == 48 and lax.axis_size("dp") == CHUNKS and lax.axis_size("fsdp") == 8


def gather_z(whole):
    width = whole.shape[1] // CHUNKS
    chunk = lax.dynamic_slice_in_dim(whole, lax.axis_index("dp") * width, width, 1)
    parts = [chunk] + [swap(chunk, "fsdp", 2 * k) for k in (1, 2, 3)]
    return in_order(parts, place("fsdp", 2, 4))


def gather_dp(mine):
    return jnp.stack([mine] + [swap(mine, "dp", k) for k in (1, 2, 3)])


def gather_core(mine):
    return [mine, swap(mine, "fsdp", 1)]


def gather_whole(whole):
    return [lax.all_gather(whole, "fsdp", axis=0, tiled=True)]


def dot(a, b):
    return jnp.dot(a, b, preferred_element_type=F32)


def dot_nt(a, b):
    return lax.dot_general(a, b, (((1,), (1,)), ((), ())), preferred_element_type=F32)


def dot_tn(a, b):
    return lax.dot_general(a, b, (((0,), (0,)), ((), ())), preferred_element_type=F32)


def layer_norm(v):
    c = v - jnp.mean(v, axis=-1, keepdims=True)
    r = lax.rsqrt(jnp.mean(c * c, axis=-1, keepdims=True) + ln_eps)
    return c * r, r


def norm_grad(dm, y, r, scale):
    dy = dm * (1.0 + scale)
    dv = r * (dy - jnp.mean(dy, axis=-1, keepdims=True) - y * jnp.mean(dy * y, axis=-1, keepdims=True))
    return dv, jnp.sum(dm, axis=0, keepdims=True), jnp.sum(dm * y, axis=0, keepdims=True)


def wpart(w, j, lo, hi):
    if len(w.shape) == 2:
        width = w.shape[1] // CHUNKS
        return w[:, j * width + lo : j * width + hi]
    return w[j, :, :, :, lo:hi].reshape(D, hi - lo)


def head_masks():
    lane = lax.broadcasted_iota(jnp.int32, (1, 2 * HDIM), 1)
    low = (lane < HDIM).astype(F32)
    return low, 1.0 - low


def block_forward(h, mod, w, bias, sv):
    qkv_ref, p_ref, o_ref, g_ref, gp_ref, att_ref, mlp_ref, h2_ref = sv
    y1, _ = layer_norm(h)
    n1 = (y1 * (1.0 + mod(1)) + mod(0)).astype(BF16)
    qkv_ref[...] = dot(n1, wpart(w, 0, 0, CW)).astype(BF16)
    masks = head_masks()
    for j in range(3):
        q2 = qkv_ref[:, 128 * j : 128 * j + 128]
        k2 = qkv_ref[:, D + 128 * j : D + 128 * j + 128]
        v2 = qkv_ref[:, 2 * D + 128 * j : 2 * D + 128 * j + 128]
        o2 = None
        for a in range(2):
            s = dot_nt(q2, k2 * (masks[a] * 0.125).astype(BF16))
            if bias is not None:
                s = s + bias
            e = jnp.exp(s - jnp.max(s, axis=-1, keepdims=True))
            p = (e * (1.0 / jnp.sum(e, axis=-1, keepdims=True))).astype(BF16)
            p_ref[2 * j + a] = p
            part = dot(p, v2 * masks[a].astype(BF16))
            o2 = part if o2 is None else o2 + part
        o_ref[:, 128 * j : 128 * j + 128] = o2.astype(BF16)
    att = dot(o_ref[...], wpart(w, 1, 0, D))
    att_ref[...] = att.astype(BF16)
    h2 = h + mod(2) * att
    h2_ref[...] = h2
    y2, _ = layer_norm(h2)
    n2 = (y2 * (1.0 + mod(4)) + mod(3)).astype(BF16)
    for j, lo, hi, at in ((1, D, CW, 0), (2, 0, 2 * D, 2 * D)):
        u = dot(n2, wpart(w, j, lo, hi))
        u2 = u * u
        t = jnp.tanh(u * (GELU_C + (GELU_C * 0.044715) * u2))
        half = 0.5 * t + 0.5
        g_ref[:, at : at + 2 * D] = (u * half).astype(BF16)
        gp = half + (u * (0.5 - 0.5 * t * t)) * (GELU_C + (3.0 * GELU_C * 0.044715) * u2)
        gp_ref[:, at : at + 2 * D] = gp.astype(BF16)
    mlp = dot_nt(g_ref[:, 0:D], wpart(w, 2, 2 * D, CW)) + dot_nt(g_ref[:, D:], wpart(w, 3, 0, CW))
    mlp_ref[...] = mlp.astype(BF16)
    return h2 + mod(5) * mlp


def block_backward(d3, h, mod, w, sv, dw, du_ref, dqkv_ref, dmod):
    qkv_ref, p_ref, o_ref, g_ref, gp_ref, att_ref, mlp_ref, h2_ref = sv
    dmlp = (d3 * mod(5)).astype(BF16)
    dmod(5, jnp.sum(d3 * mlp_ref[...].astype(F32), axis=0, keepdims=True))
    du_ref[:, 0:D] = (dot(dmlp, wpart(w, 2, 2 * D, CW)) * gp_ref[:, 0:D].astype(F32)).astype(BF16)
    du_ref[:, D:] = (dot(dmlp, wpart(w, 3, 0, CW)) * gp_ref[:, D:].astype(F32)).astype(BF16)
    dw[2, :, 2 * D : CW] += dot_tn(dmlp, g_ref[:, 0:D])
    dw[3, :, 0:CW] += dot_tn(dmlp, g_ref[:, D:])
    dn2 = dot_nt(du_ref[:, 0 : 2 * D], wpart(w, 1, D, CW)) + dot_nt(du_ref[:, 2 * D :], wpart(w, 2, 0, 2 * D))
    y2, r2 = layer_norm(h2_ref[...])
    n2 = (y2 * (1.0 + mod(4)) + mod(3)).astype(BF16)
    dw[1, :, D:CW] += dot_tn(n2, du_ref[:, 0 : 2 * D])
    dw[2, :, 0 : 2 * D] += dot_tn(n2, du_ref[:, 2 * D :])
    dv, dshift, dscale = norm_grad(dn2, y2, r2, mod(4))
    dmod(3, dshift)
    dmod(4, dscale)
    d2 = d3 + dv
    datt = (d2 * mod(2)).astype(BF16)
    dmod(2, jnp.sum(d2 * att_ref[...].astype(F32), axis=0, keepdims=True))
    do = dot_nt(datt, wpart(w, 1, 0, D)).astype(BF16)
    dw[1, :, 0:D] += dot_tn(o_ref[...], datt)
    masks = head_masks()
    for j in range(3):
        q2 = qkv_ref[:, 128 * j : 128 * j + 128]
        k2 = qkv_ref[:, D + 128 * j : D + 128 * j + 128]
        v2 = qkv_ref[:, 2 * D + 128 * j : 2 * D + 128 * j + 128]
        do2 = do[:, 128 * j : 128 * j + 128]
        dq2, dk2, dv2 = 0.0, 0.0, 0.0
        for a in range(2):
            one = masks[a].astype(BF16)
            eighth = (masks[a] * 0.125).astype(BF16)
            pb = p_ref[2 * j + a]
            p = pb.astype(F32)
            dp = dot_nt(do2, v2 * one)
            ds = (p * (dp - jnp.sum(p * dp, axis=-1, keepdims=True))).astype(BF16)
            dq2 += dot(ds, k2 * eighth)
            dk2 += dot_tn(ds, q2 * eighth)
            dv2 += dot_tn(pb, do2 * one)
        dqkv_ref[:, 128 * j : 128 * j + 128] = dq2.astype(BF16)
        dqkv_ref[:, D + 128 * j : D + 128 * j + 128] = dk2.astype(BF16)
        dqkv_ref[:, 2 * D + 128 * j : 2 * D + 128 * j + 128] = dv2.astype(BF16)
    dn1 = dot_nt(dqkv_ref[...], wpart(w, 0, 0, CW))
    y1, r1 = layer_norm(h)
    n1 = (y1 * (1.0 + mod(1)) + mod(0)).astype(BF16)
    dw[0, :, 0:CW] += dot_tn(n1, dqkv_ref[...])
    dv, dshift, dscale = norm_grad(dn1, y1, r1, mod(1))
    dmod(0, dshift)
    dmod(1, dscale)
    return d2 + dv


def load_weights(ids, pieces, w, sems, base=0):
    @pl.when(pl.program_id(0) == 0)
    def _():
        copies = []
        if len(pieces) == 1:
            copies.append(pltpu.make_async_copy(pieces[0].at[:, base : base + w.shape[1]], w, sems.at[0]))
        else:
            for c in range(2):
                for k in range(4):
                    target = w.at[ids[1] ^ k, :, ids[2] ^ c]
                    copies.append(pltpu.make_async_copy(pieces[c].at[k], target, sems.at[4 * c + k]))
        for copy in copies:
            copy.start()
        for copy in copies:
            copy.wait()


def mod_row(mods, base, step):
    return lambda i: mods[pl.ds(step, 1), base + D * i : base + D * i + D]


def row_writer(dmod, step):
    def write(i, val):
        dmod[pl.ds(step, 1), D * i : D * i + D] = val

    return write


def token_row(misc):
    lane = lax.broadcasted_iota(jnp.int32, (8, 128), 1)
    return dot_nt((lane == PIN).astype(BF16), misc[...])[0:1, :]


def enc_forward_kernel(n, ids, xin, pe, mods, bias, *rest):
    pieces, (misc, h0, h3), sv, (w, sems) = rest[:n], rest[n : n + 3], rest[n + 3 : n + 11], rest[n + 11 :]
    load_weights(ids, pieces, w, sems)
    step = pl.program_id(0)

    @pl.when(step == 0)
    def _():
        misc[...] = wpart(w, 0, CW, CW + 128)

    @pl.when(step < ids[0])
    def _():
        h = dot_nt(xin[...], misc[...]) + pe[...]
        h0[...] = h
        h3[...] = block_forward(h, mod_row(mods, 0, step), w, bias[...], sv)


def side_forward_kernel(n, ids, h_in, mask, pe, misc, mods, *rest):
    pieces, (hs, h3), sv, (w, sems) = rest[:n], rest[n : n + 2], rest[n + 2 : n + 10], rest[n + 10 :]
    load_weights(ids, pieces, w, sems)
    step = pl.program_id(0)

    @pl.when(step < ids[0])
    def _():
        m = mask[...]
        h = h_in[...] * (1.0 - m) + m * (token_row(misc) + pe[...])
        hs[...] = h
        h3[...] = block_forward(h, mod_row(mods, 0, step), w, None, sv)


def store_grads(ids, dw, outs):
    if len(outs) == 1:
        for j in range(CHUNKS):
            outs[0][j] = dw[j].astype(BF16)
        return
    for side in range(2):
        for z in range(4):
            at = pl.multiple_of((2 * z + (ids[2] ^ side)) * (D // 8), 16)
            for j in range(CHUNKS):
                outs[side][j, z] = dw[j, pl.ds(at, D // 8), :].astype(BF16)


def dec_kernel(n, m, ids, coef, h_in, noise, misc, mods, *rest):
    pieces = rest[:n]
    d_in, dmod, dmisc, loss = rest[n : n + 4]
    dw_out = rest[n + 4 : n + 4 + m]
    w, sems, dw, du, dqkv = rest[n + 4 + m : n + 9 + m]
    sv = rest[n + 9 + m :]
    load_weights(ids, pieces, w, sems, TOKW)
    step = pl.program_id(0)

    @pl.when(step == 0)
    def _():
        dw[...] = jnp.zeros_like(dw)
        dmisc[...] = jnp.zeros_like(dmisc)
        loss[...] = jnp.zeros_like(loss)
        dmod[...] = jnp.zeros_like(dmod)

    @pl.when(step < ids[0])
    def _():
        row = mod_row(mods, 6 * D, step)
        put = row_writer(dmod, step)
        h = h_in[...]
        h_dec = block_forward(h, row, w, None, sv)
        yf, rf = layer_norm(h_dec)
        nf = (yf * (1.0 + row(7)) + row(6)).astype(BF16)
        out = dot(nf, misc[...])
        ln_b, ln_pv, wmean = coef[step, 0], coef[step, 1], coef[step, 2]
        lane = lax.broadcasted_iota(jnp.int32, (1, 128), 1)
        live = (lane >= 32) & (lane < 32 + PIN)
        d = jnp.where(live, out - noise[...], 0.0)
        vf = (pltpu.roll(out, 128 - 32, 1) + 1.0) * 0.5
        vf = jnp.where(live, vf, 0.0)
        lv = vf * ln_b + (1.0 - vf) * ln_pv
        first = jnp.exp(ln_pv - lv)
        second = wmean * jnp.exp(-lv)
        inv = 0.5 / math.log(2.0)
        dd = d * d
        kl = inv * (-1.0 + lv - ln_pv + first + dd * second)
        term = jnp.where(live, dd + kl, 0.0)
        loss[...] += jnp.sum(term.reshape(NTOK // 8, 8, 128), axis=0)
        deps = d * (2.0 + (2.0 * inv) * second)
        dlog = inv * (1.0 - first - dd * second) * (0.5 * (ln_b - ln_pv))
        dlog = jnp.where(live, dlog, 0.0)
        dout = (deps + pltpu.roll(dlog, 32, 1)).astype(BF16)
        dmisc[...] += dot_tn(nf, dout)
        dnf = dot_nt(dout, misc[...])
        d3, dshift, dscale = norm_grad(dnf, yf, rf, row(7))
        put(6, dshift)
        put(7, dscale)
        d_in[...] = block_backward(d3, h, row, w, sv, dw, du, dqkv, put)

    @pl.when(step == pl.num_programs(0) - 1)
    def _():
        store_grads(ids, dw, dw_out)


def side_backward_kernel(n, m, ids, d_out, h_in, mask, mods, *rest):
    sv, pieces, rest = rest[:8], rest[8 : 8 + n], rest[8 + n :]
    d_enc, dmod, dtok = rest[:3]
    dw_out = rest[3 : 3 + m]
    w, sems, dw, du, dqkv = rest[3 + m :]
    load_weights(ids, pieces, w, sems)
    step = pl.program_id(0)

    @pl.when(step == 0)
    def _():
        dw[...] = jnp.zeros_like(dw)
        dtok[...] = jnp.zeros_like(dtok)
        dmod[...] = jnp.zeros_like(dmod)

    @pl.when(step < ids[0])
    def _():
        hidden = mask[...]
        dh = block_backward(d_out[...], h_in[...], mod_row(mods, 0, step), w, sv, dw, du, dqkv, row_writer(dmod, step))
        dm = dh * hidden
        dtok[...] += jnp.sum(dm.reshape(NTOK // 8, 8, D), axis=0)
        d_enc[...] = dh - dm

    @pl.when(step == pl.num_programs(0) - 1)
    def _():
        store_grads(ids, dw, dw_out)


def enc_backward_kernel(n, m, ids, d_out, h_in, xin, mods, dmisc, dtok, *rest):
    sv, pieces, rest = rest[:8], rest[8 : 8 + n], rest[8 + n :]
    dmod = rest[0]
    dw_out = rest[1 : 1 + m]
    w, sems, dw, du, dqkv = rest[1 + m :]
    load_weights(ids, pieces, w, sems)
    step = pl.program_id(0)

    @pl.when(step == 0)
    def _():
        dw[...] = jnp.zeros_like(dw)
        dmod[...] = jnp.zeros_like(dmod)
        lane = lax.broadcasted_iota(jnp.int32, (8, 128), 1)
        token = lax.dot_general(
            dtok[...], (lane == PIN).astype(F32), (((0,), (0,)), ((), ())), precision=lax.Precision.HIGHEST, preferred_element_type=F32
        )
        dw[0, :, CW : CW + 128] = dmisc[...] + token

    @pl.when(step < ids[0])
    def _():
        dh = block_backward(d_out[...], h_in[...], mod_row(mods, 0, step), w, sv, dw, du, dqkv, row_writer(dmod, step))
        dw[0, :, CW : CW + 128] += dot_tn(dh.astype(BF16), xin[...])

    @pl.when(step == pl.num_programs(0) - 1)
    def _():
        store_grads(ids, dw, dw_out)


def assign_kernel(nf, slots, me, packed, features, tone, ttwo, classes, mine, info_out, c_part, c_own, a_pre_out, a_out, feat_out, hot_out, pick_out):
    lats = packed.shape[0]
    info = packed[:, NTOK * PIN + NTOK :]
    used = info[:, 0:1]
    src = lax.broadcasted_iota(jnp.int32, (lats, lats), 0)
    dst = lax.broadcasted_iota(jnp.int32, (lats, lats), 1)
    before = dot((dst < src).astype(BF16), jnp.broadcast_to(used, (lats, 128)))[:, 0:1]
    turn = jnp.floor((before + 0.5) * (1.0 / nf))
    target = (before - nf * turn) * 8.0 + turn
    live = used.astype(F32) > 0.5
    pick = jnp.where(live & (target == dst.astype(F32)), 1.0, 0.0).astype(BF16)
    moved = dot_tn(pick, info)
    step_of = moved[:, 1:2] * 32.0 + moved[:, 2:3]
    label_of = moved[:, 3:4] * 32.0 + moved[:, 4:5]
    wide = lax.broadcasted_iota(jnp.int32, (lats, 1024), 1).astype(F32)
    hot_t = jnp.where(wide == step_of, 1.0, 0.0).astype(BF16)
    hot_l = jnp.where(wide == label_of, 1.0, 0.0).astype(BF16)
    feat = dot(hot_t, features[...]).astype(BF16)
    a_pre = dot_nt(tone[...], feat)
    a_act = (a_pre * jax.nn.sigmoid(a_pre)).astype(BF16)
    c_part[...] = dot_tn(ttwo[...], a_act)
    c_own[...] = dot_nt(classes[...], hot_l)
    a_pre_out[...] = a_pre
    a_out[...] = a_act
    feat_out[...] = feat
    hot_out[...] = hot_l
    lane8 = lax.broadcasted_iota(jnp.int32, (lats, 8), 1) + me[0] * 8
    pick_me = jnp.where(live & (target == lane8.astype(F32)), 1.0, 0.0).astype(BF16)
    mine[...] = dot_tn(pick_me, packed[:, : NTOK * PIN + NTOK]).astype(BF16)
    info_out[...] = dot_tn(pick_me, info)
    pick_out[...] = pick_me


SMEM = pl.BlockSpec(memory_space=pltpu.SMEM)
ANY = pl.BlockSpec(memory_space=pl.ANY)


def slot_spec(*shape):
    return pl.BlockSpec((None,) + shape, lambda s, ids: (jnp.minimum(s, jnp.maximum(ids[0] - 1, 0)),) + (0,) * len(shape))


def fixed_spec(*shape):
    return pl.BlockSpec(shape, lambda s, ids: (0,) * len(shape))


SAVES = (
    ((NTOK, 3 * D), BF16),
    ((HEADS, NTOK, NTOK), BF16),
    ((NTOK, D), BF16),
    ((NTOK, FF), BF16),
    ((NTOK, FF), BF16),
    ((NTOK, D), BF16),
    ((NTOK, D), BF16),
    ((NTOK, D), F32),
)


def weight_scratch(pieces, width):
    shape = (D, CHUNKS * width) if len(pieces) == 1 else (CHUNKS, 4, 2, D // 8, width)
    return [pltpu.VMEM(shape, BF16), pltpu.SemaphoreType.DMA((8,))]


def grad_scratch(width):
    return [
        pltpu.VMEM((CHUNKS, D, width), F32),
        pltpu.VMEM((NTOK, FF), BF16),
        pltpu.VMEM((NTOK, 3 * D), BF16),
    ]


def grad_outs(split, width):
    if split:
        return [fixed_out((CHUNKS, 4, D // 8, width), BF16)] * 2
    return [fixed_out((CHUNKS, D, width), BF16)]


def call(kernel, slots, ids, in_specs, args, pieces, outs, scratch, macs):
    specs = list(in_specs) + [ANY] * len(pieces)
    return pl.pallas_call(
        functools.partial(kernel, len(pieces)),
        grid_spec=pltpu.PrefetchScalarGridSpec(
            num_scalar_prefetch=1,
            grid=(slots,),
            in_specs=specs,
            out_specs=[o[0] for o in outs],
            scratch_shapes=scratch,
        ),
        out_shape=[jax.ShapeDtypeStruct(o[1], o[2]) for o in outs],
        compiler_params=pltpu.CompilerParams(vmem_limit_bytes=VMEM_LIMIT, dimension_semantics=("arbitrary",)),
        cost_estimate=pl.CostEstimate(flops=int(macs * slots // 2), bytes_accessed=int(4e6), transcendentals=0),
    )(ids, *args, *pieces)


def slot_out(slots, shape, kind):
    return (slot_spec(*shape), (slots,) + shape, kind)


def fixed_out(shape, kind):
    return (fixed_spec(*shape), shape, kind)


BLOCK_MACS = NTOK * (D * TOKW + 2 * NTOK * D)
MODS_E = (8, 6 * D)
MODS_R = (8, 14 * D)


def enc_forward(slots, ids, xin, pe, mods, bias, pieces):
    return call(
        enc_forward_kernel,
        slots,
        ids,
        [slot_spec(NTOK, 128), fixed_spec(NTOK, D), fixed_spec(*MODS_E), slot_spec(1, NTOK)],
        [xin, pe, mods, bias],
        pieces,
        [fixed_out((D, 128), BF16)] + [slot_out(slots, (NTOK, D), F32)] * 2 + [slot_out(slots, s, k) for s, k in SAVES],
        weight_scratch(pieces, CW + 128),
        BLOCK_MACS,
    )


def side_forward(slots, ids, h_in, mask, pe, misc, mods, pieces):
    return call(
        side_forward_kernel,
        slots,
        ids,
        [slot_spec(NTOK, D), slot_spec(NTOK, 1), fixed_spec(NTOK, D), fixed_spec(D, 128), fixed_spec(*MODS_R)],
        [h_in, mask, pe, misc, mods],
        pieces,
        [slot_out(slots, (NTOK, D), F32)] * 2 + [slot_out(slots, s, k) for s, k in SAVES],
        weight_scratch(pieces, CW),
        BLOCK_MACS,
    )


def dec_both(slots, ids, coef, h_in, noise, misc, mods, pieces, split):
    outs = grad_outs(split, CW)
    return call(
        lambda n, *refs: dec_kernel(n, len(outs), *refs),
        slots,
        ids,
        [SMEM, slot_spec(NTOK, D), slot_spec(NTOK, 128), fixed_spec(D, 128), fixed_spec(*MODS_R)],
        [coef, h_in, noise, misc, mods],
        pieces,
        [slot_out(slots, (NTOK, D), F32), fixed_out((8, 8 * D), F32), fixed_out((D, 128), F32), fixed_out((8, 128), F32)] + outs,
        weight_scratch(pieces, CW) + grad_scratch(CW) + [pltpu.VMEM(s, k) for s, k in SAVES],
        3 * BLOCK_MACS,
    )


def side_backward(slots, ids, d_out, h_in, mask, mods, saves, pieces, split):
    outs = grad_outs(split, CW)
    return call(
        lambda n, *refs: side_backward_kernel(n, len(outs), *refs),
        slots,
        ids,
        [slot_spec(NTOK, D), slot_spec(NTOK, D), slot_spec(NTOK, 1), fixed_spec(*MODS_R)] + [slot_spec(*s) for s, _ in SAVES],
        [d_out, h_in, mask, mods] + list(saves),
        pieces,
        [slot_out(slots, (NTOK, D), F32), fixed_out((8, 6 * D), F32), fixed_out((8, D), F32)] + outs,
        weight_scratch(pieces, CW) + grad_scratch(CW),
        2 * BLOCK_MACS,
    )


def enc_backward(slots, ids, d_out, h_in, xin, mods, dmisc, dtok, saves, pieces, split):
    outs = grad_outs(split, CW + 128)
    return call(
        lambda n, *refs: enc_backward_kernel(n, len(outs), *refs),
        slots,
        ids,
        [slot_spec(NTOK, D), slot_spec(NTOK, D), slot_spec(NTOK, 128), fixed_spec(*MODS_E), fixed_spec(D, 128), fixed_spec(8, D)]
        + [slot_spec(*s) for s, _ in SAVES],
        [d_out, h_in, xin, mods, dmisc, dtok] + list(saves),
        pieces,
        [fixed_out((8, 6 * D), F32)] + outs,
        weight_scratch(pieces, CW + 128) + grad_scratch(CW + 128),
        2 * BLOCK_MACS,
    )


def assign(nf, slots, me, packed, tone, ttwo, classes):
    lats, rows = packed.shape[0], tone.shape[0]
    out = [
        ((8, NTOK * PIN + NTOK), BF16),
        ((8, 128), F32),
        ((D, lats), F32),
        ((rows, lats), F32),
        ((rows, lats), F32),
        ((rows, lats), BF16),
        ((lats, FREQ), BF16),
        ((lats, 1024), BF16),
        ((lats, 8), BF16),
    ]
    vmem = pl.BlockSpec(memory_space=pltpu.VMEM)
    return pl.pallas_call(
        functools.partial(assign_kernel, nf, slots),
        in_specs=[SMEM] + [vmem] * 5,
        out_specs=[vmem] * len(out),
        out_shape=[jax.ShapeDtypeStruct(s, k) for s, k in out],
        compiler_params=pltpu.CompilerParams(vmem_limit_bytes=VMEM_LIMIT),
    )(me, packed, jnp.asarray(feature_table()), tone, ttwo, classes)


def silu_slope(val):
    s = jax.nn.sigmoid(val)
    return s * (1.0 + val * (1.0 - s))


def adam(master, first_m, second, grad_in):
    first_new = beta_one * first_m + (1.0 - beta_one) * grad_in
    second_new = beta_two * second + (1.0 - beta_two) * grad_in * grad_in
    first_hat = first_new / (1.0 - beta_one**STEP)
    second_hat = second_new / (1.0 - beta_two**STEP)
    master_new = master - learn_rate * (first_hat / (jnp.sqrt(second_hat) + adam_eps) + weight_decay * master)
    return [master_new, first_new, second_new]


def grad_core(dw, *deps):
    if len(dw) == 1:
        return dw
    keep, send = dw
    if deps:
        send = after(send, *deps)
    return [keep, swap(send, "fsdp", 1)]


def grad_dp(parts):
    if len(parts) == 1:
        return parts
    keep, got = parts
    me = lax.axis_index("dp")

    def piece(k):
        return lax.dynamic_index_in_dim(keep, me ^ k, 0, False).astype(F32) + lax.dynamic_index_in_dim(got, me ^ k, 0, False).astype(F32)

    return [piece(0).astype(BF16)] + [swap(piece(k).astype(BF16), "dp", k) for k in (1, 2, 3)]


def grad_sum(parts):
    if len(parts) == 1:
        return parts[0]
    return sum(p.astype(F32) for p in parts)


def grad_z(part):
    if part.shape[0] == CHUNKS and part.shape[1] == D:
        part = lax.psum_scatter(part, "fsdp", scatter_dimension=1, tiled=True)
        return reduce_stage(part, 0, "dp", 1, CHUNKS, BF16).astype(BF16)
    return reduce_stage(part, 0, "fsdp", 2, 4, BF16).astype(BF16)


def dp_share(val):
    rows = val.shape[0]
    return reduce_stage(val.reshape(rows, CHUNKS, -1).transpose(1, 0, 2), 0, "dp", 1, CHUNKS, BF16).astype(BF16)


def columns(parts, lo, hi):
    return jnp.concatenate([parts[j, :, lo:hi] for j in range(CHUNKS)], axis=1)


def on_device(latents, noise, timesteps, labels, patch_mask, counts, owners, tables_w, tables_m, tables_v, rows_w, rows_m, rows_v, down_w, down_m, down_v):
    nd, nf = lax.axis_size("dp"), lax.axis_size("fsdp")
    me_d, me_f = lax.axis_index("dp"), lax.axis_index("fsdp")
    rows = tables_w.shape[0]
    micro, per = latents.shape[0], latents.shape[1]
    slots = micro * per
    split = small_mesh(rows)

    steps = timesteps.reshape(slots)
    names = labels.reshape(slots)
    plan = jnp.take(jnp.asarray(plan_table()), steps, axis=0)
    used = (jnp.arange(per)[None, :] < counts).astype(jnp.int32).reshape(slots)
    x_zero, eps = latents.reshape(slots, NTOK * PIN), noise.reshape(slots, NTOK * PIN)
    x_in = (plan[:, 0:1] * x_zero + plan[:, 1:2] * eps).astype(BF16)
    words = jnp.stack([used, steps // 32, steps % 32, names // 32, names % 32], axis=1).astype(BF16)
    words = jnp.concatenate([words, jnp.zeros((slots, 3), BF16), plan[:, 8:].astype(BF16)], axis=1)
    packed = jnp.concatenate([x_in, patch_mask.reshape(slots, NTOK).astype(BF16), words], axis=1)
    packed = jnp.pad(packed, ((0, 8 - slots), (0, 0)))
    eps = jnp.pad(eps.astype(BF16), ((0, 8 - slots), (0, 0)))
    packed = gather(packed, "fsdp").reshape(nf * 8, -1)
    wholes = []

    rows_b, down_b, tables_b = rows_w.astype(BF16), down_w.astype(BF16), tables_w.astype(BF16)
    head_at = D + 3 * STRIDE + 2 * D
    gap = jnp.zeros((rows, 16), BF16)
    misc_own = jnp.concatenate(
        [tables_b[:, : PIN + 1], gap[:, :15], rows_b[:, head_at : head_at + PIN], gap, rows_b[:, head_at + PIN : head_at + 2 * PIN], gap, gap, gap],
        axis=1,
    )
    for b in range(3):
        at = D + b * STRIDE
        row_part, down_part = rows_b[:, at : at + 4 * D + FF], down_b[:, b * FF : (b + 1) * FF]
        cols = [row_part[:, :CW], row_part[:, CW : 2 * CW], row_part[:, 2 * CW :], down_part[:, :D], down_part[:, D:]]
        if b == 0:
            cols = [cols[0], misc_own, cols[1], misc_own, cols[2], cols[3], misc_own, cols[4], misc_own]
        whole = jnp.concatenate(cols, axis=1)
        wholes.append(whole)
    enc_z = gather_z(wholes[0]) if split else None
    late_w = gather_whole(jnp.concatenate(wholes[1:], axis=1))

    w_tone = tables_b[:, PIN + 1 : PIN + 1 + FREQ]
    class_tab = jnp.pad(tables_b[:, PIN + 1 + FREQ :], ((0, 0), (0, 1024 - CLASSES)))
    w_ttwo = rows_b[:, :D]
    ada_at = [D + b * STRIDE + 4 * D + FF for b in range(3)]
    fin_at = D + 3 * STRIDE
    w_ada = jnp.concatenate([rows_b[:, a : a + 6 * D] for a in ada_at] + [rows_b[:, fin_at : fin_at + 2 * D]], axis=1)
    me = me_f.astype(jnp.int32).reshape(1)
    mine, info, c_part, c_own, a_pre, a_act, feat, hot, pick = assign(nf, slots, me, packed, w_tone, w_ttwo, class_tab)
    cond = reduce_parts(c_part.reshape(nf, rows, nf * 8), "fsdp", F32) + c_own
    s_cond = jax.nn.silu(cond).astype(BF16)
    mods_e = reduce_parts(dot_tn(s_cond, w_ada[:, : 6 * D]).reshape(nf, 8, 6 * D), "fsdp", BF16)
    if split:
        enc_w = gather_core(after(gather_dp(after(enc_z, c_part)), s_cond))
    else:
        enc_w = gather_whole(wholes[0])
    mods_r = reduce_open(dot_tn(s_cond, w_ada[:, 6 * D :]).reshape(nf, 8, 14 * D), "fsdp", BF16)

    work = jnp.sum(info[:, 0]).astype(jnp.int32)
    ids = jnp.stack([work, me_d.astype(jnp.int32), (me_f % 2).astype(jnp.int32)])
    coef = jnp.stack([info[:, 8 + 3 * k] + info[:, 9 + 3 * k] + info[:, 10 + 3 * k] for k in range(3)], axis=1)
    size = NTOK * PIN
    x_in = jnp.pad(mine[:slots, :size].reshape(slots, NTOK, PIN), ((0, 0), (0, 0), (0, 128 - PIN)))
    masked = mine[:slots, size:].astype(F32)
    bias = (-1e9 * masked)[:, None, :]
    mask_col = masked[:, :, None]
    pe = jnp.asarray(position_table())

    last = len(axis_stages("fsdp")) - 1
    misc, h0, h_enc, *save_e = enc_forward(slots, ids, x_in, pe, mods_e, bias, enc_w)
    mods_r = total_of(tie(mods_r, misc))
    level = gather_open(after(eps, mods_r), "fsdp", 0)
    hs, h_side, *save_s = side_forward(slots, ids, h_enc, mask_col, pe, misc, mods_r, late_w)
    level = tie(level, hs)
    for at in range(last):
        level = gather_open(gather_close(level, "fsdp", at), "fsdp", at + 1)
    eps = gather_shape(gather_close(level, "fsdp", last), "fsdp", (8, size)).reshape(nf * 8, size)
    eps = dot_tn(pick, eps)[:slots].reshape(slots, NTOK, PIN)
    eps = jnp.pad(eps, ((0, 0), (0, 0), (32, 96 - PIN)))

    d_side, dmod_d, dmisc, loss, *dw_d = dec_both(slots, ids, coef, h_side, eps, misc, mods_r, late_w, False)
    mine_d = lax.psum_scatter(dw_d[0], "fsdp", scatter_dimension=1, tiled=True)
    d_enc, dmod_s, dtok, *dw_s = side_backward(slots, ids, d_side, hs, mask_col, mods_r, save_s, late_w, split)
    part_s = grad_dp(grad_core(dw_s))
    d_enc = after(d_enc, part_s[0])
    dmod_e, *dw_e = enc_backward(slots, ids, d_enc, h0, x_in, mods_e, dmisc, dtok, save_e, enc_w, split)
    total_s = grad_sum(tie(part_s, dmod_e, mine_d))
    dmods = jnp.concatenate([dmod_e, dmod_s, dmod_d], axis=1).astype(BF16)
    core_e = grad_core(dw_e, total_s)
    part_d = reduce_open(after(mine_d, total_s), "dp", BF16)
    part_e = grad_dp(core_e)

    dm_all = gather(after(dmods, part_e[0]), "fsdp").reshape(nf * 8, -1)
    g_side = grad_z(after(total_s, dm_all)) if split else grad_z(total_s)
    g_dec = total_of(tie(part_d, part_e[0])).astype(BF16)
    d_cond = dot_nt(w_ada, dm_all) * silu_slope(cond)
    d_cond_all = gather(d_cond.astype(BF16), "fsdp").reshape(D, nf * 8)
    d_apre = (dot(w_ttwo, d_cond_all) * silu_slope(a_pre)).astype(BF16)
    g_class = jnp.dot(d_cond, hot.astype(F32), precision=lax.Precision.HIGHEST, preferred_element_type=F32)
    kinds = [dot(s_cond, dm_all), dot_nt(a_act, d_cond_all), dot(d_apre, feat), g_class, jnp.zeros((rows, 128), F32)]
    kinds = jnp.concatenate([k.astype(BF16) for k in kinds], axis=1).reshape(rows, CHUNKS, -1).transpose(1, 0, 2)

    total_e = grad_sum(tie(part_e, dm_all, g_dec))
    g_enc = grad_z(total_e)
    first = after(jnp.concatenate([g_side, g_dec], axis=1), total_e)
    full = gather_open(first, "dp", 0)
    g_other = total_of(reduce_open(after(kinds, full[0]), "dp", BF16)).astype(BF16)
    second = after(jnp.concatenate([g_enc, g_other], axis=1), *full)
    full = gather_shape(gather_close(full, "dp", 0), "dp", first.shape)
    squares = jnp.sum(jnp.square(first.astype(F32))) + jnp.sum(jnp.square(second.astype(F32)))
    norm_sq, loss_sum, count = sum_all(jnp.stack([squares, jnp.sum(loss), jnp.sum(used).astype(F32)]), ("fsdp", "dp"))
    rest = gather(second, "dp")
    scale = 1.0 / (count * (NTOK * PIN))
    loss_out = loss_sum * scale
    grad_norm = jnp.sqrt(norm_sq) * scale
    factor = scale * jnp.minimum(1.0, clip_level / (grad_norm + 1e-06))

    up = 4 * D + FF
    wide_e = CW + 128
    f_side, f_dec = columns(full, 0, CW), columns(full, CW, 2 * CW)
    f_enc, small = columns(rest, 0, CW), rest[0, :, CW:wide_e]
    f_rest = columns(rest, wide_e, rest.shape[2])
    at = 20 * D
    ttwo, tone, klass = f_rest[:, at : at + D], f_rest[:, at + D : at + D + FREQ], f_rest[:, at + D + FREQ : at + D + FREQ + CLASSES]
    rows_g = [ttwo, f_enc[:, :up], f_rest[:, : 6 * D], f_side[:, :up], f_rest[:, 6 * D : 12 * D], f_dec[:, :up], f_rest[:, 12 * D : 20 * D]]
    rows_g = jnp.concatenate(rows_g + [small[:, 32 : 32 + PIN], small[:, 64 : 64 + PIN]], axis=1)
    down_g = jnp.concatenate([blk[:, up:] for blk in (f_enc, f_side, f_dec)], axis=1)
    tables_g = jnp.concatenate([small[:, : PIN + 1], tone, klass], axis=1)
    results = adam(tables_w, tables_m, tables_v, factor * tables_g.astype(F32))

    def own(val):
        size = val.shape[1] // nd
        return lax.dynamic_slice_in_dim(val, me_d * size, size, 1)

    results += adam(own(rows_w), own(rows_m), own(rows_v), factor * own(rows_g).astype(F32))
    results += adam(own(down_w), own(down_m), own(down_v), factor * own(down_g).astype(F32))
    return tuple([loss_out, grad_norm] + results)


def solution(mesh):
    lat = P(None, ("dp", "fsdp"), None)
    num = P(None, ("dp", "fsdp"))
    row = P("fsdp", None)
    both = P("fsdp", "dp")
    return jax.shard_map(
        on_device,
        mesh=mesh,
        in_specs=(lat, lat, num, num, lat, num, P()) + (row,) * 9,
        out_specs=(P(), P()) + (row,) * 3 + (both,) * 6,
        check_vma=False,
    )
```

```python
import functools
import math

import jax
import jax.numpy as jnp
import numpy as np
from jax import lax
from jax.experimental import pallas as pl
from jax.experimental.pallas import tpu as pltpu
from jax.sharding import PartitionSpec as P

D = 384
HEADS = 6
HDIM = 64
FF = 1536
NTOK = 256
PIN = 16
FREQ = 256
CLASSES = 1000
TSTEPS = 1000
STEP = 10
POUT = 32

beta_one = 0.9
beta_two = 0.999
adam_eps = 1e-08
learn_rate = 0.05
weight_decay = 0.1
clip_level = 0.005
ln_eps = 1e-06

F32 = jnp.float32
BF16 = jnp.bfloat16
STRIDE = 10 * D + FF
TOKW = 3 * D + D + FF + FF
CHUNKS = 4
CW = TOKW // CHUNKS
GELU_C = math.sqrt(2.0 / math.pi)
VMEM_LIMIT = 60 * 1024 * 1024


def plan_table():
    j = np.arange(TSTEPS, dtype=np.float64)
    beta = 0.0001 + (0.02 - 0.0001) * j / (TSTEPS - 1)
    abar = np.cumprod(1.0 - beta)
    prev = np.concatenate([[1.0], abar[:-1]])
    out = np.zeros((TSTEPS, 5), np.float64)
    out[:, 0] = np.sqrt(abar)
    out[:, 1] = np.sqrt(1.0 - abar)
    out[1:, 2] = np.log(beta[1:])
    out[1:, 3] = np.log(beta[1:] * (1.0 - prev[1:]) / (1.0 - abar[1:]))
    out[1:, 4] = prev[1:] * beta[1:] ** 2 / ((1.0 - abar[1:]) * abar[1:])
    full = np.zeros((TSTEPS, 128), np.float32)
    full[:, 0:2] = out[:, 0:2]
    for k in range(3):
        left = out[:, 2 + k].astype(np.float32)
        for part in range(3):
            full[:, 8 + 3 * k + part] = bf16_of(left)
            left = left - full[:, 8 + 3 * k + part]
    return full


def bf16_of(val):
    return val.astype(jnp.bfloat16).astype(np.float32)


def feature_table():
    half = FREQ // 2
    rates = np.exp(-math.log(10000.0) * np.arange(half) / half)
    angles = np.arange(1024)[:, None] * rates[None, :]
    return np.concatenate([np.cos(angles), np.sin(angles)], axis=1).astype(jnp.bfloat16)


def position_table():
    half = D // 2
    rates = np.exp(-math.log(10000.0) * 2.0 * np.arange(half) / D)
    angles = np.arange(NTOK)[:, None] * rates[None, :]
    return np.concatenate([np.sin(angles), np.cos(angles)], axis=1).astype(np.float32)


def stages(size, pair_first):
    out, stride = [], 1
    if pair_first and size % 2 == 0:
        out.append((1, 2))
        stride, size = 2, size // 2
    while size > 1:
        step = 4 if size % 4 == 0 else 2
        out.append((stride, step))
        stride, size = stride * step, size // step
    return out


def axis_stages(axis):
    return stages(lax.axis_size(axis), axis == "fsdp")


def swap(val, axis, mask):
    size = lax.axis_size(axis)
    return lax.ppermute(val, axis, [(i, i ^ mask) for i in range(size)])


def place(axis, stride, size):
    return (lax.axis_index(axis) // stride) % size


def in_order(parts, pos):
    size = len(parts)
    if size == 2:
        return jnp.stack([lax.select(pos == 1, parts[1 - j], parts[j]) for j in range(2)])
    return jnp.stack([lax.select_n(pos, *[parts[j ^ p] for p in range(size)]) for j in range(size)])


def gather_open(val, axis, level):
    stride, size = list(reversed(axis_stages(axis)))[level]
    return [val] + [swap(val, axis, k * stride) for k in range(1, size)]


def gather_close(parts, axis, level):
    stride, size = list(reversed(axis_stages(axis)))[level]
    return in_order(parts, place(axis, stride, size))


def gather_shape(val, axis, shape):
    n = len(axis_stages(axis))
    order = tuple(reversed(range(n))) + tuple(range(n, n + len(shape)))
    return val.transpose(order).reshape((lax.axis_size(axis),) + shape)


def gather(val, axis):
    shape = val.shape
    for level in range(len(axis_stages(axis))):
        val = gather_close(gather_open(val, axis, level), axis, level)
    return gather_shape(val, axis, shape)


def reduce_stage(val, dim, axis, stride, size, send_type):
    pos = place(axis, stride, size)
    total = lax.dynamic_index_in_dim(val, pos, dim, keepdims=False).astype(F32)
    for k in range(1, size):
        piece = lax.dynamic_index_in_dim(val, pos ^ k, dim, keepdims=False)
        total = total + swap(piece.astype(send_type), axis, k * stride).astype(F32)
    return total


def reduce_open(val, axis, send_type):
    plan = axis_stages(axis)
    sizes = [s for _, s in reversed(plan)]
    val = val.reshape(tuple(sizes) + val.shape[1:])
    for dim in range(len(sizes) - 1, 0, -1):
        stride, size = plan[len(sizes) - 1 - dim]
        val = reduce_stage(val, dim, axis, stride, size, send_type)
    stride, size = plan[-1]
    pos = place(axis, stride, size)
    out = [lax.dynamic_index_in_dim(val, pos ^ k, 0, keepdims=False) for k in range(size)]
    return [out[0]] + [swap(out[k].astype(send_type), axis, k * stride) for k in range(1, size)]


def total_of(parts):
    return sum(p.astype(F32) for p in parts)


def reduce_parts(val, axis, send_type):
    return total_of(reduce_open(val, axis, send_type))


def after(val, *deps):
    return lax.optimization_barrier((val,) + deps)[0]


def tie(parts, *deps):
    return list(lax.optimization_barrier(tuple(parts) + deps)[: len(parts)])


def sum_all(val, axes):
    for axis in axes:
        for stride, size in axis_stages(axis):
            parts = [val] + [swap(val, axis, k * stride) for k in range(1, size)]
            while len(parts) > 1:
                parts = [parts[i] + parts[i + 1] for i in range(0, len(parts), 2)]
            val = parts[0]
    return val


def small_mesh(rows):
    return rows == 48 and lax.axis_size("dp") == CHUNKS and lax.axis_size("fsdp") == 8


def gather_z(whole):
    width = whole.shape[1] // CHUNKS
    chunk = lax.dynamic_slice_in_dim(whole, lax.axis_index("dp") * width, width, 1)
    parts = [chunk] + [swap(chunk, "fsdp", 2 * k) for k in (1, 2, 3)]
    return in_order(parts, place("fsdp", 2, 4))


def gather_dp(mine):
    return jnp.stack([mine] + [swap(mine, "dp", k) for k in (1, 2, 3)])


def gather_core(mine):
    return [mine, swap(mine, "fsdp", 1)]


def gather_whole(whole):
    return [lax.all_gather(whole, "fsdp", axis=0, tiled=True)]


def dot(a, b):
    return jnp.dot(a, b, preferred_element_type=F32)


def dot_nt(a, b):
    return lax.dot_general(a, b, (((1,), (1,)), ((), ())), preferred_element_type=F32)


def dot_tn(a, b):
    return lax.dot_general(a, b, (((0,), (0,)), ((), ())), preferred_element_type=F32)


def layer_norm(v):
    c = v - jnp.mean(v, axis=-1, keepdims=True)
    r = lax.rsqrt(jnp.mean(c * c, axis=-1, keepdims=True) + ln_eps)
    return c * r, r


def wcols(w, lo, hi):
    if len(w.shape) == 2:
        return w[:, lo:hi]
    return w[:, :, :, lo:hi].reshape(D, hi - lo)


def head_masks():
    lane = lax.broadcasted_iota(jnp.int32, (1, 2 * HDIM), 1)
    low = (lane < HDIM).astype(F32)
    return low, 1.0 - low


def each(fn, *vals):
    outs = [fn(t, *[v[t * NTOK : (t + 1) * NTOK] for v in vals]) for t in range(vals[0].shape[0] // NTOK)]
    return jnp.concatenate(outs, axis=0)


def flat(ref):
    return ref[...].reshape(ref.shape[0] * NTOK, ref.shape[-1])


def flat_cols(ref, lo, hi):
    return ref[:, :, lo:hi].reshape(ref.shape[0] * NTOK, hi - lo)


def unflat(val):
    return val.reshape(val.shape[0] // NTOK, NTOK, val.shape[-1])


QKV, OUT, UP, DOWN = (0, 3 * D), (3 * D, 4 * D), (4 * D, 4 * D + FF), (4 * D + FF, TOKW)
HALF = FF // 2


def block_forward(h, mod, w, bias, sv):
    qkv_ref, p_ref, o_ref, g_ref, gp_ref, att_ref, mlp_ref, h2_ref = sv
    y1, _ = layer_norm(h)
    n1 = each(lambda t, y: (y * (1.0 + mod(t, 1)) + mod(t, 0)).astype(BF16), y1)
    qkv_ref[...] = unflat(dot(n1, wcols(w, *QKV)).astype(BF16))
    masks = head_masks()
    for j in range(3):
        for t in range(h.shape[0] // NTOK):
            q2 = qkv_ref[t, :, 128 * j : 128 * j + 128]
            k2 = qkv_ref[t, :, D + 128 * j : D + 128 * j + 128]
            v2 = qkv_ref[t, :, 2 * D + 128 * j : 2 * D + 128 * j + 128]
            o2 = None
            for a in range(2):
                s = dot_nt(q2, k2 * (masks[a] * 0.125).astype(BF16))
                if bias is not None:
                    s = s + bias[t]
                e = jnp.exp(s - jnp.max(s, axis=-1, keepdims=True))
                p = (e * (1.0 / jnp.sum(e, axis=-1, keepdims=True))).astype(BF16)
                p_ref[t, 2 * j + a] = p
                part = dot(p, v2 * masks[a].astype(BF16))
                o2 = part if o2 is None else o2 + part
            o_ref[t, :, 128 * j : 128 * j + 128] = o2.astype(BF16)
    att = dot(flat(o_ref), wcols(w, *OUT))
    att_ref[...] = unflat(att.astype(BF16))
    h2 = each(lambda t, x, y: x + mod(t, 2) * y, h, att)
    h2_ref[...] = unflat(h2)
    y2, _ = layer_norm(h2)
    n2 = each(lambda t, y: (y * (1.0 + mod(t, 4)) + mod(t, 3)).astype(BF16), y2)
    for at in range(0, FF, HALF):
        u = dot(n2, wcols(w, UP[0] + at, UP[0] + at + HALF))
        u2 = u * u
        t = jnp.tanh(u * (GELU_C + (GELU_C * 0.044715) * u2))
        half = 0.5 * t + 0.5
        g_ref[:, :, at : at + HALF] = unflat((u * half).astype(BF16))
        gp = half + (u * (0.5 - 0.5 * t * t)) * (GELU_C + (3.0 * GELU_C * 0.044715) * u2)
        gp_ref[:, :, at : at + HALF] = unflat(gp.astype(BF16))
    mlp = dot_nt(flat(g_ref), wcols(w, *DOWN))
    mlp_ref[...] = unflat(mlp.astype(BF16))
    return each(lambda t, x, y: x + mod(t, 5) * y, h2, mlp)


def put_sums(put, i, val):
    for t in range(val.shape[0] // NTOK):
        put(t, i, jnp.sum(val[t * NTOK : (t + 1) * NTOK], axis=0, keepdims=True))


def norm_grad(dm, y, r, mod, i, put):
    put_sums(put, i, dm)
    put_sums(put, i + 1, dm * y)
    dy = each(lambda t, x: x * (1.0 + mod(t, i + 1)), dm)
    return r * (dy - jnp.mean(dy, axis=-1, keepdims=True) - y * jnp.mean(dy * y, axis=-1, keepdims=True))


def block_backward(d3, h, mod, w, sv, dw, du_ref, dqkv_ref, put):
    qkv_ref, p_ref, o_ref, g_ref, gp_ref, att_ref, mlp_ref, h2_ref = sv
    dmlp = each(lambda t, x: (x * mod(t, 5)).astype(BF16), d3)
    put_sums(put, 5, d3 * flat(mlp_ref).astype(F32))
    for at in range(0, FF, HALF):
        dg = dot(dmlp, wcols(w, DOWN[0] + at, DOWN[0] + at + HALF))
        du_ref[:, at : at + HALF] = (dg * flat_cols(gp_ref, at, at + HALF).astype(F32)).astype(BF16)
    dw[:, DOWN[0] : DOWN[1]] += dot_tn(dmlp, flat(g_ref))
    dn2 = dot_nt(du_ref[...], wcols(w, *UP))
    y2, r2 = layer_norm(flat(h2_ref))
    n2 = each(lambda t, y: (y * (1.0 + mod(t, 4)) + mod(t, 3)).astype(BF16), y2)
    dw[:, UP[0] : UP[1]] += dot_tn(n2, du_ref[...])
    d2 = d3 + norm_grad(dn2, y2, r2, mod, 3, put)
    datt = each(lambda t, x: (x * mod(t, 2)).astype(BF16), d2)
    put_sums(put, 2, d2 * flat(att_ref).astype(F32))
    do = dot_nt(datt, wcols(w, *OUT)).astype(BF16)
    dw[:, OUT[0] : OUT[1]] += dot_tn(flat(o_ref), datt)
    masks = head_masks()
    for j in range(3):
        for t in range(h.shape[0] // NTOK):
            rows = slice(t * NTOK, (t + 1) * NTOK)
            q2 = qkv_ref[t, :, 128 * j : 128 * j + 128]
            k2 = qkv_ref[t, :, D + 128 * j : D + 128 * j + 128]
            v2 = qkv_ref[t, :, 2 * D + 128 * j : 2 * D + 128 * j + 128]
            do2 = do[rows, 128 * j : 128 * j + 128]
            dq2, dk2, dv2 = 0.0, 0.0, 0.0
            for a in range(2):
                one = masks[a].astype(BF16)
                eighth = (masks[a] * 0.125).astype(BF16)
                pb = p_ref[t, 2 * j + a]
                p = pb.astype(F32)
                dp = dot_nt(do2, v2 * one)
                ds = (p * (dp - jnp.sum(p * dp, axis=-1, keepdims=True))).astype(BF16)
                dq2 += dot(ds, k2 * eighth)
                dk2 += dot_tn(ds, q2 * eighth)
                dv2 += dot_tn(pb, do2 * one)
            dqkv_ref[rows, 128 * j : 128 * j + 128] = dq2.astype(BF16)
            dqkv_ref[rows, D + 128 * j : D + 128 * j + 128] = dk2.astype(BF16)
            dqkv_ref[rows, 2 * D + 128 * j : 2 * D + 128 * j + 128] = dv2.astype(BF16)
    dn1 = dot_nt(dqkv_ref[...], wcols(w, *QKV))
    y1, r1 = layer_norm(h)
    n1 = each(lambda t, y: (y * (1.0 + mod(t, 1)) + mod(t, 0)).astype(BF16), y1)
    dw[:, QKV[0] : QKV[1]] += dot_tn(n1, dqkv_ref[...])
    return d2 + norm_grad(dn1, y1, r1, mod, 0, put)


def weight_copies(ids, pieces, w, sems, base):
    copies = []
    if len(pieces) == 1:
        for n, (lo, hi) in enumerate((QKV, OUT, UP, (DOWN[0], w.shape[1]))):
            copies.append(pltpu.make_async_copy(pieces[0].at[:, base + lo : base + hi], w.at[:, lo:hi], sems.at[n]))
        return [[c] for c in copies]
    for c in range(2):
        core = ids[2] ^ c
        for k in range(4):
            at = pl.multiple_of((ids[1] ^ k) * CW, 128)
            copies.append(pltpu.make_async_copy(pieces[c].at[k, :, :, 0:CW], w.at[:, core, :, pl.ds(at, CW)], sems.at[4 * c + k]))
        copies.append(pltpu.make_async_copy(pieces[c].at[0, :, :, CW:], w.at[:, core, :, TOKW:], sems.at[8 + c]))
    return [copies, [], [], []]


def load_weights(ids, pieces, w, sems, base=0, work=None):
    first = pl.program_id(0) == 0

    @pl.when(first)
    def _():
        copies = [c for part in weight_copies(ids, pieces, w, sems, base) for c in part]
        for copy in copies:
            copy.start()
        if work is not None:
            work()
        for copy in copies:
            copy.wait()


def mod_row(mods, base, slot):
    return lambda t, i: mods[pl.ds(slot + t, 1), base + D * i : base + D * i + D]


def row_writer(dmod, slot):
    def write(t, i, val):
        dmod[pl.ds(slot + t, 1), D * i : D * i + D] = val

    return write


def token_row(misc):
    lane = lax.broadcasted_iota(jnp.int32, (8, 128), 1)
    return dot_nt((lane == PIN).astype(BF16), misc[...])[0:1, :]


def enc_forward_kernel(n, ids, xin, pe, mods, bias, *rest):
    pieces, (misc, h0, h3), sv, (w, sems) = rest[:n], rest[n : n + 3], rest[n + 3 : n + 11], rest[n + 11 :]
    load_weights(ids, pieces, w, sems)
    step = pl.program_id(0)
    slot = step * xin.shape[0]

    @pl.when(step == 0)
    def _():
        misc[...] = wcols(w, TOKW, TOKW + 128)

    @pl.when(slot < ids[0])
    def _():
        h = each(lambda t, x: x + pe[...], dot_nt(flat(xin), misc[...]))
        h0[...] = unflat(h)
        h3[...] = unflat(block_forward(h, mod_row(mods, 0, slot), w, bias, sv))


def side_forward_kernel(n, ids, h_in, mask, pe, misc, mods, *rest):
    pieces, (hs, h3), sv, (w, sems) = rest[:n], rest[n : n + 2], rest[n + 2 : n + 10], rest[n + 10 :]
    load_weights(ids, pieces, w, sems)
    step = pl.program_id(0)
    slot = step * h_in.shape[0]

    @pl.when(slot < ids[0])
    def _():
        token = token_row(misc) + pe[...]
        h = each(lambda t, x: x * (1.0 - mask[t]) + mask[t] * token, flat(h_in))
        hs[...] = unflat(h)
        h3[...] = unflat(block_forward(h, mod_row(mods, 0, slot), w, None, sv))


def store_grads(ids, dw, outs):
    def cols(rows, j):
        return dw[rows, j * CW : (j + 1) * CW].astype(BF16)

    extra = dw.shape[1] > TOKW
    zero = jnp.zeros((D // 8, 128), BF16)
    if len(outs) == 1:
        for j in range(CHUNKS):
            outs[0][j, :, 0:CW] = cols(slice(None), j)
            if extra:
                outs[0][j, :, CW:] = dw[:, TOKW:].astype(BF16) if j == 0 else jnp.zeros((D, 128), BF16)
        return
    for side in range(2):
        for z in range(4):
            rows = pl.ds(pl.multiple_of((2 * z + (ids[2] ^ side)) * (D // 8), 16), D // 8)
            for j in range(CHUNKS):
                outs[side][j, z, :, 0:CW] = cols(rows, j)
                if extra:
                    outs[side][j, z, :, CW:] = dw[rows, TOKW:].astype(BF16) if j == 0 else zero


def dec_kernel(n, m, ids, coef, h_in, noise, misc, mods, *rest):
    pieces = rest[:n]
    d_in, dmod, dmisc, loss = rest[n : n + 4]
    dw_out = rest[n + 4 : n + 4 + m]
    w, sems, dw, du, dqkv = rest[n + 4 + m : n + 9 + m]
    sv = rest[n + 9 + m :]
    step = pl.program_id(0)
    slot = step * h_in.shape[0]

    def clear():
        dw[...] = jnp.zeros_like(dw)
        dmisc[...] = jnp.zeros_like(dmisc)
        loss[...] = jnp.zeros_like(loss)
        dmod[...] = jnp.zeros_like(dmod)

    load_weights(ids, pieces, w, sems, TOKW, clear)

    @pl.when(slot < ids[0])
    def _():
        row = mod_row(mods, 6 * D, slot)
        put = row_writer(dmod, slot)
        h = flat(h_in)
        h_dec = block_forward(h, row, w, None, sv)
        yf, rf = layer_norm(h_dec)
        nf = each(lambda t, y: (y * (1.0 + row(t, 7)) + row(t, 6)).astype(BF16), yf)
        lane = lax.broadcasted_iota(jnp.int32, (1, 128), 1)

        def head(t, out):
            ln_b, ln_pv, wmean = coef[slot + t, 0], coef[slot + t, 1], coef[slot + t, 2]
            live = (lane >= 32) & (lane < 32 + PIN) & (slot + t < ids[0])
            d = jnp.where(live, out - noise[t], 0.0)
            vf = (pltpu.roll(out, 128 - 32, 1) + 1.0) * 0.5
            vf = jnp.where(live, vf, 0.0)
            lv = vf * ln_b + (1.0 - vf) * ln_pv
            first = jnp.exp(ln_pv - lv)
            second = wmean * jnp.exp(-lv)
            inv = 0.5 / math.log(2.0)
            dd = d * d
            kl = inv * (-1.0 + lv - ln_pv + first + dd * second)
            term = jnp.where(live, dd + kl, 0.0)
            loss[...] += jnp.sum(term.reshape(NTOK // 8, 8, 128), axis=0)
            deps = d * (2.0 + (2.0 * inv) * second)
            dlog = inv * (1.0 - first - dd * second) * (0.5 * (ln_b - ln_pv))
            dlog = jnp.where(live, dlog, 0.0)
            return (deps + pltpu.roll(dlog, 32, 1)).astype(BF16)

        dout = each(head, dot(nf, misc[...]))
        dmisc[...] += dot_tn(nf, dout)
        d3 = norm_grad(dot_nt(dout, misc[...]), yf, rf, row, 6, put)
        d_in[...] = unflat(block_backward(d3, h, row, w, sv, dw, du, dqkv, put))

    @pl.when(step == pl.num_programs(0) - 1)
    def _():
        store_grads(ids, dw, dw_out)


def side_backward_kernel(n, m, ids, d_out, h_in, mask, mods, *rest):
    sv, pieces, rest = rest[:8], rest[8 : 8 + n], rest[8 + n :]
    d_enc, dmod, dtok = rest[:3]
    dw_out = rest[3 : 3 + m]
    w, sems, dw, du, dqkv = rest[3 + m :]
    step = pl.program_id(0)
    slot = step * h_in.shape[0]

    def clear():
        dw[...] = jnp.zeros_like(dw)
        dtok[...] = jnp.zeros_like(dtok)
        dmod[...] = jnp.zeros_like(dmod)

    load_weights(ids, pieces, w, sems, 0, clear)

    @pl.when(slot < ids[0])
    def _():
        dh = block_backward(flat(d_out), flat(h_in), mod_row(mods, 0, slot), w, sv, dw, du, dqkv, row_writer(dmod, slot))
        dm = each(lambda t, x: x * mask[t], dh)
        dtok[...] += jnp.sum(dm.reshape(-1, 8, D), axis=0)
        d_enc[...] = unflat(dh - dm)

    @pl.when(step == pl.num_programs(0) - 1)
    def _():
        store_grads(ids, dw, dw_out)


def enc_backward_kernel(n, m, ids, d_out, h_in, xin, mods, dmisc, dtok, *rest):
    sv, pieces, rest = rest[:8], rest[8 : 8 + n], rest[8 + n :]
    dmod = rest[0]
    dw_out = rest[1 : 1 + m]
    w, sems, dw, du, dqkv = rest[1 + m :]
    step = pl.program_id(0)
    slot = step * h_in.shape[0]

    def clear():
        dw[...] = jnp.zeros_like(dw)
        dmod[...] = jnp.zeros_like(dmod)
        lane = lax.broadcasted_iota(jnp.int32, (8, 128), 1)
        token = lax.dot_general(
            dtok[...], (lane == PIN).astype(F32), (((0,), (0,)), ((), ())), precision=lax.Precision.HIGHEST, preferred_element_type=F32
        )
        dw[:, TOKW:] = dmisc[...] + token

    load_weights(ids, pieces, w, sems, 0, clear)

    @pl.when(slot < ids[0])
    def _():
        dh = block_backward(flat(d_out), flat(h_in), mod_row(mods, 0, slot), w, sv, dw, du, dqkv, row_writer(dmod, slot))
        dw[:, TOKW:] += dot_tn(dh.astype(BF16), flat(xin))

    @pl.when(step == pl.num_programs(0) - 1)
    def _():
        store_grads(ids, dw, dw_out)


def assign_kernel(nf, slots, me, packed, features, tone, ttwo, classes, mine, info_out, c_part, c_own, a_pre_out, a_out, feat_out, hot_out, pick_out):
    lats = packed.shape[0]
    info = packed[:, NTOK * PIN + NTOK :]
    used = info[:, 0:1]
    src = lax.broadcasted_iota(jnp.int32, (lats, lats), 0)
    dst = lax.broadcasted_iota(jnp.int32, (lats, lats), 1)
    before = dot((dst < src).astype(BF16), jnp.broadcast_to(used, (lats, 128)))[:, 0:1]
    turn = jnp.floor((before + 0.5) * (1.0 / nf))
    target = (before - nf * turn) * 8.0 + turn
    live = used.astype(F32) > 0.5
    pick = jnp.where(live & (target == dst.astype(F32)), 1.0, 0.0).astype(BF16)
    moved = dot_tn(pick, info)
    step_of = moved[:, 1:2] * 32.0 + moved[:, 2:3]
    label_of = moved[:, 3:4] * 32.0 + moved[:, 4:5]
    wide = lax.broadcasted_iota(jnp.int32, (lats, 1024), 1).astype(F32)
    hot_t = jnp.where(wide == step_of, 1.0, 0.0).astype(BF16)
    hot_l = jnp.where(wide == label_of, 1.0, 0.0).astype(BF16)
    feat = dot(hot_t, features[...]).astype(BF16)
    a_pre = dot_nt(tone[...], feat)
    a_act = (a_pre * jax.nn.sigmoid(a_pre)).astype(BF16)
    c_part[...] = dot_tn(ttwo[...], a_act)
    c_own[...] = dot_nt(classes[...], hot_l)
    a_pre_out[...] = a_pre
    a_out[...] = a_act
    feat_out[...] = feat
    hot_out[...] = hot_l
    lane8 = lax.broadcasted_iota(jnp.int32, (lats, 8), 1) + me[0] * 8
    pick_me = jnp.where(live & (target == lane8.astype(F32)), 1.0, 0.0).astype(BF16)
    mine[...] = dot_tn(pick_me, packed[:, : NTOK * PIN + NTOK]).astype(BF16)
    info_out[...] = dot_tn(pick_me, info)
    pick_out[...] = pick_me


SMEM = pl.BlockSpec(memory_space=pltpu.SMEM)
ANY = pl.BlockSpec(memory_space=pl.ANY)


def slot_spec(*shape, together=1):
    def index(s, ids):
        return (jnp.minimum(s, jnp.maximum((ids[0] + together - 1) // together - 1, 0)),) + (0,) * len(shape)

    return pl.BlockSpec((together,) + shape, index)


def fixed_spec(*shape):
    return pl.BlockSpec(shape, lambda s, ids: (0,) * len(shape))


SAVES = (
    ((NTOK, 3 * D), BF16),
    ((HEADS, NTOK, NTOK), BF16),
    ((NTOK, D), BF16),
    ((NTOK, FF), BF16),
    ((NTOK, FF), BF16),
    ((NTOK, D), BF16),
    ((NTOK, D), BF16),
    ((NTOK, D), F32),
)


def weight_scratch(pieces, width):
    shape = (D, width) if len(pieces) == 1 else (4, 2, D // 8, width)
    return [pltpu.VMEM(shape, BF16), pltpu.SemaphoreType.DMA((10,))]


def grad_scratch(width, together=1):
    return [
        pltpu.VMEM((D, width), F32),
        pltpu.VMEM((together * NTOK, FF), BF16),
        pltpu.VMEM((together * NTOK, 3 * D), BF16),
    ]


def grad_outs(split, width):
    if split:
        return [fixed_out((CHUNKS, 4, D // 8, width), BF16)] * 2
    return [fixed_out((CHUNKS, D, width), BF16)]


def call(kernel, slots, ids, in_specs, args, pieces, outs, scratch, macs, together=1):
    specs = list(in_specs) + [ANY] * len(pieces)
    return pl.pallas_call(
        functools.partial(kernel, len(pieces)),
        grid_spec=pltpu.PrefetchScalarGridSpec(
            num_scalar_prefetch=1,
            grid=(slots // together,),
            in_specs=specs,
            out_specs=[o[0] for o in outs],
            scratch_shapes=scratch,
        ),
        out_shape=[jax.ShapeDtypeStruct(o[1], o[2]) for o in outs],
        compiler_params=pltpu.CompilerParams(vmem_limit_bytes=VMEM_LIMIT, dimension_semantics=("arbitrary",)),
        cost_estimate=pl.CostEstimate(flops=int(macs * slots // 2), bytes_accessed=int(4e6), transcendentals=0),
    )(ids, *args, *pieces)


def slot_out(slots, shape, kind, together=1):
    return (slot_spec(*shape, together=together), (slots,) + shape, kind)


def fixed_out(shape, kind):
    return (fixed_spec(*shape), shape, kind)


BLOCK_MACS = NTOK * (D * TOKW + 2 * NTOK * D)
MODS_E = (8, 6 * D)
MODS_R = (8, 14 * D)


def enc_forward(slots, ids, xin, pe, mods, bias, pieces):
    return call(
        enc_forward_kernel,
        slots,
        ids,
        [slot_spec(NTOK, 128), fixed_spec(NTOK, D), fixed_spec(*MODS_E), slot_spec(1, NTOK)],
        [xin, pe, mods, bias],
        pieces,
        [fixed_out((D, 128), BF16)] + [slot_out(slots, (NTOK, D), F32)] * 2 + [slot_out(slots, s, k) for s, k in SAVES],
        weight_scratch(pieces, TOKW + 128),
        BLOCK_MACS,
    )


def side_forward(slots, ids, h_in, mask, pe, misc, mods, pieces):
    return call(
        side_forward_kernel,
        slots,
        ids,
        [slot_spec(NTOK, D), slot_spec(NTOK, 1), fixed_spec(NTOK, D), fixed_spec(D, 128), fixed_spec(*MODS_R)],
        [h_in, mask, pe, misc, mods],
        pieces,
        [slot_out(slots, (NTOK, D), F32)] * 2 + [slot_out(slots, s, k) for s, k in SAVES],
        weight_scratch(pieces, TOKW),
        BLOCK_MACS,
    )


def dec_both(slots, ids, coef, h_in, noise, misc, mods, pieces, split):
    outs = grad_outs(split, CW)
    pair = 2 if slots % 2 == 0 else 1
    return call(
        lambda n, *refs: dec_kernel(n, len(outs), *refs),
        slots,
        ids,
        [SMEM, slot_spec(NTOK, D, together=pair), slot_spec(NTOK, 128, together=pair), fixed_spec(D, 128), fixed_spec(*MODS_R)],
        [coef, h_in, noise, misc, mods],
        pieces,
        [slot_out(slots, (NTOK, D), F32, pair), fixed_out((8, 8 * D), F32), fixed_out((D, 128), F32), fixed_out((8, 128), F32)] + outs,
        weight_scratch(pieces, TOKW) + grad_scratch(TOKW, pair) + [pltpu.VMEM((pair,) + s, k) for s, k in SAVES],
        3 * BLOCK_MACS,
        pair,
    )


def side_backward(slots, ids, d_out, h_in, mask, mods, saves, pieces, split):
    outs = grad_outs(split, CW)
    return call(
        lambda n, *refs: side_backward_kernel(n, len(outs), *refs),
        slots,
        ids,
        [slot_spec(NTOK, D), slot_spec(NTOK, D), slot_spec(NTOK, 1), fixed_spec(*MODS_R)] + [slot_spec(*s) for s, _ in SAVES],
        [d_out, h_in, mask, mods] + list(saves),
        pieces,
        [slot_out(slots, (NTOK, D), F32), fixed_out((8, 6 * D), F32), fixed_out((8, D), F32)] + outs,
        weight_scratch(pieces, TOKW) + grad_scratch(TOKW),
        2 * BLOCK_MACS,
    )


def enc_backward(slots, ids, d_out, h_in, xin, mods, dmisc, dtok, saves, pieces, split):
    outs = grad_outs(split, CW + 128)
    return call(
        lambda n, *refs: enc_backward_kernel(n, len(outs), *refs),
        slots,
        ids,
        [slot_spec(NTOK, D), slot_spec(NTOK, D), slot_spec(NTOK, 128), fixed_spec(*MODS_E), fixed_spec(D, 128), fixed_spec(8, D)]
        + [slot_spec(*s) for s, _ in SAVES],
        [d_out, h_in, xin, mods, dmisc, dtok] + list(saves),
        pieces,
        [fixed_out((8, 6 * D), F32)] + outs,
        weight_scratch(pieces, TOKW + 128) + grad_scratch(TOKW + 128),
        2 * BLOCK_MACS,
    )


def assign(nf, slots, me, packed, tone, ttwo, classes):
    lats, rows = packed.shape[0], tone.shape[0]
    out = [
        ((8, NTOK * PIN + NTOK), BF16),
        ((8, 128), F32),
        ((D, lats), F32),
        ((rows, lats), F32),
        ((rows, lats), F32),
        ((rows, lats), BF16),
        ((lats, FREQ), BF16),
        ((lats, 1024), BF16),
        ((lats, 8), BF16),
    ]
    vmem = pl.BlockSpec(memory_space=pltpu.VMEM)
    return pl.pallas_call(
        functools.partial(assign_kernel, nf, slots),
        in_specs=[SMEM] + [vmem] * 5,
        out_specs=[vmem] * len(out),
        out_shape=[jax.ShapeDtypeStruct(s, k) for s, k in out],
        compiler_params=pltpu.CompilerParams(vmem_limit_bytes=VMEM_LIMIT),
    )(me, packed, jnp.asarray(feature_table()), tone, ttwo, classes)


def silu_slope(val):
    s = jax.nn.sigmoid(val)
    return s * (1.0 + val * (1.0 - s))


def adam(master, first_m, second, grad_in):
    first_new = beta_one * first_m + (1.0 - beta_one) * grad_in
    second_new = beta_two * second + (1.0 - beta_two) * grad_in * grad_in
    first_hat = first_new / (1.0 - beta_one**STEP)
    second_hat = second_new / (1.0 - beta_two**STEP)
    master_new = master - learn_rate * (first_hat / (jnp.sqrt(second_hat) + adam_eps) + weight_decay * master)
    return [master_new, first_new, second_new]


def grad_core(dw, *deps):
    if len(dw) == 1:
        return dw
    keep, send = dw
    if deps:
        send = after(send, *deps)
    return [keep, swap(send, "fsdp", 1)]


def grad_dp(parts):
    if len(parts) == 1:
        return parts
    keep, got = parts
    me = lax.axis_index("dp")

    def piece(k):
        return lax.dynamic_index_in_dim(keep, me ^ k, 0, False).astype(F32) + lax.dynamic_index_in_dim(got, me ^ k, 0, False).astype(F32)

    return [piece(0).astype(BF16)] + [swap(piece(k).astype(BF16), "dp", k) for k in (1, 2, 3)]


def grad_sum(parts):
    if len(parts) == 1:
        return parts[0]
    return sum(p.astype(F32) for p in parts)


def grad_z(part):
    if part.shape[0] == CHUNKS and part.shape[1] == D:
        part = lax.psum_scatter(part, "fsdp", scatter_dimension=1, tiled=True)
        return reduce_stage(part, 0, "dp", 1, CHUNKS, BF16).astype(BF16)
    return reduce_stage(part, 0, "fsdp", 2, 4, BF16).astype(BF16)


def dp_share(val):
    rows = val.shape[0]
    return reduce_stage(val.reshape(rows, CHUNKS, -1).transpose(1, 0, 2), 0, "dp", 1, CHUNKS, BF16).astype(BF16)


def columns(parts, lo, hi):
    return jnp.concatenate([parts[j, :, lo:hi] for j in range(CHUNKS)], axis=1)


def on_device(latents, noise, timesteps, labels, patch_mask, counts, owners, tables_w, tables_m, tables_v, rows_w, rows_m, rows_v, down_w, down_m, down_v):
    nd, nf = lax.axis_size("dp"), lax.axis_size("fsdp")
    me_d, me_f = lax.axis_index("dp"), lax.axis_index("fsdp")
    rows = tables_w.shape[0]
    micro, per = latents.shape[0], latents.shape[1]
    slots = micro * per
    split = small_mesh(rows)

    steps = timesteps.reshape(slots)
    names = labels.reshape(slots)
    plan = jnp.take(jnp.asarray(plan_table()), steps, axis=0)
    used = (jnp.arange(per)[None, :] < counts).astype(jnp.int32).reshape(slots)
    x_zero, eps = latents.reshape(slots, NTOK * PIN), noise.reshape(slots, NTOK * PIN)
    x_in = (plan[:, 0:1] * x_zero + plan[:, 1:2] * eps).astype(BF16)
    words = jnp.stack([used, steps // 32, steps % 32, names // 32, names % 32], axis=1).astype(BF16)
    words = jnp.concatenate([words, jnp.zeros((slots, 3), BF16), plan[:, 8:].astype(BF16)], axis=1)
    packed = jnp.concatenate([x_in, patch_mask.reshape(slots, NTOK).astype(BF16), words], axis=1)
    packed = jnp.pad(packed, ((0, 8 - slots), (0, 0)))
    eps = jnp.pad(eps.astype(BF16), ((0, 8 - slots), (0, 0)))
    packed = gather(packed, "fsdp").reshape(nf * 8, -1)
    wholes = []

    rows_b, down_b, tables_b = rows_w.astype(BF16), down_w.astype(BF16), tables_w.astype(BF16)
    head_at = D + 3 * STRIDE + 2 * D
    gap = jnp.zeros((rows, 16), BF16)
    misc_own = jnp.concatenate(
        [tables_b[:, : PIN + 1], gap[:, :15], rows_b[:, head_at : head_at + PIN], gap, rows_b[:, head_at + PIN : head_at + 2 * PIN], gap, gap, gap],
        axis=1,
    )
    for b in range(3):
        at = D + b * STRIDE
        row_part, down_part = rows_b[:, at : at + 4 * D + FF], down_b[:, b * FF : (b + 1) * FF]
        cols = [row_part[:, :CW], row_part[:, CW : 2 * CW], row_part[:, 2 * CW :], down_part[:, :D], down_part[:, D:]]
        if b == 0 and split:
            cols = [cols[0], misc_own, cols[1], misc_own, cols[2], cols[3], misc_own, cols[4], misc_own]
        elif b == 0:
            cols = cols + [misc_own]
        whole = jnp.concatenate(cols, axis=1)
        wholes.append(whole)
    enc_z = gather_z(wholes[0]) if split else None
    late_w = gather_whole(jnp.concatenate(wholes[1:], axis=1))

    w_tone = tables_b[:, PIN + 1 : PIN + 1 + FREQ]
    class_tab = jnp.pad(tables_b[:, PIN + 1 + FREQ :], ((0, 0), (0, 1024 - CLASSES)))
    w_ttwo = rows_b[:, :D]
    ada_at = [D + b * STRIDE + 4 * D + FF for b in range(3)]
    fin_at = D + 3 * STRIDE
    w_ada = jnp.concatenate([rows_b[:, a : a + 6 * D] for a in ada_at] + [rows_b[:, fin_at : fin_at + 2 * D]], axis=1)
    me = me_f.astype(jnp.int32).reshape(1)
    mine, info, c_part, c_own, a_pre, a_act, feat, hot, pick = assign(nf, slots, me, packed, w_tone, w_ttwo, class_tab)
    cond = reduce_parts(c_part.reshape(nf, rows, nf * 8), "fsdp", F32) + c_own
    s_cond = jax.nn.silu(cond).astype(BF16)
    mods_e = reduce_parts(dot_tn(s_cond, w_ada[:, : 6 * D]).reshape(nf, 8, 6 * D), "fsdp", BF16)
    if split:
        enc_w = gather_core(after(gather_dp(after(enc_z, c_part)), s_cond))
    else:
        enc_w = gather_whole(wholes[0])
    mods_r = reduce_open(dot_tn(s_cond, w_ada[:, 6 * D :]).reshape(nf, 8, 14 * D), "fsdp", BF16)

    work = jnp.sum(info[:, 0]).astype(jnp.int32)
    ids = jnp.stack([work, me_d.astype(jnp.int32), (me_f % 2).astype(jnp.int32)])
    coef = jnp.stack([info[:, 8 + 3 * k] + info[:, 9 + 3 * k] + info[:, 10 + 3 * k] for k in range(3)], axis=1)
    size = NTOK * PIN
    x_in = jnp.pad(mine[:slots, :size].reshape(slots, NTOK, PIN), ((0, 0), (0, 0), (0, 128 - PIN)))
    masked = mine[:slots, size:].astype(F32)
    bias = (-1e9 * masked)[:, None, :]
    mask_col = masked[:, :, None]
    pe = jnp.asarray(position_table())

    last = len(axis_stages("fsdp")) - 1
    misc, h0, h_enc, *save_e = enc_forward(slots, ids, x_in, pe, mods_e, bias, enc_w)
    mods_r = total_of(tie(mods_r, misc))
    level = gather_open(after(eps, mods_r), "fsdp", 0)
    hs, h_side, *save_s = side_forward(slots, ids, h_enc, mask_col, pe, misc, mods_r, late_w)
    level = tie(level, hs)
    for at in range(last):
        level = gather_open(gather_close(level, "fsdp", at), "fsdp", at + 1)
    eps = gather_shape(gather_close(level, "fsdp", last), "fsdp", (8, size)).reshape(nf * 8, size)
    eps = dot_tn(pick, eps)[:slots].reshape(slots, NTOK, PIN)
    eps = jnp.pad(eps, ((0, 0), (0, 0), (32, 96 - PIN)))

    d_side, dmod_d, dmisc, loss, *dw_d = dec_both(slots, ids, coef, h_side, eps, misc, mods_r, late_w, False)
    mine_d = lax.psum_scatter(dw_d[0], "fsdp", scatter_dimension=1, tiled=True)
    d_enc, dmod_s, dtok, *dw_s = side_backward(slots, ids, d_side, hs, mask_col, mods_r, save_s, late_w, split)
    part_s = grad_dp(grad_core(dw_s))
    d_enc = after(d_enc, part_s[0])
    dmod_e, *dw_e = enc_backward(slots, ids, d_enc, h0, x_in, mods_e, dmisc, dtok, save_e, enc_w, split)
    total_s = grad_sum(tie(part_s, dmod_e, mine_d))
    dmods = jnp.concatenate([dmod_e, dmod_s, dmod_d], axis=1).astype(BF16)
    level = gather_open(after(dmods, total_s), "fsdp", 0)
    core_e = grad_core(dw_e, total_s)
    if split:
        core_e[1] = after(core_e[1], *level[1:])
    part_e = grad_dp(core_e)

    level = tie(level, part_e[0])
    for at in range(last):
        level = gather_open(gather_close(level, "fsdp", at), "fsdp", at + 1)
    dm_all = gather_shape(gather_close(level, "fsdp", last), "fsdp", dmods.shape).reshape(nf * 8, -1)
    d_cond = dot_nt(w_ada, dm_all) * silu_slope(cond)
    d_cond_all = gather(d_cond.astype(BF16), "fsdp").reshape(D, nf * 8)
    d_apre = (dot(w_ttwo, d_cond_all) * silu_slope(a_pre)).astype(BF16)
    g_class = jnp.dot(d_cond, hot.astype(F32), precision=lax.Precision.HIGHEST, preferred_element_type=F32)
    kinds = [dot(s_cond, dm_all), dot_nt(a_act, d_cond_all), dot(d_apre, feat), g_class, jnp.zeros((rows, 128), F32)]
    kinds = jnp.concatenate([k.astype(BF16) for k in kinds], axis=1).reshape(rows, CHUNKS, -1).transpose(1, 0, 2)

    g_side = grad_z(after(total_s, d_cond)) if split else grad_z(total_s)
    total_e = grad_sum(tie(part_e, d_cond_all))
    g_enc = grad_z(total_e)
    g_dec = total_of(reduce_open(after(mine_d, total_e), "dp", BF16)).astype(BF16)
    first = jnp.concatenate([g_side, g_dec], axis=1)
    full = gather_open(first, "dp", 0)
    g_other = total_of(reduce_open(after(kinds, full[0]), "dp", BF16)).astype(BF16)
    second = after(jnp.concatenate([g_enc, g_other], axis=1), *full)
    full = gather_shape(gather_close(full, "dp", 0), "dp", first.shape)
    squares = jnp.sum(jnp.square(first.astype(F32))) + jnp.sum(jnp.square(second.astype(F32)))
    norm_sq, loss_sum, count = sum_all(jnp.stack([squares, jnp.sum(loss), jnp.sum(used).astype(F32)]), ("fsdp", "dp"))
    rest = gather(second, "dp")
    scale = 1.0 / (count * (NTOK * PIN))
    loss_out = loss_sum * scale
    grad_norm = jnp.sqrt(norm_sq) * scale
    factor = scale * jnp.minimum(1.0, clip_level / (grad_norm + 1e-06))

    up = 4 * D + FF
    wide_e = CW + 128
    f_side, f_dec = columns(full, 0, CW), columns(full, CW, 2 * CW)
    f_enc, small = columns(rest, 0, CW), rest[0, :, CW:wide_e]
    f_rest = columns(rest, wide_e, rest.shape[2])
    at = 20 * D
    ttwo, tone, klass = f_rest[:, at : at + D], f_rest[:, at + D : at + D + FREQ], f_rest[:, at + D + FREQ : at + D + FREQ + CLASSES]
    rows_g = [ttwo, f_enc[:, :up], f_rest[:, : 6 * D], f_side[:, :up], f_rest[:, 6 * D : 12 * D], f_dec[:, :up], f_rest[:, 12 * D : 20 * D]]
    rows_g = jnp.concatenate(rows_g + [small[:, 32 : 32 + PIN], small[:, 64 : 64 + PIN]], axis=1)
    down_g = jnp.concatenate([blk[:, up:] for blk in (f_enc, f_side, f_dec)], axis=1)
    tables_g = jnp.concatenate([small[:, : PIN + 1], tone, klass], axis=1)
    results = adam(tables_w, tables_m, tables_v, factor * tables_g.astype(F32))

    def own(val):
        size = val.shape[1] // nd
        return lax.dynamic_slice_in_dim(val, me_d * size, size, 1)

    results += adam(own(rows_w), own(rows_m), own(rows_v), factor * own(rows_g).astype(F32))
    results += adam(own(down_w), own(down_m), own(down_v), factor * own(down_g).astype(F32))
    return tuple([loss_out, grad_norm] + results)


def solution(mesh):
    lat = P(None, ("dp", "fsdp"), None)
    num = P(None, ("dp", "fsdp"))
    row = P("fsdp", None)
    both = P("fsdp", "dp")
    return jax.shard_map(
        on_device,
        mesh=mesh,
        in_specs=(lat, lat, num, num, lat, num, P()) + (row,) * 9,
        out_specs=(P(), P()) + (row,) * 3 + (both,) * 6,
        check_vma=False,
    )
```

```python
import functools
import math

import jax
import jax.numpy as jnp
import numpy as np
from jax import lax
from jax.experimental import pallas as pl
from jax.experimental.pallas import tpu as pltpu
from jax.sharding import PartitionSpec as P

D = 384
HEADS = 6
HDIM = 64
FF = 1536
NTOK = 256
PIN = 16
FREQ = 256
CLASSES = 1000
TSTEPS = 1000
STEP = 10
POUT = 32

beta_one = 0.9
beta_two = 0.999
adam_eps = 1e-08
learn_rate = 0.05
weight_decay = 0.1
clip_level = 0.005
ln_eps = 1e-06

F32 = jnp.float32
BF16 = jnp.bfloat16
STRIDE = 10 * D + FF
TOKW = 3 * D + D + FF + FF
CHUNKS = 4
CW = TOKW // CHUNKS
GELU_C = math.sqrt(2.0 / math.pi)
VMEM_LIMIT = 60 * 1024 * 1024


def plan_table():
    j = np.arange(TSTEPS, dtype=np.float64)
    beta = 0.0001 + (0.02 - 0.0001) * j / (TSTEPS - 1)
    abar = np.cumprod(1.0 - beta)
    prev = np.concatenate([[1.0], abar[:-1]])
    out = np.zeros((TSTEPS, 5), np.float64)
    out[:, 0] = np.sqrt(abar)
    out[:, 1] = np.sqrt(1.0 - abar)
    out[1:, 2] = np.log(beta[1:])
    out[1:, 3] = np.log(beta[1:] * (1.0 - prev[1:]) / (1.0 - abar[1:]))
    out[1:, 4] = prev[1:] * beta[1:] ** 2 / ((1.0 - abar[1:]) * abar[1:])
    full = np.zeros((TSTEPS, 128), np.float32)
    full[:, 0:2] = out[:, 0:2]
    for k in range(3):
        left = out[:, 2 + k].astype(np.float32)
        for part in range(3):
            full[:, 8 + 3 * k + part] = bf16_of(left)
            left = left - full[:, 8 + 3 * k + part]
    return full


def bf16_of(val):
    return val.astype(jnp.bfloat16).astype(np.float32)


def feature_table():
    half = FREQ // 2
    rates = np.exp(-math.log(10000.0) * np.arange(half) / half)
    angles = np.arange(1024)[:, None] * rates[None, :]
    return np.concatenate([np.cos(angles), np.sin(angles)], axis=1).astype(jnp.bfloat16)


def position_table():
    half = D // 2
    rates = np.exp(-math.log(10000.0) * 2.0 * np.arange(half) / D)
    angles = np.arange(NTOK)[:, None] * rates[None, :]
    return np.concatenate([np.sin(angles), np.cos(angles)], axis=1).astype(np.float32)


def stages(size, pair_first):
    out, stride = [], 1
    if pair_first and size % 2 == 0:
        out.append((1, 2))
        stride, size = 2, size // 2
    while size > 1:
        step = 4 if size % 4 == 0 else 2
        out.append((stride, step))
        stride, size = stride * step, size // step
    return out


def axis_stages(axis):
    return stages(lax.axis_size(axis), axis == "fsdp")


def swap(val, axis, mask):
    size = lax.axis_size(axis)
    return lax.ppermute(val, axis, [(i, i ^ mask) for i in range(size)])


def place(axis, stride, size):
    return (lax.axis_index(axis) // stride) % size


def in_order(parts, pos):
    size = len(parts)
    if size == 2:
        return jnp.stack([lax.select(pos == 1, parts[1 - j], parts[j]) for j in range(2)])
    return jnp.stack([lax.select_n(pos, *[parts[j ^ p] for p in range(size)]) for j in range(size)])


def gather_open(val, axis, level):
    stride, size = list(reversed(axis_stages(axis)))[level]
    return [val] + [swap(val, axis, k * stride) for k in range(1, size)]


def gather_close(parts, axis, level):
    stride, size = list(reversed(axis_stages(axis)))[level]
    return in_order(parts, place(axis, stride, size))


def gather_shape(val, axis, shape):
    n = len(axis_stages(axis))
    order = tuple(reversed(range(n))) + tuple(range(n, n + len(shape)))
    return val.transpose(order).reshape((lax.axis_size(axis),) + shape)


def gather(val, axis):
    shape = val.shape
    for level in range(len(axis_stages(axis))):
        val = gather_close(gather_open(val, axis, level), axis, level)
    return gather_shape(val, axis, shape)


def reduce_stage(val, dim, axis, stride, size, send_type):
    pos = place(axis, stride, size)
    total = lax.dynamic_index_in_dim(val, pos, dim, keepdims=False).astype(F32)
    for k in range(1, size):
        piece = lax.dynamic_index_in_dim(val, pos ^ k, dim, keepdims=False)
        total = total + swap(piece.astype(send_type), axis, k * stride).astype(F32)
    return total


def reduce_open(val, axis, send_type):
    plan = axis_stages(axis)
    sizes = [s for _, s in reversed(plan)]
    val = val.reshape(tuple(sizes) + val.shape[1:])
    for dim in range(len(sizes) - 1, 0, -1):
        stride, size = plan[len(sizes) - 1 - dim]
        val = reduce_stage(val, dim, axis, stride, size, send_type)
    stride, size = plan[-1]
    pos = place(axis, stride, size)
    out = [lax.dynamic_index_in_dim(val, pos ^ k, 0, keepdims=False) for k in range(size)]
    return [out[0]] + [swap(out[k].astype(send_type), axis, k * stride) for k in range(1, size)]


def total_of(parts):
    return sum(p.astype(F32) for p in parts)


def reduce_parts(val, axis, send_type):
    return total_of(reduce_open(val, axis, send_type))


def after(val, *deps):
    return lax.optimization_barrier((val,) + deps)[0]


def tie(parts, *deps):
    return list(lax.optimization_barrier(tuple(parts) + deps)[: len(parts)])


def sum_all(val, axes):
    for axis in axes:
        for stride, size in axis_stages(axis):
            parts = [val] + [swap(val, axis, k * stride) for k in range(1, size)]
            while len(parts) > 1:
                parts = [parts[i] + parts[i + 1] for i in range(0, len(parts), 2)]
            val = parts[0]
    return val


def small_mesh(rows):
    return rows == 48 and lax.axis_size("dp") == CHUNKS and lax.axis_size("fsdp") == 8


def gather_z(whole):
    width = whole.shape[1] // CHUNKS
    chunk = lax.dynamic_slice_in_dim(whole, lax.axis_index("dp") * width, width, 1)
    parts = [chunk] + [swap(chunk, "fsdp", 2 * k) for k in (1, 2, 3)]
    return in_order(parts, place("fsdp", 2, 4))


def gather_dp(mine):
    return jnp.stack([mine] + [swap(mine, "dp", k) for k in (1, 2, 3)])


def gather_core(mine):
    return [mine, swap(mine, "fsdp", 1)]


def gather_whole(whole):
    return [lax.all_gather(whole, "fsdp", axis=0, tiled=True)]


def dot(a, b):
    return jnp.dot(a, b, preferred_element_type=F32)


def dot_nt(a, b):
    return lax.dot_general(a, b, (((1,), (1,)), ((), ())), preferred_element_type=F32)


def dot_tn(a, b):
    return lax.dot_general(a, b, (((0,), (0,)), ((), ())), preferred_element_type=F32)


def layer_norm(v):
    c = v - jnp.mean(v, axis=-1, keepdims=True)
    r = lax.rsqrt(jnp.mean(c * c, axis=-1, keepdims=True) + ln_eps)
    return c * r, r


def wcols(w, lo, hi):
    if len(w.shape) == 2:
        return w[:, lo:hi]
    return w[:, :, :, lo:hi].reshape(D, hi - lo)


def head_masks():
    lane = lax.broadcasted_iota(jnp.int32, (1, 2 * HDIM), 1)
    low = (lane < HDIM).astype(F32)
    return low, 1.0 - low


def each(fn, *vals):
    outs = [fn(t, *[v[t * NTOK : (t + 1) * NTOK] for v in vals]) for t in range(vals[0].shape[0] // NTOK)]
    return jnp.concatenate(outs, axis=0)


def flat(ref):
    return ref[...].reshape(ref.shape[0] * NTOK, ref.shape[-1])


def flat_cols(ref, lo, hi):
    return ref[:, :, lo:hi].reshape(ref.shape[0] * NTOK, hi - lo)


def unflat(val):
    return val.reshape(val.shape[0] // NTOK, NTOK, val.shape[-1])


QKV, OUT, UP, DOWN = (0, 3 * D), (3 * D, 4 * D), (4 * D, 4 * D + FF), (4 * D + FF, TOKW)
HALF = FF // 2


def block_forward(h, mod, w, bias, sv):
    qkv_ref, p_ref, o_ref, g_ref, gp_ref, att_ref, mlp_ref, h2_ref = sv
    y1, _ = layer_norm(h)
    n1 = each(lambda t, y: (y * (1.0 + mod(t, 1)) + mod(t, 0)).astype(BF16), y1)
    qkv_ref[...] = unflat(dot(n1, wcols(w, *QKV)).astype(BF16))
    masks = head_masks()
    for j in range(3):
        for t in range(h.shape[0] // NTOK):
            q2 = qkv_ref[t, :, 128 * j : 128 * j + 128]
            k2 = qkv_ref[t, :, D + 128 * j : D + 128 * j + 128]
            v2 = qkv_ref[t, :, 2 * D + 128 * j : 2 * D + 128 * j + 128]
            o2 = None
            for a in range(2):
                s = dot_nt(q2, k2 * (masks[a] * 0.125).astype(BF16))
                if bias is not None:
                    s = s + bias[t]
                e = jnp.exp(s - jnp.max(s, axis=-1, keepdims=True))
                p = (e * (1.0 / jnp.sum(e, axis=-1, keepdims=True))).astype(BF16)
                p_ref[t, 2 * j + a] = p
                part = dot(p, v2 * masks[a].astype(BF16))
                o2 = part if o2 is None else o2 + part
            o_ref[t, :, 128 * j : 128 * j + 128] = o2.astype(BF16)
    att = dot(flat(o_ref), wcols(w, *OUT))
    att_ref[...] = unflat(att.astype(BF16))
    h2 = each(lambda t, x, y: x + mod(t, 2) * y, h, att)
    h2_ref[...] = unflat(h2)
    y2, _ = layer_norm(h2)
    n2 = each(lambda t, y: (y * (1.0 + mod(t, 4)) + mod(t, 3)).astype(BF16), y2)
    for at in range(0, FF, HALF):
        u = dot(n2, wcols(w, UP[0] + at, UP[0] + at + HALF))
        u2 = u * u
        t = jnp.tanh(u * (GELU_C + (GELU_C * 0.044715) * u2))
        half = 0.5 * t + 0.5
        g_ref[:, :, at : at + HALF] = unflat((u * half).astype(BF16))
        gp = half + (u * (0.5 - 0.5 * t * t)) * (GELU_C + (3.0 * GELU_C * 0.044715) * u2)
        gp_ref[:, :, at : at + HALF] = unflat(gp.astype(BF16))
    mlp = dot_nt(flat(g_ref), wcols(w, *DOWN))
    mlp_ref[...] = unflat(mlp.astype(BF16))
    return each(lambda t, x, y: x + mod(t, 5) * y, h2, mlp)


def put_sums(put, i, val):
    for t in range(val.shape[0] // NTOK):
        put(t, i, jnp.sum(val[t * NTOK : (t + 1) * NTOK], axis=0, keepdims=True))


def norm_grad(dm, y, r, mod, i, put):
    put_sums(put, i, dm)
    put_sums(put, i + 1, dm * y)
    dy = each(lambda t, x: x * (1.0 + mod(t, i + 1)), dm)
    return r * (dy - jnp.mean(dy, axis=-1, keepdims=True) - y * jnp.mean(dy * y, axis=-1, keepdims=True))


def block_backward(d3, h, mod, w, sv, dw, du_ref, dqkv_ref, put):
    qkv_ref, p_ref, o_ref, g_ref, gp_ref, att_ref, mlp_ref, h2_ref = sv
    dmlp = each(lambda t, x: (x * mod(t, 5)).astype(BF16), d3)
    put_sums(put, 5, d3 * flat(mlp_ref).astype(F32))
    for at in range(0, FF, HALF):
        dg = dot(dmlp, wcols(w, DOWN[0] + at, DOWN[0] + at + HALF))
        du_ref[:, at : at + HALF] = (dg * flat_cols(gp_ref, at, at + HALF).astype(F32)).astype(BF16)
    dw[:, DOWN[0] : DOWN[1]] += dot_tn(dmlp, flat(g_ref))
    dn2 = dot_nt(du_ref[...], wcols(w, *UP))
    y2, r2 = layer_norm(flat(h2_ref))
    n2 = each(lambda t, y: (y * (1.0 + mod(t, 4)) + mod(t, 3)).astype(BF16), y2)
    dw[:, UP[0] : UP[1]] += dot_tn(n2, du_ref[...])
    d2 = d3 + norm_grad(dn2, y2, r2, mod, 3, put)
    datt = each(lambda t, x: (x * mod(t, 2)).astype(BF16), d2)
    put_sums(put, 2, d2 * flat(att_ref).astype(F32))
    do = dot_nt(datt, wcols(w, *OUT)).astype(BF16)
    dw[:, OUT[0] : OUT[1]] += dot_tn(flat(o_ref), datt)
    masks = head_masks()
    for j in range(3):
        for t in range(h.shape[0] // NTOK):
            rows = slice(t * NTOK, (t + 1) * NTOK)
            q2 = qkv_ref[t, :, 128 * j : 128 * j + 128]
            k2 = qkv_ref[t, :, D + 128 * j : D + 128 * j + 128]
            v2 = qkv_ref[t, :, 2 * D + 128 * j : 2 * D + 128 * j + 128]
            do2 = do[rows, 128 * j : 128 * j + 128]
            dq2, dk2, dv2 = 0.0, 0.0, 0.0
            for a in range(2):
                one = masks[a].astype(BF16)
                eighth = (masks[a] * 0.125).astype(BF16)
                pb = p_ref[t, 2 * j + a]
                p = pb.astype(F32)
                dp = dot_nt(do2, v2 * one)
                ds = (p * (dp - jnp.sum(p * dp, axis=-1, keepdims=True))).astype(BF16)
                dq2 += dot(ds, k2 * eighth)
                dk2 += dot_tn(ds, q2 * eighth)
                dv2 += dot_tn(pb, do2 * one)
            dqkv_ref[rows, 128 * j : 128 * j + 128] = dq2.astype(BF16)
            dqkv_ref[rows, D + 128 * j : D + 128 * j + 128] = dk2.astype(BF16)
            dqkv_ref[rows, 2 * D + 128 * j : 2 * D + 128 * j + 128] = dv2.astype(BF16)
    dn1 = dot_nt(dqkv_ref[...], wcols(w, *QKV))
    y1, r1 = layer_norm(h)
    n1 = each(lambda t, y: (y * (1.0 + mod(t, 1)) + mod(t, 0)).astype(BF16), y1)
    dw[:, QKV[0] : QKV[1]] += dot_tn(n1, dqkv_ref[...])
    return d2 + norm_grad(dn1, y1, r1, mod, 0, put)


def weight_copies(ids, pieces, w, sems, base):
    copies = []
    if len(pieces) == 1:
        for n, (lo, hi) in enumerate((QKV, OUT, UP, (DOWN[0], w.shape[1]))):
            copies.append(pltpu.make_async_copy(pieces[0].at[:, base + lo : base + hi], w.at[:, lo:hi], sems.at[n]))
        return [[c] for c in copies]
    for c in range(2):
        core = ids[2] ^ c
        for k in range(4):
            at = pl.multiple_of((ids[1] ^ k) * CW, 128)
            copies.append(pltpu.make_async_copy(pieces[c].at[k, :, :, 0:CW], w.at[:, core, :, pl.ds(at, CW)], sems.at[4 * c + k]))
        copies.append(pltpu.make_async_copy(pieces[c].at[0, :, :, CW:], w.at[:, core, :, TOKW:], sems.at[8 + c]))
    return [copies, [], [], []]


def load_weights(ids, pieces, w, sems, base=0, work=None):
    first = pl.program_id(0) == 0

    @pl.when(first)
    def _():
        copies = [c for part in weight_copies(ids, pieces, w, sems, base) for c in part]
        for copy in copies:
            copy.start()
        if work is not None:
            work()
        for copy in copies:
            copy.wait()


def mod_row(mods, base, slot):
    return lambda t, i: mods[pl.ds(slot + t, 1), base + D * i : base + D * i + D]


def row_writer(dmod, slot):
    def write(t, i, val):
        dmod[pl.ds(slot + t, 1), D * i : D * i + D] = val

    return write


def token_row(misc):
    lane = lax.broadcasted_iota(jnp.int32, (8, 128), 1)
    return dot_nt((lane == PIN).astype(BF16), misc[...])[0:1, :]


def enc_forward_kernel(n, ids, xin, pe, mods, bias, *rest):
    pieces, (misc, h0, h3), sv, (w, sems) = rest[:n], rest[n : n + 3], rest[n + 3 : n + 11], rest[n + 11 :]
    load_weights(ids, pieces, w, sems)
    step = pl.program_id(0)
    slot = step * xin.shape[0]

    @pl.when(step == 0)
    def _():
        misc[...] = wcols(w, TOKW, TOKW + 128)

    @pl.when(slot < ids[0])
    def _():
        h = each(lambda t, x: x + pe[...], dot_nt(flat(xin), misc[...]))
        h0[...] = unflat(h)
        h3[...] = unflat(block_forward(h, mod_row(mods, 0, slot), w, bias, sv))


def side_forward_kernel(n, ids, h_in, mask, pe, misc, mods, *rest):
    pieces, (hs, h3), sv, (w, sems) = rest[:n], rest[n : n + 2], rest[n + 2 : n + 10], rest[n + 10 :]
    load_weights(ids, pieces, w, sems)
    step = pl.program_id(0)
    slot = step * h_in.shape[0]

    @pl.when(slot < ids[0])
    def _():
        token = token_row(misc) + pe[...]
        h = each(lambda t, x: x * (1.0 - mask[t]) + mask[t] * token, flat(h_in))
        hs[...] = unflat(h)
        h3[...] = unflat(block_forward(h, mod_row(mods, 0, slot), w, None, sv))


def store_grads(ids, dw, outs):
    def cols(rows, j):
        return dw[rows, j * CW : (j + 1) * CW].astype(BF16)

    extra = dw.shape[1] > TOKW
    zero = jnp.zeros((D // 8, 128), BF16)
    if len(outs) == 1:
        for j in range(CHUNKS):
            outs[0][j, :, 0:CW] = cols(slice(None), j)
            if extra:
                outs[0][j, :, CW:] = dw[:, TOKW:].astype(BF16) if j == 0 else jnp.zeros((D, 128), BF16)
        return
    for side in range(2):
        for z in range(4):
            rows = pl.ds(pl.multiple_of((2 * z + (ids[2] ^ side)) * (D // 8), 16), D // 8)
            for j in range(CHUNKS):
                outs[side][j, z, :, 0:CW] = cols(rows, j)
                if extra:
                    outs[side][j, z, :, CW:] = dw[rows, TOKW:].astype(BF16) if j == 0 else zero


def dec_kernel(n, m, ids, coef, h_in, noise, misc, mods, *rest):
    pieces = rest[:n]
    d_in, dmod, dmisc, loss = rest[n : n + 4]
    dw_out = rest[n + 4 : n + 4 + m]
    w, sems, dw, du, dqkv = rest[n + 4 + m : n + 9 + m]
    sv = rest[n + 9 + m :]
    step = pl.program_id(0)
    slot = step * h_in.shape[0]

    def clear():
        dw[...] = jnp.zeros_like(dw)
        dmisc[...] = jnp.zeros_like(dmisc)
        loss[...] = jnp.zeros_like(loss)
        dmod[...] = jnp.zeros_like(dmod)

    load_weights(ids, pieces, w, sems, TOKW, clear)

    @pl.when(slot < ids[0])
    def _():
        row = mod_row(mods, 6 * D, slot)
        put = row_writer(dmod, slot)
        h = flat(h_in)
        h_dec = block_forward(h, row, w, None, sv)
        yf, rf = layer_norm(h_dec)
        nf = each(lambda t, y: (y * (1.0 + row(t, 7)) + row(t, 6)).astype(BF16), yf)
        lane = lax.broadcasted_iota(jnp.int32, (1, 128), 1)

        def head(t, out):
            ln_b, ln_pv, wmean = coef[slot + t, 0], coef[slot + t, 1], coef[slot + t, 2]
            live = (lane >= 32) & (lane < 32 + PIN) & (slot + t < ids[0])
            d = jnp.where(live, out - noise[t], 0.0)
            vf = (pltpu.roll(out, 128 - 32, 1) + 1.0) * 0.5
            vf = jnp.where(live, vf, 0.0)
            lv = vf * ln_b + (1.0 - vf) * ln_pv
            first = jnp.exp(ln_pv - lv)
            second = wmean * jnp.exp(-lv)
            inv = 0.5 / math.log(2.0)
            dd = d * d
            kl = inv * (-1.0 + lv - ln_pv + first + dd * second)
            term = jnp.where(live, dd + kl, 0.0)
            loss[...] += jnp.sum(term.reshape(NTOK // 8, 8, 128), axis=0)
            deps = d * (2.0 + (2.0 * inv) * second)
            dlog = inv * (1.0 - first - dd * second) * (0.5 * (ln_b - ln_pv))
            dlog = jnp.where(live, dlog, 0.0)
            return (deps + pltpu.roll(dlog, 32, 1)).astype(BF16)

        dout = each(head, dot(nf, misc[...]))
        dmisc[...] += dot_tn(nf, dout)
        d3 = norm_grad(dot_nt(dout, misc[...]), yf, rf, row, 6, put)
        d_in[...] = unflat(block_backward(d3, h, row, w, sv, dw, du, dqkv, put))

    @pl.when(step == pl.num_programs(0) - 1)
    def _():
        store_grads(ids, dw, dw_out)


def side_backward_kernel(n, m, ids, d_out, h_in, mask, mods, *rest):
    sv, pieces, rest = rest[:8], rest[8 : 8 + n], rest[8 + n :]
    d_enc, dmod, dtok = rest[:3]
    dw_out = rest[3 : 3 + m]
    w, sems, dw, du, dqkv = rest[3 + m :]
    step = pl.program_id(0)
    slot = step * h_in.shape[0]

    def clear():
        dw[...] = jnp.zeros_like(dw)
        dtok[...] = jnp.zeros_like(dtok)
        dmod[...] = jnp.zeros_like(dmod)

    load_weights(ids, pieces, w, sems, 0, clear)

    @pl.when(slot < ids[0])
    def _():
        dh = block_backward(flat(d_out), flat(h_in), mod_row(mods, 0, slot), w, sv, dw, du, dqkv, row_writer(dmod, slot))
        dm = each(lambda t, x: x * mask[t], dh)
        dtok[...] += jnp.sum(dm.reshape(-1, 8, D), axis=0)
        d_enc[...] = unflat(dh - dm)

    @pl.when(step == pl.num_programs(0) - 1)
    def _():
        store_grads(ids, dw, dw_out)


def enc_backward_kernel(n, m, ids, d_out, h_in, xin, mods, dmisc, dtok, *rest):
    sv, pieces, rest = rest[:8], rest[8 : 8 + n], rest[8 + n :]
    dmod = rest[0]
    dw_out = rest[1 : 1 + m]
    w, sems, dw, du, dqkv = rest[1 + m :]
    step = pl.program_id(0)
    slot = step * h_in.shape[0]

    def clear():
        dw[...] = jnp.zeros_like(dw)
        dmod[...] = jnp.zeros_like(dmod)
        lane = lax.broadcasted_iota(jnp.int32, (8, 128), 1)
        token = lax.dot_general(
            dtok[...], (lane == PIN).astype(F32), (((0,), (0,)), ((), ())), precision=lax.Precision.HIGHEST, preferred_element_type=F32
        )
        dw[:, TOKW:] = dmisc[...] + token

    load_weights(ids, pieces, w, sems, 0, clear)

    @pl.when(slot < ids[0])
    def _():
        dh = block_backward(flat(d_out), flat(h_in), mod_row(mods, 0, slot), w, sv, dw, du, dqkv, row_writer(dmod, slot))
        dw[:, TOKW:] += dot_tn(dh.astype(BF16), flat(xin))

    @pl.when(step == pl.num_programs(0) - 1)
    def _():
        store_grads(ids, dw, dw_out)


def assign_kernel(nf, slots, me, packed, features, tone, ttwo, classes, mine, info_out, c_part, c_own, a_pre_out, a_out, feat_out, hot_out, pick_out):
    lats = packed.shape[0]
    info = packed[:, NTOK * PIN + NTOK :]
    used = info[:, 0:1]
    src = lax.broadcasted_iota(jnp.int32, (lats, lats), 0)
    dst = lax.broadcasted_iota(jnp.int32, (lats, lats), 1)
    before = dot((dst < src).astype(BF16), jnp.broadcast_to(used, (lats, 128)))[:, 0:1]
    turn = jnp.floor((before + 0.5) * (1.0 / nf))
    target = (before - nf * turn) * 8.0 + turn
    live = used.astype(F32) > 0.5
    pick = jnp.where(live & (target == dst.astype(F32)), 1.0, 0.0).astype(BF16)
    moved = dot_tn(pick, info)
    step_of = moved[:, 1:2] * 32.0 + moved[:, 2:3]
    label_of = moved[:, 3:4] * 32.0 + moved[:, 4:5]
    wide = lax.broadcasted_iota(jnp.int32, (lats, 1024), 1).astype(F32)
    hot_t = jnp.where(wide == step_of, 1.0, 0.0).astype(BF16)
    hot_l = jnp.where(wide == label_of, 1.0, 0.0).astype(BF16)
    feat = dot(hot_t, features[...]).astype(BF16)
    a_pre = dot_nt(tone[...], feat)
    a_act = (a_pre * jax.nn.sigmoid(a_pre)).astype(BF16)
    c_part[...] = dot_tn(ttwo[...], a_act)
    c_own[...] = dot_nt(classes[...], hot_l)
    a_pre_out[...] = a_pre
    a_out[...] = a_act
    feat_out[...] = feat
    hot_out[...] = hot_l
    lane8 = lax.broadcasted_iota(jnp.int32, (lats, 8), 1) + me[0] * 8
    pick_me = jnp.where(live & (target == lane8.astype(F32)), 1.0, 0.0).astype(BF16)
    mine[...] = dot_tn(pick_me, packed[:, : NTOK * PIN + NTOK]).astype(BF16)
    info_out[...] = dot_tn(pick_me, info)
    pick_out[...] = pick_me


SMEM = pl.BlockSpec(memory_space=pltpu.SMEM)
ANY = pl.BlockSpec(memory_space=pl.ANY)


def slot_spec(*shape, together=1):
    def index(s, ids):
        return (jnp.minimum(s, jnp.maximum((ids[0] + together - 1) // together - 1, 0)),) + (0,) * len(shape)

    return pl.BlockSpec((together,) + shape, index)


def fixed_spec(*shape):
    return pl.BlockSpec(shape, lambda s, ids: (0,) * len(shape))


SAVES = (
    ((NTOK, 3 * D), BF16),
    ((HEADS, NTOK, NTOK), BF16),
    ((NTOK, D), BF16),
    ((NTOK, FF), BF16),
    ((NTOK, FF), BF16),
    ((NTOK, D), BF16),
    ((NTOK, D), BF16),
    ((NTOK, D), F32),
)


def weight_scratch(pieces, width):
    shape = (D, width) if len(pieces) == 1 else (4, 2, D // 8, width)
    return [pltpu.VMEM(shape, BF16), pltpu.SemaphoreType.DMA((10,))]


def grad_scratch(width, together=1):
    return [
        pltpu.VMEM((D, width), F32),
        pltpu.VMEM((together * NTOK, FF), BF16),
        pltpu.VMEM((together * NTOK, 3 * D), BF16),
    ]


def grad_outs(split, width):
    if split:
        return [fixed_out((CHUNKS, 4, D // 8, width), BF16)] * 2
    return [fixed_out((CHUNKS, D, width), BF16)]


def call(kernel, slots, ids, in_specs, args, pieces, outs, scratch, macs, together=1):
    specs = list(in_specs) + [ANY] * len(pieces)
    return pl.pallas_call(
        functools.partial(kernel, len(pieces)),
        grid_spec=pltpu.PrefetchScalarGridSpec(
            num_scalar_prefetch=1,
            grid=(slots // together,),
            in_specs=specs,
            out_specs=[o[0] for o in outs],
            scratch_shapes=scratch,
        ),
        out_shape=[jax.ShapeDtypeStruct(o[1], o[2]) for o in outs],
        compiler_params=pltpu.CompilerParams(vmem_limit_bytes=VMEM_LIMIT, dimension_semantics=("arbitrary",)),
        cost_estimate=pl.CostEstimate(flops=int(macs * slots // 2), bytes_accessed=int(4e6), transcendentals=0),
    )(ids, *args, *pieces)


def slot_out(slots, shape, kind, together=1):
    return (slot_spec(*shape, together=together), (slots,) + shape, kind)


def fixed_out(shape, kind):
    return (fixed_spec(*shape), shape, kind)


BLOCK_MACS = NTOK * (D * TOKW + 2 * NTOK * D)
MODS_E = (8, 6 * D)
MODS_R = (8, 14 * D)


def enc_forward(slots, ids, xin, pe, mods, bias, pieces):
    return call(
        enc_forward_kernel,
        slots,
        ids,
        [slot_spec(NTOK, 128), fixed_spec(NTOK, D), fixed_spec(*MODS_E), slot_spec(1, NTOK)],
        [xin, pe, mods, bias],
        pieces,
        [fixed_out((D, 128), BF16)] + [slot_out(slots, (NTOK, D), F32)] * 2 + [slot_out(slots, s, k) for s, k in SAVES],
        weight_scratch(pieces, TOKW + 128),
        BLOCK_MACS,
    )


def side_forward(slots, ids, h_in, mask, pe, misc, mods, pieces):
    return call(
        side_forward_kernel,
        slots,
        ids,
        [slot_spec(NTOK, D), slot_spec(NTOK, 1), fixed_spec(NTOK, D), fixed_spec(D, 128), fixed_spec(*MODS_R)],
        [h_in, mask, pe, misc, mods],
        pieces,
        [slot_out(slots, (NTOK, D), F32)] * 2 + [slot_out(slots, s, k) for s, k in SAVES],
        weight_scratch(pieces, TOKW),
        BLOCK_MACS,
    )


def dec_both(slots, ids, coef, h_in, noise, misc, mods, pieces, split):
    outs = grad_outs(split, CW)
    pair = 2 if slots % 2 == 0 else 1
    return call(
        lambda n, *refs: dec_kernel(n, len(outs), *refs),
        slots,
        ids,
        [SMEM, slot_spec(NTOK, D, together=pair), slot_spec(NTOK, 128, together=pair), fixed_spec(D, 128), fixed_spec(*MODS_R)],
        [coef, h_in, noise, misc, mods],
        pieces,
        [slot_out(slots, (NTOK, D), F32, pair), fixed_out((8, 8 * D), F32), fixed_out((D, 128), F32), fixed_out((8, 128), F32)] + outs,
        weight_scratch(pieces, TOKW) + grad_scratch(TOKW, pair) + [pltpu.VMEM((pair,) + s, k) for s, k in SAVES],
        3 * BLOCK_MACS,
        pair,
    )


def side_backward(slots, ids, d_out, h_in, mask, mods, saves, pieces, split):
    outs = grad_outs(split, CW)
    return call(
        lambda n, *refs: side_backward_kernel(n, len(outs), *refs),
        slots,
        ids,
        [slot_spec(NTOK, D), slot_spec(NTOK, D), slot_spec(NTOK, 1), fixed_spec(*MODS_R)] + [slot_spec(*s) for s, _ in SAVES],
        [d_out, h_in, mask, mods] + list(saves),
        pieces,
        [slot_out(slots, (NTOK, D), F32), fixed_out((8, 6 * D), F32), fixed_out((8, D), F32)] + outs,
        weight_scratch(pieces, TOKW) + grad_scratch(TOKW),
        2 * BLOCK_MACS,
    )


def enc_backward(slots, ids, d_out, h_in, xin, mods, dmisc, dtok, saves, pieces, split):
    outs = grad_outs(split, CW + 128)
    return call(
        lambda n, *refs: enc_backward_kernel(n, len(outs), *refs),
        slots,
        ids,
        [slot_spec(NTOK, D), slot_spec(NTOK, D), slot_spec(NTOK, 128), fixed_spec(*MODS_E), fixed_spec(D, 128), fixed_spec(8, D)]
        + [slot_spec(*s) for s, _ in SAVES],
        [d_out, h_in, xin, mods, dmisc, dtok] + list(saves),
        pieces,
        [fixed_out((8, 6 * D), F32)] + outs,
        weight_scratch(pieces, TOKW + 128) + grad_scratch(TOKW + 128),
        2 * BLOCK_MACS,
    )


def assign(nf, slots, me, packed, tone, ttwo, classes):
    lats, rows = packed.shape[0], tone.shape[0]
    out = [
        ((8, NTOK * PIN + NTOK), BF16),
        ((8, 128), F32),
        ((D, lats), F32),
        ((rows, lats), F32),
        ((rows, lats), F32),
        ((rows, lats), BF16),
        ((lats, FREQ), BF16),
        ((lats, 1024), BF16),
        ((lats, 8), BF16),
    ]
    vmem = pl.BlockSpec(memory_space=pltpu.VMEM)
    return pl.pallas_call(
        functools.partial(assign_kernel, nf, slots),
        in_specs=[SMEM] + [vmem] * 5,
        out_specs=[vmem] * len(out),
        out_shape=[jax.ShapeDtypeStruct(s, k) for s, k in out],
        compiler_params=pltpu.CompilerParams(vmem_limit_bytes=VMEM_LIMIT),
    )(me, packed, jnp.asarray(feature_table()), tone, ttwo, classes)


def silu_slope(val):
    s = jax.nn.sigmoid(val)
    return s * (1.0 + val * (1.0 - s))


def adam(master, first_m, second, grad_in):
    first_new = beta_one * first_m + (1.0 - beta_one) * grad_in
    second_new = beta_two * second + (1.0 - beta_two) * grad_in * grad_in
    first_hat = first_new / (1.0 - beta_one**STEP)
    second_hat = second_new / (1.0 - beta_two**STEP)
    master_new = master - learn_rate * (first_hat / (jnp.sqrt(second_hat) + adam_eps) + weight_decay * master)
    return [master_new, first_new, second_new]


def grad_core(dw, *deps):
    if len(dw) == 1:
        return dw
    keep, send = dw
    if deps:
        send = after(send, *deps)
    return [keep, swap(send, "fsdp", 1)]


def grad_dp(parts):
    if len(parts) == 1:
        return parts
    keep, got = parts
    me = lax.axis_index("dp")

    def piece(k):
        return lax.dynamic_index_in_dim(keep, me ^ k, 0, False).astype(F32) + lax.dynamic_index_in_dim(got, me ^ k, 0, False).astype(F32)

    return [piece(0).astype(BF16)] + [swap(piece(k).astype(BF16), "dp", k) for k in (1, 2, 3)]


def grad_sum(parts):
    if len(parts) == 1:
        return parts[0]
    return sum(p.astype(F32) for p in parts)


def grad_z(part):
    if part.shape[0] == CHUNKS and part.shape[1] == D:
        part = lax.psum_scatter(part, "fsdp", scatter_dimension=1, tiled=True)
        return reduce_stage(part, 0, "dp", 1, CHUNKS, BF16).astype(BF16)
    return reduce_stage(part, 0, "fsdp", 2, 4, BF16).astype(BF16)


def dp_share(val):
    rows = val.shape[0]
    return reduce_stage(val.reshape(rows, CHUNKS, -1).transpose(1, 0, 2), 0, "dp", 1, CHUNKS, BF16).astype(BF16)


def columns(parts, lo, hi):
    return jnp.concatenate([parts[j, :, lo:hi] for j in range(CHUNKS)], axis=1)


def on_device(latents, noise, timesteps, labels, patch_mask, counts, owners, tables_w, tables_m, tables_v, rows_w, rows_m, rows_v, down_w, down_m, down_v):
    nd, nf = lax.axis_size("dp"), lax.axis_size("fsdp")
    me_d, me_f = lax.axis_index("dp"), lax.axis_index("fsdp")
    rows = tables_w.shape[0]
    micro, per = latents.shape[0], latents.shape[1]
    slots = micro * per
    split = small_mesh(rows)

    steps = timesteps.reshape(slots)
    names = labels.reshape(slots)
    plan = jnp.take(jnp.asarray(plan_table()), steps, axis=0)
    used = (jnp.arange(per)[None, :] < counts).astype(jnp.int32).reshape(slots)
    x_zero, eps = latents.reshape(slots, NTOK * PIN), noise.reshape(slots, NTOK * PIN)
    x_in = (plan[:, 0:1] * x_zero + plan[:, 1:2] * eps).astype(BF16)
    words = jnp.stack([used, steps // 32, steps % 32, names // 32, names % 32], axis=1).astype(BF16)
    words = jnp.concatenate([words, jnp.zeros((slots, 3), BF16), plan[:, 8:].astype(BF16)], axis=1)
    packed = jnp.concatenate([x_in, patch_mask.reshape(slots, NTOK).astype(BF16), words], axis=1)
    packed = jnp.pad(packed, ((0, 8 - slots), (0, 0)))
    eps = jnp.pad(eps.astype(BF16), ((0, 8 - slots), (0, 0)))
    packed = gather(packed, "fsdp").reshape(nf * 8, -1)
    wholes = []

    rows_b, down_b, tables_b = rows_w.astype(BF16), down_w.astype(BF16), tables_w.astype(BF16)
    head_at = D + 3 * STRIDE + 2 * D
    gap = jnp.zeros((rows, 16), BF16)
    misc_own = jnp.concatenate(
        [tables_b[:, : PIN + 1], gap[:, :15], rows_b[:, head_at : head_at + PIN], gap, rows_b[:, head_at + PIN : head_at + 2 * PIN], gap, gap, gap],
        axis=1,
    )
    for b in range(3):
        at = D + b * STRIDE
        row_part, down_part = rows_b[:, at : at + 4 * D + FF], down_b[:, b * FF : (b + 1) * FF]
        cols = [row_part[:, :CW], row_part[:, CW : 2 * CW], row_part[:, 2 * CW :], down_part[:, :D], down_part[:, D:]]
        if b == 0 and split:
            cols = [cols[0], misc_own, cols[1], misc_own, cols[2], cols[3], misc_own, cols[4], misc_own]
        elif b == 0:
            cols = cols + [misc_own]
        whole = jnp.concatenate(cols, axis=1)
        wholes.append(whole)
    enc_z = gather_z(wholes[0]) if split else None
    late_w = gather_whole(jnp.concatenate(wholes[1:], axis=1))

    w_tone = tables_b[:, PIN + 1 : PIN + 1 + FREQ]
    class_tab = jnp.pad(tables_b[:, PIN + 1 + FREQ :], ((0, 0), (0, 1024 - CLASSES)))
    w_ttwo = rows_b[:, :D]
    ada_at = [D + b * STRIDE + 4 * D + FF for b in range(3)]
    fin_at = D + 3 * STRIDE
    w_ada = jnp.concatenate([rows_b[:, a : a + 6 * D] for a in ada_at] + [rows_b[:, fin_at : fin_at + 2 * D]], axis=1)
    me = me_f.astype(jnp.int32).reshape(1)
    mine, info, c_part, c_own, a_pre, a_act, feat, hot, pick = assign(nf, slots, me, packed, w_tone, w_ttwo, class_tab)
    cond = reduce_parts(c_part.reshape(nf, rows, nf * 8), "fsdp", F32) + c_own
    s_cond = jax.nn.silu(cond).astype(BF16)
    mods_e = reduce_parts(dot_tn(s_cond, w_ada[:, : 6 * D]).reshape(nf, 8, 6 * D), "fsdp", BF16)
    if split:
        enc_w = gather_core(after(gather_dp(after(enc_z, c_part)), s_cond))
    else:
        enc_w = gather_whole(wholes[0])
    mods_r = reduce_open(dot_tn(s_cond, w_ada[:, 6 * D :]).reshape(nf, 8, 14 * D), "fsdp", BF16)

    work = jnp.sum(info[:, 0]).astype(jnp.int32)
    ids = jnp.stack([work, me_d.astype(jnp.int32), (me_f % 2).astype(jnp.int32)])
    coef = jnp.stack([info[:, 8 + 3 * k] + info[:, 9 + 3 * k] + info[:, 10 + 3 * k] for k in range(3)], axis=1)
    size = NTOK * PIN
    x_in = jnp.pad(mine[:slots, :size].reshape(slots, NTOK, PIN), ((0, 0), (0, 0), (0, 128 - PIN)))
    masked = mine[:slots, size:].astype(F32)
    bias = (-1e9 * masked)[:, None, :]
    mask_col = masked[:, :, None]
    pe = jnp.asarray(position_table())

    last = len(axis_stages("fsdp")) - 1
    misc, h0, h_enc, *save_e = enc_forward(slots, ids, x_in, pe, mods_e, bias, enc_w)
    mods_r = total_of(tie(mods_r, misc))
    level = gather_open(after(eps, mods_r), "fsdp", 0)
    hs, h_side, *save_s = side_forward(slots, ids, h_enc, mask_col, pe, misc, mods_r, late_w)
    level = tie(level, hs)
    for at in range(last):
        level = gather_open(gather_close(level, "fsdp", at), "fsdp", at + 1)
    eps = gather_shape(gather_close(level, "fsdp", last), "fsdp", (8, size)).reshape(nf * 8, size)
    eps = dot_tn(pick, eps)[:slots].reshape(slots, NTOK, PIN)
    eps = jnp.pad(eps, ((0, 0), (0, 0), (32, 96 - PIN)))

    d_side, dmod_d, dmisc, loss, *dw_d = dec_both(slots, ids, coef, h_side, eps, misc, mods_r, late_w, False)
    mine_d = lax.psum_scatter(dw_d[0], "fsdp", scatter_dimension=1, tiled=True)
    d_enc, dmod_s, dtok, *dw_s = side_backward(slots, ids, d_side, hs, mask_col, mods_r, save_s, late_w, split)
    part_s = grad_dp(grad_core(dw_s))
    d_enc = after(d_enc, part_s[0])
    dmod_e, *dw_e = enc_backward(slots, ids, d_enc, h0, x_in, mods_e, dmisc, dtok, save_e, enc_w, split)
    total_s = grad_sum(tie(part_s, dmod_e, mine_d))
    dmods = jnp.concatenate([dmod_e, dmod_s, dmod_d], axis=1).astype(BF16)
    level = gather_open(after(dmods, total_s), "fsdp", 0)
    core_e = grad_core(dw_e, total_s)
    part_e = grad_dp(core_e)

    level = tie(level, part_e[0])
    for at in range(last):
        level = gather_open(gather_close(level, "fsdp", at), "fsdp", at + 1)
    dm_all = gather_shape(gather_close(level, "fsdp", last), "fsdp", dmods.shape).reshape(nf * 8, -1)
    d_cond = dot_nt(w_ada, dm_all) * silu_slope(cond)
    d_cond_all = gather(d_cond.astype(BF16), "fsdp").reshape(D, nf * 8)
    d_apre = (dot(w_ttwo, d_cond_all) * silu_slope(a_pre)).astype(BF16)
    g_class = jnp.dot(d_cond, hot.astype(F32), precision=lax.Precision.HIGHEST, preferred_element_type=F32)
    kinds = [dot(s_cond, dm_all), dot_nt(a_act, d_cond_all), dot(d_apre, feat), g_class, jnp.zeros((rows, 128), F32)]
    kinds = jnp.concatenate([k.astype(BF16) for k in kinds], axis=1).reshape(rows, CHUNKS, -1).transpose(1, 0, 2)

    g_side = grad_z(after(total_s, d_cond)) if split else grad_z(total_s)
    total_e = grad_sum(tie(part_e, d_cond_all))
    g_enc = grad_z(total_e)
    others = after(jnp.concatenate([mine_d, kinds], axis=2), total_e)
    g_other = total_of(reduce_open(others, "dp", BF16)).astype(BF16)
    parts = jnp.concatenate([g_enc, g_side, g_other], axis=1)
    squares = jnp.sum(jnp.square(parts.astype(F32)))
    norm_sq, loss_sum, count = sum_all(jnp.stack([squares, jnp.sum(loss), jnp.sum(used).astype(F32)]), ("fsdp", "dp"))
    full = gather(parts, "dp")
    scale = 1.0 / (count * (NTOK * PIN))
    loss_out = loss_sum * scale
    grad_norm = jnp.sqrt(norm_sq) * scale
    factor = scale * jnp.minimum(1.0, clip_level / (grad_norm + 1e-06))

    up = 4 * D + FF
    wide_e = CW + 128
    f_enc, small = columns(full, 0, CW), full[0, :, CW:wide_e]
    f_side, f_dec = columns(full, wide_e, wide_e + CW), columns(full, wide_e + CW, wide_e + 2 * CW)
    f_rest = columns(full, wide_e + 2 * CW, full.shape[2])
    at = 20 * D
    ttwo, tone, klass = f_rest[:, at : at + D], f_rest[:, at + D : at + D + FREQ], f_rest[:, at + D + FREQ : at + D + FREQ + CLASSES]
    rows_g = [ttwo, f_enc[:, :up], f_rest[:, : 6 * D], f_side[:, :up], f_rest[:, 6 * D : 12 * D], f_dec[:, :up], f_rest[:, 12 * D : 20 * D]]
    rows_g = jnp.concatenate(rows_g + [small[:, 32 : 32 + PIN], small[:, 64 : 64 + PIN]], axis=1)
    down_g = jnp.concatenate([blk[:, up:] for blk in (f_enc, f_side, f_dec)], axis=1)
    tables_g = jnp.concatenate([small[:, : PIN + 1], tone, klass], axis=1)
    results = adam(tables_w, tables_m, tables_v, factor * tables_g.astype(F32))

    def own(val):
        size = val.shape[1] // nd
        return lax.dynamic_slice_in_dim(val, me_d * size, size, 1)

    results += adam(own(rows_w), own(rows_m), own(rows_v), factor * own(rows_g).astype(F32))
    results += adam(own(down_w), own(down_m), own(down_v), factor * own(down_g).astype(F32))
    return tuple([loss_out, grad_norm] + results)


def solution(mesh):
    lat = P(None, ("dp", "fsdp"), None)
    num = P(None, ("dp", "fsdp"))
    row = P("fsdp", None)
    both = P("fsdp", "dp")
    return jax.shard_map(
        on_device,
        mesh=mesh,
        in_specs=(lat, lat, num, num, lat, num, P()) + (row,) * 9,
        out_specs=(P(), P()) + (row,) * 3 + (both,) * 6,
        check_vma=False,
    )
```

```python
import functools
import math

import jax
import jax.numpy as jnp
import numpy as np
from jax import lax
from jax.experimental import pallas as pl
from jax.experimental.pallas import tpu as pltpu
from jax.sharding import PartitionSpec as P

D = 384
HEADS = 6
HDIM = 64
FF = 1536
NTOK = 256
PIN = 16
FREQ = 256
CLASSES = 1000
TSTEPS = 1000
STEP = 10
POUT = 32

beta_one = 0.9
beta_two = 0.999
adam_eps = 1e-08
learn_rate = 0.05
weight_decay = 0.1
clip_level = 0.005
ln_eps = 1e-06

F32 = jnp.float32
BF16 = jnp.bfloat16
STRIDE = 10 * D + FF
TOKW = 3 * D + D + FF + FF
CHUNKS = 4
CW = TOKW // CHUNKS
GELU_C = math.sqrt(2.0 / math.pi)
VMEM_LIMIT = 60 * 1024 * 1024


def plan_table():
    j = np.arange(TSTEPS, dtype=np.float64)
    beta = 0.0001 + (0.02 - 0.0001) * j / (TSTEPS - 1)
    abar = np.cumprod(1.0 - beta)
    prev = np.concatenate([[1.0], abar[:-1]])
    out = np.zeros((TSTEPS, 5), np.float64)
    out[:, 0] = np.sqrt(abar)
    out[:, 1] = np.sqrt(1.0 - abar)
    out[1:, 2] = np.log(beta[1:])
    out[1:, 3] = np.log(beta[1:] * (1.0 - prev[1:]) / (1.0 - abar[1:]))
    out[1:, 4] = prev[1:] * beta[1:] ** 2 / ((1.0 - abar[1:]) * abar[1:])
    full = np.zeros((TSTEPS, 128), np.float32)
    full[:, 0:2] = out[:, 0:2]
    for k in range(3):
        left = out[:, 2 + k].astype(np.float32)
        for part in range(3):
            full[:, 8 + 3 * k + part] = bf16_of(left)
            left = left - full[:, 8 + 3 * k + part]
    return full


def bf16_of(val):
    return val.astype(jnp.bfloat16).astype(np.float32)


def feature_table():
    half = FREQ // 2
    rates = np.exp(-math.log(10000.0) * np.arange(half) / half)
    angles = np.arange(1024)[:, None] * rates[None, :]
    return np.concatenate([np.cos(angles), np.sin(angles)], axis=1).astype(jnp.bfloat16)


def position_table():
    half = D // 2
    rates = np.exp(-math.log(10000.0) * 2.0 * np.arange(half) / D)
    angles = np.arange(NTOK)[:, None] * rates[None, :]
    return np.concatenate([np.sin(angles), np.cos(angles)], axis=1).astype(np.float32)


def stages(size, pair_first):
    out, stride = [], 1
    if pair_first and size % 2 == 0:
        out.append((1, 2))
        stride, size = 2, size // 2
    while size > 1:
        step = 4 if size % 4 == 0 else 2
        out.append((stride, step))
        stride, size = stride * step, size // step
    return out


def axis_stages(axis):
    return stages(lax.axis_size(axis), axis == "fsdp")


def swap(val, axis, mask):
    size = lax.axis_size(axis)
    return lax.ppermute(val, axis, [(i, i ^ mask) for i in range(size)])


def place(axis, stride, size):
    return (lax.axis_index(axis) // stride) % size


def in_order(parts, pos):
    size = len(parts)
    if size == 2:
        return jnp.stack([lax.select(pos == 1, parts[1 - j], parts[j]) for j in range(2)])
    return jnp.stack([lax.select_n(pos, *[parts[j ^ p] for p in range(size)]) for j in range(size)])


def gather_open(val, axis, level):
    stride, size = list(reversed(axis_stages(axis)))[level]
    return [val] + [swap(val, axis, k * stride) for k in range(1, size)]


def gather_close(parts, axis, level):
    stride, size = list(reversed(axis_stages(axis)))[level]
    return in_order(parts, place(axis, stride, size))


def gather_shape(val, axis, shape):
    n = len(axis_stages(axis))
    order = tuple(reversed(range(n))) + tuple(range(n, n + len(shape)))
    return val.transpose(order).reshape((lax.axis_size(axis),) + shape)


def gather(val, axis):
    shape = val.shape
    for level in range(len(axis_stages(axis))):
        val = gather_close(gather_open(val, axis, level), axis, level)
    return gather_shape(val, axis, shape)


def reduce_stage(val, dim, axis, stride, size, send_type):
    pos = place(axis, stride, size)
    total = lax.dynamic_index_in_dim(val, pos, dim, keepdims=False).astype(F32)
    for k in range(1, size):
        piece = lax.dynamic_index_in_dim(val, pos ^ k, dim, keepdims=False)
        total = total + swap(piece.astype(send_type), axis, k * stride).astype(F32)
    return total


def reduce_open(val, axis, send_type):
    plan = axis_stages(axis)
    sizes = [s for _, s in reversed(plan)]
    val = val.reshape(tuple(sizes) + val.shape[1:])
    for dim in range(len(sizes) - 1, 0, -1):
        stride, size = plan[len(sizes) - 1 - dim]
        val = reduce_stage(val, dim, axis, stride, size, send_type)
    stride, size = plan[-1]
    pos = place(axis, stride, size)
    out = [lax.dynamic_index_in_dim(val, pos ^ k, 0, keepdims=False) for k in range(size)]
    return [out[0]] + [swap(out[k].astype(send_type), axis, k * stride) for k in range(1, size)]


def total_of(parts):
    return sum(p.astype(F32) for p in parts)


def reduce_parts(val, axis, send_type):
    return total_of(reduce_open(val, axis, send_type))


def after(val, *deps):
    return lax.optimization_barrier((val,) + deps)[0]


def tie(parts, *deps):
    return list(lax.optimization_barrier(tuple(parts) + deps)[: len(parts)])


def sum_all(val, axes):
    for axis in axes:
        for stride, size in axis_stages(axis):
            parts = [val] + [swap(val, axis, k * stride) for k in range(1, size)]
            while len(parts) > 1:
                parts = [parts[i] + parts[i + 1] for i in range(0, len(parts), 2)]
            val = parts[0]
    return val


def small_mesh(rows):
    return rows == 48 and lax.axis_size("dp") == CHUNKS and lax.axis_size("fsdp") == 8


def gather_z(whole):
    width = whole.shape[1] // CHUNKS
    chunk = lax.dynamic_slice_in_dim(whole, lax.axis_index("dp") * width, width, 1)
    parts = [chunk] + [swap(chunk, "fsdp", 2 * k) for k in (1, 2, 3)]
    return in_order(parts, place("fsdp", 2, 4))


def gather_dp(mine):
    return jnp.stack([mine] + [swap(mine, "dp", k) for k in (1, 2, 3)])


def gather_core(mine):
    return [mine, swap(mine, "fsdp", 1)]


def gather_whole(whole):
    return [lax.all_gather(whole, "fsdp", axis=0, tiled=True)]


def dot(a, b):
    return jnp.dot(a, b, preferred_element_type=F32)


def dot_nt(a, b):
    return lax.dot_general(a, b, (((1,), (1,)), ((), ())), preferred_element_type=F32)


def dot_tn(a, b):
    return lax.dot_general(a, b, (((0,), (0,)), ((), ())), preferred_element_type=F32)


def layer_norm(v):
    c = v - jnp.mean(v, axis=-1, keepdims=True)
    r = lax.rsqrt(jnp.mean(c * c, axis=-1, keepdims=True) + ln_eps)
    return c * r, r


def wcols(w, lo, hi):
    if len(w.shape) == 2:
        return w[:, lo:hi]
    return w[:, :, :, lo:hi].reshape(D, hi - lo)


def head_masks():
    lane = lax.broadcasted_iota(jnp.int32, (1, 2 * HDIM), 1)
    low = (lane < HDIM).astype(F32)
    return low, 1.0 - low


def each(fn, *vals):
    outs = [fn(t, *[v[t * NTOK : (t + 1) * NTOK] for v in vals]) for t in range(vals[0].shape[0] // NTOK)]
    return jnp.concatenate(outs, axis=0)


def flat(ref):
    return ref[...].reshape(ref.shape[0] * NTOK, ref.shape[-1])


def flat_cols(ref, lo, hi):
    return ref[:, :, lo:hi].reshape(ref.shape[0] * NTOK, hi - lo)


def unflat(val):
    return val.reshape(val.shape[0] // NTOK, NTOK, val.shape[-1])


QKV, OUT, UP, DOWN = (0, 3 * D), (3 * D, 4 * D), (4 * D, 4 * D + FF), (4 * D + FF, TOKW)
HALF = FF // 2


def block_forward(h, mod, w, bias, sv):
    qkv_ref, p_ref, o_ref, g_ref, gp_ref, att_ref, mlp_ref, h2_ref = sv
    y1, _ = layer_norm(h)
    n1 = each(lambda t, y: (y * (1.0 + mod(t, 1)) + mod(t, 0)).astype(BF16), y1)
    qkv_ref[...] = unflat(dot(n1, wcols(w, *QKV)).astype(BF16))
    masks = head_masks()
    for j in range(3):
        for t in range(h.shape[0] // NTOK):
            q2 = qkv_ref[t, :, 128 * j : 128 * j + 128]
            k2 = qkv_ref[t, :, D + 128 * j : D + 128 * j + 128]
            v2 = qkv_ref[t, :, 2 * D + 128 * j : 2 * D + 128 * j + 128]
            o2 = None
            for a in range(2):
                s = dot_nt(q2, k2 * (masks[a] * 0.125).astype(BF16))
                if bias is not None:
                    s = s + bias[t]
                e = jnp.exp(s - jnp.max(s, axis=-1, keepdims=True))
                p = (e * (1.0 / jnp.sum(e, axis=-1, keepdims=True))).astype(BF16)
                p_ref[t, 2 * j + a] = p
                part = dot(p, v2 * masks[a].astype(BF16))
                o2 = part if o2 is None else o2 + part
            o_ref[t, :, 128 * j : 128 * j + 128] = o2.astype(BF16)
    att = dot(flat(o_ref), wcols(w, *OUT))
    att_ref[...] = unflat(att.astype(BF16))
    h2 = each(lambda t, x, y: x + mod(t, 2) * y, h, att)
    h2_ref[...] = unflat(h2)
    y2, _ = layer_norm(h2)
    n2 = each(lambda t, y: (y * (1.0 + mod(t, 4)) + mod(t, 3)).astype(BF16), y2)
    for at in range(0, FF, HALF):
        u = dot(n2, wcols(w, UP[0] + at, UP[0] + at + HALF))
        u2 = u * u
        t = jnp.tanh(u * (GELU_C + (GELU_C * 0.044715) * u2))
        half = 0.5 * t + 0.5
        g_ref[:, :, at : at + HALF] = unflat((u * half).astype(BF16))
        gp = half + (u * (0.5 - 0.5 * t * t)) * (GELU_C + (3.0 * GELU_C * 0.044715) * u2)
        gp_ref[:, :, at : at + HALF] = unflat(gp.astype(BF16))
    mlp = dot_nt(flat(g_ref), wcols(w, *DOWN))
    mlp_ref[...] = unflat(mlp.astype(BF16))
    return each(lambda t, x, y: x + mod(t, 5) * y, h2, mlp)


def put_sums(put, i, val):
    for t in range(val.shape[0] // NTOK):
        put(t, i, jnp.sum(val[t * NTOK : (t + 1) * NTOK], axis=0, keepdims=True))


def norm_grad(dm, y, r, mod, i, put):
    put_sums(put, i, dm)
    put_sums(put, i + 1, dm * y)
    dy = each(lambda t, x: x * (1.0 + mod(t, i + 1)), dm)
    return r * (dy - jnp.mean(dy, axis=-1, keepdims=True) - y * jnp.mean(dy * y, axis=-1, keepdims=True))


def block_backward(d3, h, mod, w, sv, dw, du_ref, dqkv_ref, put):
    qkv_ref, p_ref, o_ref, g_ref, gp_ref, att_ref, mlp_ref, h2_ref = sv
    dmlp = each(lambda t, x: (x * mod(t, 5)).astype(BF16), d3)
    put_sums(put, 5, d3 * flat(mlp_ref).astype(F32))
    for at in range(0, FF, HALF):
        dg = dot(dmlp, wcols(w, DOWN[0] + at, DOWN[0] + at + HALF))
        du_ref[:, at : at + HALF] = (dg * flat_cols(gp_ref, at, at + HALF).astype(F32)).astype(BF16)
    dw[:, DOWN[0] : DOWN[1]] += dot_tn(dmlp, flat(g_ref))
    dn2 = dot_nt(du_ref[...], wcols(w, *UP))
    y2, r2 = layer_norm(flat(h2_ref))
    n2 = each(lambda t, y: (y * (1.0 + mod(t, 4)) + mod(t, 3)).astype(BF16), y2)
    dw[:, UP[0] : UP[1]] += dot_tn(n2, du_ref[...])
    d2 = d3 + norm_grad(dn2, y2, r2, mod, 3, put)
    datt = each(lambda t, x: (x * mod(t, 2)).astype(BF16), d2)
    put_sums(put, 2, d2 * flat(att_ref).astype(F32))
    do = dot_nt(datt, wcols(w, *OUT)).astype(BF16)
    dw[:, OUT[0] : OUT[1]] += dot_tn(flat(o_ref), datt)
    masks = head_masks()
    for j in range(3):
        for t in range(h.shape[0] // NTOK):
            rows = slice(t * NTOK, (t + 1) * NTOK)
            q2 = qkv_ref[t, :, 128 * j : 128 * j + 128]
            k2 = qkv_ref[t, :, D + 128 * j : D + 128 * j + 128]
            v2 = qkv_ref[t, :, 2 * D + 128 * j : 2 * D + 128 * j + 128]
            do2 = do[rows, 128 * j : 128 * j + 128]
            dq2, dk2, dv2 = 0.0, 0.0, 0.0
            for a in range(2):
                one = masks[a].astype(BF16)
                eighth = (masks[a] * 0.125).astype(BF16)
                pb = p_ref[t, 2 * j + a]
                p = pb.astype(F32)
                dp = dot_nt(do2, v2 * one)
                ds = (p * (dp - jnp.sum(p * dp, axis=-1, keepdims=True))).astype(BF16)
                dq2 += dot(ds, k2 * eighth)
                dk2 += dot_tn(ds, q2 * eighth)
                dv2 += dot_tn(pb, do2 * one)
            dqkv_ref[rows, 128 * j : 128 * j + 128] = dq2.astype(BF16)
            dqkv_ref[rows, D + 128 * j : D + 128 * j + 128] = dk2.astype(BF16)
            dqkv_ref[rows, 2 * D + 128 * j : 2 * D + 128 * j + 128] = dv2.astype(BF16)
    dn1 = dot_nt(dqkv_ref[...], wcols(w, *QKV))
    y1, r1 = layer_norm(h)
    n1 = each(lambda t, y: (y * (1.0 + mod(t, 1)) + mod(t, 0)).astype(BF16), y1)
    dw[:, QKV[0] : QKV[1]] += dot_tn(n1, dqkv_ref[...])
    return d2 + norm_grad(dn1, y1, r1, mod, 0, put)


def weight_copies(ids, pieces, w, sems, base):
    copies = []
    if len(pieces) == 1:
        for n, (lo, hi) in enumerate((QKV, OUT, UP, (DOWN[0], w.shape[1]))):
            copies.append(pltpu.make_async_copy(pieces[0].at[:, base + lo : base + hi], w.at[:, lo:hi], sems.at[n]))
        return [[c] for c in copies]
    for c in range(2):
        core = ids[2] ^ c
        for k in range(4):
            at = pl.multiple_of((ids[1] ^ k) * CW, 128)
            copies.append(pltpu.make_async_copy(pieces[c].at[k, :, :, 0:CW], w.at[:, core, :, pl.ds(at, CW)], sems.at[4 * c + k]))
        copies.append(pltpu.make_async_copy(pieces[c].at[0, :, :, CW:], w.at[:, core, :, TOKW:], sems.at[8 + c]))
    return [copies, [], [], []]


def load_weights(ids, pieces, w, sems, base=0, work=None):
    first = pl.program_id(0) == 0

    @pl.when(first)
    def _():
        copies = [c for part in weight_copies(ids, pieces, w, sems, base) for c in part]
        for copy in copies:
            copy.start()
        if work is not None:
            work()
        for copy in copies:
            copy.wait()


def mod_row(mods, base, slot):
    return lambda t, i: mods[pl.ds(slot + t, 1), base + D * i : base + D * i + D]


def row_writer(dmod, slot):
    def write(t, i, val):
        dmod[pl.ds(slot + t, 1), D * i : D * i + D] = val

    return write


def token_row(misc):
    lane = lax.broadcasted_iota(jnp.int32, (8, 128), 1)
    return dot_nt((lane == PIN).astype(BF16), misc[...])[0:1, :]


def enc_forward_kernel(n, ids, xin, pe, mods, bias, *rest):
    pieces, (misc, h0, h3), sv, (w, sems) = rest[:n], rest[n : n + 3], rest[n + 3 : n + 11], rest[n + 11 :]
    load_weights(ids, pieces, w, sems)
    step = pl.program_id(0)
    slot = step * xin.shape[0]

    @pl.when(step == 0)
    def _():
        misc[...] = wcols(w, TOKW, TOKW + 128)

    @pl.when(slot < ids[0])
    def _():
        h = each(lambda t, x: x + pe[...], dot_nt(flat(xin), misc[...]))
        h0[...] = unflat(h)
        h3[...] = unflat(block_forward(h, mod_row(mods, 0, slot), w, bias, sv))


def side_forward_kernel(n, ids, h_in, mask, pe, misc, mods, *rest):
    pieces, (hs, h3), sv, (w, sems) = rest[:n], rest[n : n + 2], rest[n + 2 : n + 10], rest[n + 10 :]
    load_weights(ids, pieces, w, sems)
    step = pl.program_id(0)
    slot = step * h_in.shape[0]

    @pl.when(slot < ids[0])
    def _():
        token = token_row(misc) + pe[...]
        h = each(lambda t, x: x * (1.0 - mask[t]) + mask[t] * token, flat(h_in))
        hs[...] = unflat(h)
        h3[...] = unflat(block_forward(h, mod_row(mods, 0, slot), w, None, sv))


def store_grads(ids, dw, outs):
    def cols(rows, j):
        return dw[rows, j * CW : (j + 1) * CW].astype(BF16)

    extra = dw.shape[1] > TOKW
    zero = jnp.zeros((D // 8, 128), BF16)
    if len(outs) == 1:
        for j in range(CHUNKS):
            outs[0][j, :, 0:CW] = cols(slice(None), j)
            if extra:
                outs[0][j, :, CW:] = dw[:, TOKW:].astype(BF16) if j == 0 else jnp.zeros((D, 128), BF16)
        return
    for side in range(2):
        for z in range(4):
            rows = pl.ds(pl.multiple_of((2 * z + (ids[2] ^ side)) * (D // 8), 16), D // 8)
            for j in range(CHUNKS):
                outs[side][j, z, :, 0:CW] = cols(rows, j)
                if extra:
                    outs[side][j, z, :, CW:] = dw[rows, TOKW:].astype(BF16) if j == 0 else zero


def dec_kernel(n, m, ids, coef, h_in, noise, misc, mods, *rest):
    pieces = rest[:n]
    d_in, dmod, dmisc, loss = rest[n : n + 4]
    dw_out = rest[n + 4 : n + 4 + m]
    w, sems, dw, du, dqkv = rest[n + 4 + m : n + 9 + m]
    sv = rest[n + 9 + m :]
    step = pl.program_id(0)
    slot = step * h_in.shape[0]

    def clear():
        dw[...] = jnp.zeros_like(dw)
        dmisc[...] = jnp.zeros_like(dmisc)
        loss[...] = jnp.zeros_like(loss)
        dmod[...] = jnp.zeros_like(dmod)

    load_weights(ids, pieces, w, sems, TOKW, clear)

    @pl.when(slot < ids[0])
    def _():
        row = mod_row(mods, 6 * D, slot)
        put = row_writer(dmod, slot)
        h = flat(h_in)
        h_dec = block_forward(h, row, w, None, sv)
        yf, rf = layer_norm(h_dec)
        nf = each(lambda t, y: (y * (1.0 + row(t, 7)) + row(t, 6)).astype(BF16), yf)
        lane = lax.broadcasted_iota(jnp.int32, (1, 128), 1)

        def head(t, out):
            ln_b, ln_pv, wmean = coef[slot + t, 0], coef[slot + t, 1], coef[slot + t, 2]
            live = (lane >= 32) & (lane < 32 + PIN) & (slot + t < ids[0])
            d = jnp.where(live, out - noise[t], 0.0)
            vf = (pltpu.roll(out, 128 - 32, 1) + 1.0) * 0.5
            vf = jnp.where(live, vf, 0.0)
            lv = vf * ln_b + (1.0 - vf) * ln_pv
            first = jnp.exp(ln_pv - lv)
            second = wmean * jnp.exp(-lv)
            inv = 0.5 / math.log(2.0)
            dd = d * d
            kl = inv * (-1.0 + lv - ln_pv + first + dd * second)
            term = jnp.where(live, dd + kl, 0.0)
            loss[...] += jnp.sum(term.reshape(NTOK // 8, 8, 128), axis=0)
            deps = d * (2.0 + (2.0 * inv) * second)
            dlog = inv * (1.0 - first - dd * second) * (0.5 * (ln_b - ln_pv))
            dlog = jnp.where(live, dlog, 0.0)
            return (deps + pltpu.roll(dlog, 32, 1)).astype(BF16)

        dout = each(head, dot(nf, misc[...]))
        dmisc[...] += dot_tn(nf, dout)
        d3 = norm_grad(dot_nt(dout, misc[...]), yf, rf, row, 6, put)
        d_in[...] = unflat(block_backward(d3, h, row, w, sv, dw, du, dqkv, put))

    @pl.when(step == pl.num_programs(0) - 1)
    def _():
        store_grads(ids, dw, dw_out)


def side_backward_kernel(n, m, ids, d_out, h_in, mask, mods, *rest):
    sv, pieces, rest = rest[:8], rest[8 : 8 + n], rest[8 + n :]
    d_enc, dmod, dtok = rest[:3]
    dw_out = rest[3 : 3 + m]
    w, sems, dw, du, dqkv = rest[3 + m :]
    step = pl.program_id(0)
    slot = step * h_in.shape[0]

    def clear():
        dw[...] = jnp.zeros_like(dw)
        dtok[...] = jnp.zeros_like(dtok)
        dmod[...] = jnp.zeros_like(dmod)

    load_weights(ids, pieces, w, sems, 0, clear)

    @pl.when(slot < ids[0])
    def _():
        dh = block_backward(flat(d_out), flat(h_in), mod_row(mods, 0, slot), w, sv, dw, du, dqkv, row_writer(dmod, slot))
        dm = each(lambda t, x: x * mask[t], dh)
        dtok[...] += jnp.sum(dm.reshape(-1, 8, D), axis=0)
        d_enc[...] = unflat(dh - dm)

    @pl.when(step == pl.num_programs(0) - 1)
    def _():
        store_grads(ids, dw, dw_out)


def enc_backward_kernel(n, m, ids, d_out, h_in, xin, mods, dmisc, dtok, *rest):
    sv, pieces, rest = rest[:8], rest[8 : 8 + n], rest[8 + n :]
    dmod = rest[0]
    dw_out = rest[1 : 1 + m]
    w, sems, dw, du, dqkv = rest[1 + m :]
    step = pl.program_id(0)
    slot = step * h_in.shape[0]

    def clear():
        dw[...] = jnp.zeros_like(dw)
        dmod[...] = jnp.zeros_like(dmod)
        lane = lax.broadcasted_iota(jnp.int32, (8, 128), 1)
        token = lax.dot_general(
            dtok[...], (lane == PIN).astype(F32), (((0,), (0,)), ((), ())), precision=lax.Precision.HIGHEST, preferred_element_type=F32
        )
        dw[:, TOKW:] = dmisc[...] + token

    load_weights(ids, pieces, w, sems, 0, clear)

    @pl.when(slot < ids[0])
    def _():
        dh = block_backward(flat(d_out), flat(h_in), mod_row(mods, 0, slot), w, sv, dw, du, dqkv, row_writer(dmod, slot))
        dw[:, TOKW:] += dot_tn(dh.astype(BF16), flat(xin))

    @pl.when(step == pl.num_programs(0) - 1)
    def _():
        store_grads(ids, dw, dw_out)


def assign_kernel(nf, slots, me, packed, features, tone, ttwo, classes, mine, info_out, c_part, c_own, a_pre_out, a_out, feat_out, hot_out, pick_out):
    lats = packed.shape[0]
    info = packed[:, NTOK * PIN + NTOK :]
    used = info[:, 0:1]
    src = lax.broadcasted_iota(jnp.int32, (lats, lats), 0)
    dst = lax.broadcasted_iota(jnp.int32, (lats, lats), 1)
    before = dot((dst < src).astype(BF16), jnp.broadcast_to(used, (lats, 128)))[:, 0:1]
    turn = jnp.floor((before + 0.5) * (1.0 / nf))
    target = (before - nf * turn) * 8.0 + turn
    live = used.astype(F32) > 0.5
    pick = jnp.where(live & (target == dst.astype(F32)), 1.0, 0.0).astype(BF16)
    moved = dot_tn(pick, info)
    step_of = moved[:, 1:2] * 32.0 + moved[:, 2:3]
    label_of = moved[:, 3:4] * 32.0 + moved[:, 4:5]
    wide = lax.broadcasted_iota(jnp.int32, (lats, 1024), 1).astype(F32)
    hot_t = jnp.where(wide == step_of, 1.0, 0.0).astype(BF16)
    hot_l = jnp.where(wide == label_of, 1.0, 0.0).astype(BF16)
    feat = dot(hot_t, features[...]).astype(BF16)
    a_pre = dot_nt(tone[...], feat)
    a_act = (a_pre * jax.nn.sigmoid(a_pre)).astype(BF16)
    c_part[...] = dot_tn(ttwo[...], a_act)
    c_own[...] = dot_nt(classes[...], hot_l)
    a_pre_out[...] = a_pre
    a_out[...] = a_act
    feat_out[...] = feat
    hot_out[...] = hot_l
    lane8 = lax.broadcasted_iota(jnp.int32, (lats, 8), 1) + me[0] * 8
    pick_me = jnp.where(live & (target == lane8.astype(F32)), 1.0, 0.0).astype(BF16)
    mine[...] = dot_tn(pick_me, packed[:, : NTOK * PIN + NTOK]).astype(BF16)
    info_out[...] = dot_tn(pick_me, info)
    pick_out[...] = pick_me


SMEM = pl.BlockSpec(memory_space=pltpu.SMEM)
ANY = pl.BlockSpec(memory_space=pl.ANY)


def slot_spec(*shape, together=1):
    def index(s, ids):
        return (jnp.minimum(s, jnp.maximum((ids[0] + together - 1) // together - 1, 0)),) + (0,) * len(shape)

    return pl.BlockSpec((together,) + shape, index)


def fixed_spec(*shape):
    return pl.BlockSpec(shape, lambda s, ids: (0,) * len(shape))


SAVES = (
    ((NTOK, 3 * D), BF16),
    ((HEADS, NTOK, NTOK), BF16),
    ((NTOK, D), BF16),
    ((NTOK, FF), BF16),
    ((NTOK, FF), BF16),
    ((NTOK, D), BF16),
    ((NTOK, D), BF16),
    ((NTOK, D), F32),
)


def weight_scratch(pieces, width):
    shape = (D, width) if len(pieces) == 1 else (4, 2, D // 8, width)
    return [pltpu.VMEM(shape, BF16), pltpu.SemaphoreType.DMA((10,))]


def grad_scratch(width, together=1):
    return [
        pltpu.VMEM((D, width), F32),
        pltpu.VMEM((together * NTOK, FF), BF16),
        pltpu.VMEM((together * NTOK, 3 * D), BF16),
    ]


def grad_outs(split, width):
    if split:
        return [fixed_out((CHUNKS, 4, D // 8, width), BF16)] * 2
    return [fixed_out((CHUNKS, D, width), BF16)]


def call(kernel, slots, ids, in_specs, args, pieces, outs, scratch, macs, together=1):
    specs = list(in_specs) + [ANY] * len(pieces)
    return pl.pallas_call(
        functools.partial(kernel, len(pieces)),
        grid_spec=pltpu.PrefetchScalarGridSpec(
            num_scalar_prefetch=1,
            grid=(slots // together,),
            in_specs=specs,
            out_specs=[o[0] for o in outs],
            scratch_shapes=scratch,
        ),
        out_shape=[jax.ShapeDtypeStruct(o[1], o[2]) for o in outs],
        compiler_params=pltpu.CompilerParams(vmem_limit_bytes=VMEM_LIMIT, dimension_semantics=("arbitrary",)),
        cost_estimate=pl.CostEstimate(flops=int(macs * slots // 2), bytes_accessed=int(4e6), transcendentals=0),
    )(ids, *args, *pieces)


def slot_out(slots, shape, kind, together=1):
    return (slot_spec(*shape, together=together), (slots,) + shape, kind)


def fixed_out(shape, kind):
    return (fixed_spec(*shape), shape, kind)


BLOCK_MACS = NTOK * (D * TOKW + 2 * NTOK * D)
MODS_E = (8, 6 * D)
MODS_R = (8, 14 * D)


def enc_forward(slots, ids, xin, pe, mods, bias, pieces):
    return call(
        enc_forward_kernel,
        slots,
        ids,
        [slot_spec(NTOK, 128), fixed_spec(NTOK, D), fixed_spec(*MODS_E), slot_spec(1, NTOK)],
        [xin, pe, mods, bias],
        pieces,
        [fixed_out((D, 128), BF16)] + [slot_out(slots, (NTOK, D), F32)] * 2 + [slot_out(slots, s, k) for s, k in SAVES],
        weight_scratch(pieces, TOKW + 128),
        BLOCK_MACS,
    )


def side_forward(slots, ids, h_in, mask, pe, misc, mods, pieces):
    return call(
        side_forward_kernel,
        slots,
        ids,
        [slot_spec(NTOK, D), slot_spec(NTOK, 1), fixed_spec(NTOK, D), fixed_spec(D, 128), fixed_spec(*MODS_R)],
        [h_in, mask, pe, misc, mods],
        pieces,
        [slot_out(slots, (NTOK, D), F32)] * 2 + [slot_out(slots, s, k) for s, k in SAVES],
        weight_scratch(pieces, TOKW),
        BLOCK_MACS,
    )


def dec_both(slots, ids, coef, h_in, noise, misc, mods, pieces, split):
    outs = grad_outs(split, CW)
    pair = 2 if slots % 2 == 0 else 1
    return call(
        lambda n, *refs: dec_kernel(n, len(outs), *refs),
        slots,
        ids,
        [SMEM, slot_spec(NTOK, D, together=pair), slot_spec(NTOK, 128, together=pair), fixed_spec(D, 128), fixed_spec(*MODS_R)],
        [coef, h_in, noise, misc, mods],
        pieces,
        [slot_out(slots, (NTOK, D), F32, pair), fixed_out((8, 8 * D), F32), fixed_out((D, 128), F32), fixed_out((8, 128), F32)] + outs,
        weight_scratch(pieces, TOKW) + grad_scratch(TOKW, pair) + [pltpu.VMEM((pair,) + s, k) for s, k in SAVES],
        3 * BLOCK_MACS,
        pair,
    )


def side_backward(slots, ids, d_out, h_in, mask, mods, saves, pieces, split):
    outs = grad_outs(split, CW)
    return call(
        lambda n, *refs: side_backward_kernel(n, len(outs), *refs),
        slots,
        ids,
        [slot_spec(NTOK, D), slot_spec(NTOK, D), slot_spec(NTOK, 1), fixed_spec(*MODS_R)] + [slot_spec(*s) for s, _ in SAVES],
        [d_out, h_in, mask, mods] + list(saves),
        pieces,
        [slot_out(slots, (NTOK, D), F32), fixed_out((8, 6 * D), F32), fixed_out((8, D), F32)] + outs,
        weight_scratch(pieces, TOKW) + grad_scratch(TOKW),
        2 * BLOCK_MACS,
    )


def enc_backward(slots, ids, d_out, h_in, xin, mods, dmisc, dtok, saves, pieces, split):
    outs = grad_outs(split, CW + 128)
    return call(
        lambda n, *refs: enc_backward_kernel(n, len(outs), *refs),
        slots,
        ids,
        [slot_spec(NTOK, D), slot_spec(NTOK, D), slot_spec(NTOK, 128), fixed_spec(*MODS_E), fixed_spec(D, 128), fixed_spec(8, D)]
        + [slot_spec(*s) for s, _ in SAVES],
        [d_out, h_in, xin, mods, dmisc, dtok] + list(saves),
        pieces,
        [fixed_out((8, 6 * D), F32)] + outs,
        weight_scratch(pieces, TOKW + 128) + grad_scratch(TOKW + 128),
        2 * BLOCK_MACS,
    )


def assign(nf, slots, me, packed, tone, ttwo, classes):
    lats, rows = packed.shape[0], tone.shape[0]
    out = [
        ((8, NTOK * PIN + NTOK), BF16),
        ((8, 128), F32),
        ((D, lats), F32),
        ((rows, lats), F32),
        ((rows, lats), F32),
        ((rows, lats), BF16),
        ((lats, FREQ), BF16),
        ((lats, 1024), BF16),
        ((lats, 8), BF16),
    ]
    vmem = pl.BlockSpec(memory_space=pltpu.VMEM)
    return pl.pallas_call(
        functools.partial(assign_kernel, nf, slots),
        in_specs=[SMEM] + [vmem] * 5,
        out_specs=[vmem] * len(out),
        out_shape=[jax.ShapeDtypeStruct(s, k) for s, k in out],
        compiler_params=pltpu.CompilerParams(vmem_limit_bytes=VMEM_LIMIT),
    )(me, packed, jnp.asarray(feature_table()), tone, ttwo, classes)


def silu_slope(val):
    s = jax.nn.sigmoid(val)
    return s * (1.0 + val * (1.0 - s))


def adam(master, first_m, second, grad_in):
    first_new = beta_one * first_m + (1.0 - beta_one) * grad_in
    second_new = beta_two * second + (1.0 - beta_two) * grad_in * grad_in
    first_hat = first_new / (1.0 - beta_one**STEP)
    second_hat = second_new / (1.0 - beta_two**STEP)
    master_new = master - learn_rate * (first_hat / (jnp.sqrt(second_hat) + adam_eps) + weight_decay * master)
    return [master_new, first_new, second_new]


def grad_core(dw, *deps):
    if len(dw) == 1:
        return dw
    keep, send = dw
    if deps:
        send = after(send, *deps)
    return [keep, swap(send, "fsdp", 1)]


def grad_dp(parts):
    if len(parts) == 1:
        return parts
    keep, got = parts
    me = lax.axis_index("dp")

    def piece(k):
        return lax.dynamic_index_in_dim(keep, me ^ k, 0, False).astype(F32) + lax.dynamic_index_in_dim(got, me ^ k, 0, False).astype(F32)

    return [piece(0).astype(BF16)] + [swap(piece(k).astype(BF16), "dp", k) for k in (1, 2, 3)]


def grad_sum(parts):
    if len(parts) == 1:
        return parts[0]
    return sum(p.astype(F32) for p in parts)


def grad_z(part):
    if part.shape[0] == CHUNKS and part.shape[1] == D:
        part = lax.psum_scatter(part, "fsdp", scatter_dimension=1, tiled=True)
        return reduce_stage(part, 0, "dp", 1, CHUNKS, BF16).astype(BF16)
    return reduce_stage(part, 0, "fsdp", 2, 4, BF16).astype(BF16)


def dp_share(val):
    rows = val.shape[0]
    return reduce_stage(val.reshape(rows, CHUNKS, -1).transpose(1, 0, 2), 0, "dp", 1, CHUNKS, BF16).astype(BF16)


def columns(parts, lo, hi):
    return jnp.concatenate([parts[j, :, lo:hi] for j in range(CHUNKS)], axis=1)


def on_device(latents, noise, timesteps, labels, patch_mask, counts, owners, tables_w, tables_m, tables_v, rows_w, rows_m, rows_v, down_w, down_m, down_v):
    nd, nf = lax.axis_size("dp"), lax.axis_size("fsdp")
    me_d, me_f = lax.axis_index("dp"), lax.axis_index("fsdp")
    rows = tables_w.shape[0]
    micro, per = latents.shape[0], latents.shape[1]
    slots = micro * per
    split = small_mesh(rows)

    steps = timesteps.reshape(slots)
    names = labels.reshape(slots)
    plan = jnp.take(jnp.asarray(plan_table()), steps, axis=0)
    used = (jnp.arange(per)[None, :] < counts).astype(jnp.int32).reshape(slots)
    x_zero, eps = latents.reshape(slots, NTOK * PIN), noise.reshape(slots, NTOK * PIN)
    x_in = (plan[:, 0:1] * x_zero + plan[:, 1:2] * eps).astype(BF16)
    words = jnp.stack([used, steps // 32, steps % 32, names // 32, names % 32], axis=1).astype(BF16)
    words = jnp.concatenate([words, jnp.zeros((slots, 3), BF16), plan[:, 8:].astype(BF16)], axis=1)
    packed = jnp.concatenate([x_in, patch_mask.reshape(slots, NTOK).astype(BF16), words], axis=1)
    packed = jnp.pad(packed, ((0, 8 - slots), (0, 0)))
    eps = jnp.pad(eps.astype(BF16), ((0, 8 - slots), (0, 0)))
    packed = gather(packed, "fsdp").reshape(nf * 8, -1)
    wholes = []

    rows_b, down_b, tables_b = rows_w.astype(BF16), down_w.astype(BF16), tables_w.astype(BF16)
    head_at = D + 3 * STRIDE + 2 * D
    gap = jnp.zeros((rows, 16), BF16)
    misc_own = jnp.concatenate(
        [tables_b[:, : PIN + 1], gap[:, :15], rows_b[:, head_at : head_at + PIN], gap, rows_b[:, head_at + PIN : head_at + 2 * PIN], gap, gap, gap],
        axis=1,
    )
    for b in range(3):
        at = D + b * STRIDE
        row_part, down_part = rows_b[:, at : at + 4 * D + FF], down_b[:, b * FF : (b + 1) * FF]
        cols = [row_part[:, :CW], row_part[:, CW : 2 * CW], row_part[:, 2 * CW :], down_part[:, :D], down_part[:, D:]]
        if b == 0 and split:
            cols = [cols[0], misc_own, cols[1], misc_own, cols[2], cols[3], misc_own, cols[4], misc_own]
        elif b == 0:
            cols = cols + [misc_own]
        whole = jnp.concatenate(cols, axis=1)
        wholes.append(whole)
    enc_z = gather_z(wholes[0]) if split else None
    late_w = gather_whole(jnp.concatenate(wholes[1:], axis=1))

    w_tone = tables_b[:, PIN + 1 : PIN + 1 + FREQ]
    class_tab = jnp.pad(tables_b[:, PIN + 1 + FREQ :], ((0, 0), (0, 1024 - CLASSES)))
    w_ttwo = rows_b[:, :D]
    ada_at = [D + b * STRIDE + 4 * D + FF for b in range(3)]
    fin_at = D + 3 * STRIDE
    w_ada = jnp.concatenate([rows_b[:, a : a + 6 * D] for a in ada_at] + [rows_b[:, fin_at : fin_at + 2 * D]], axis=1)
    me = me_f.astype(jnp.int32).reshape(1)
    mine, info, c_part, c_own, a_pre, a_act, feat, hot, pick = assign(nf, slots, me, packed, w_tone, w_ttwo, class_tab)
    cond = reduce_parts(c_part.reshape(nf, rows, nf * 8), "fsdp", F32) + c_own
    s_cond = jax.nn.silu(cond).astype(BF16)
    mods_e = reduce_parts(dot_tn(s_cond, w_ada[:, : 6 * D]).reshape(nf, 8, 6 * D), "fsdp", BF16)
    if split:
        enc_w = gather_core(after(gather_dp(after(enc_z, c_part)), s_cond))
    else:
        enc_w = gather_whole(wholes[0])
    mods_r = reduce_open(dot_tn(s_cond, w_ada[:, 6 * D :]).reshape(nf, 8, 14 * D), "fsdp", BF16)

    work = jnp.sum(info[:, 0]).astype(jnp.int32)
    ids = jnp.stack([work, me_d.astype(jnp.int32), (me_f % 2).astype(jnp.int32)])
    coef = jnp.stack([info[:, 8 + 3 * k] + info[:, 9 + 3 * k] + info[:, 10 + 3 * k] for k in range(3)], axis=1)
    size = NTOK * PIN
    x_in = jnp.pad(mine[:slots, :size].reshape(slots, NTOK, PIN), ((0, 0), (0, 0), (0, 128 - PIN)))
    masked = mine[:slots, size:].astype(F32)
    bias = (-1e9 * masked)[:, None, :]
    mask_col = masked[:, :, None]
    pe = jnp.asarray(position_table())

    last = len(axis_stages("fsdp")) - 1
    level = gather_open(after(eps, s_cond), "fsdp", last)
    misc, h0, h_enc, *save_e = enc_forward(slots, ids, x_in, pe, mods_e, bias, enc_w)
    mods_r = total_of(tie(mods_r, misc))
    eps = gather_close(tie(level, misc), "fsdp", last)
    for at in range(last):
        level = gather_open(eps, "fsdp", at)
        if at < last - 1:
            eps = gather_close(level, "fsdp", at)
    hs, h_side, *save_s = side_forward(slots, ids, h_enc, mask_col, pe, misc, mods_r, late_w)
    eps = gather_close(tie(level, hs), "fsdp", last - 1)
    eps = eps.transpose(tuple(reversed(range(last))) + tuple(range(last, last + 3))).reshape(nf * 8, size)
    eps = dot_tn(pick, eps)[:slots].reshape(slots, NTOK, PIN)
    eps = jnp.pad(eps, ((0, 0), (0, 0), (32, 96 - PIN)))

    d_side, dmod_d, dmisc, loss, *dw_d = dec_both(slots, ids, coef, h_side, eps, misc, mods_r, late_w, False)
    mine_d = lax.psum_scatter(dw_d[0], "fsdp", scatter_dimension=1, tiled=True)
    d_enc, dmod_s, dtok, *dw_s = side_backward(slots, ids, d_side, hs, mask_col, mods_r, save_s, late_w, split)
    part_s = grad_dp(grad_core(dw_s))
    d_enc = after(d_enc, part_s[0])
    dmod_e, *dw_e = enc_backward(slots, ids, d_enc, h0, x_in, mods_e, dmisc, dtok, save_e, enc_w, split)
    total_s = grad_sum(tie(part_s, dmod_e, mine_d))
    dmods = jnp.concatenate([dmod_e, dmod_s, dmod_d], axis=1).astype(BF16)
    level = gather_open(after(dmods, total_s), "fsdp", 0)
    core_e = grad_core(dw_e, total_s)
    part_e = grad_dp(core_e)

    level = tie(level, part_e[0])
    for at in range(last):
        level = gather_open(gather_close(level, "fsdp", at), "fsdp", at + 1)
    dm_all = gather_shape(gather_close(level, "fsdp", last), "fsdp", dmods.shape).reshape(nf * 8, -1)
    d_cond = dot_nt(w_ada, dm_all) * silu_slope(cond)
    d_cond_all = gather(d_cond.astype(BF16), "fsdp").reshape(D, nf * 8)
    d_apre = (dot(w_ttwo, d_cond_all) * silu_slope(a_pre)).astype(BF16)
    g_class = jnp.dot(d_cond, hot.astype(F32), precision=lax.Precision.HIGHEST, preferred_element_type=F32)
    kinds = [dot(s_cond, dm_all), dot_nt(a_act, d_cond_all), dot(d_apre, feat), g_class, jnp.zeros((rows, 384), F32)]
    kinds = jnp.concatenate([k.astype(BF16) for k in kinds], axis=1).reshape(rows, CHUNKS, -1).transpose(1, 0, 2)

    g_side = grad_z(after(total_s, d_cond)) if split else grad_z(total_s)
    total_e = grad_sum(tie(part_e, d_cond_all))
    g_enc = grad_z(total_e)
    others = after(jnp.concatenate([mine_d, kinds], axis=2), total_e)
    g_other = total_of(reduce_open(others, "dp", BF16)).astype(BF16)
    parts = jnp.concatenate([g_enc, g_side, g_other], axis=1)
    squares = jnp.sum(jnp.square(parts.astype(F32)))
    norm_sq, loss_sum, count = sum_all(jnp.stack([squares, jnp.sum(loss), jnp.sum(used).astype(F32)]), ("fsdp", "dp"))
    full = gather(parts, "dp")
    scale = 1.0 / (count * (NTOK * PIN))
    loss_out = loss_sum * scale
    grad_norm = jnp.sqrt(norm_sq) * scale
    factor = scale * jnp.minimum(1.0, clip_level / (grad_norm + 1e-06))

    up = 4 * D + FF
    wide_e = CW + 128
    f_enc, small = columns(full, 0, CW), full[0, :, CW:wide_e]
    f_side, f_dec = columns(full, wide_e, wide_e + CW), columns(full, wide_e + CW, wide_e + 2 * CW)
    f_rest = columns(full, wide_e + 2 * CW, full.shape[2])
    at = 20 * D
    ttwo, tone, klass = f_rest[:, at : at + D], f_rest[:, at + D : at + D + FREQ], f_rest[:, at + D + FREQ : at + D + FREQ + CLASSES]
    rows_g = [ttwo, f_enc[:, :up], f_rest[:, : 6 * D], f_side[:, :up], f_rest[:, 6 * D : 12 * D], f_dec[:, :up], f_rest[:, 12 * D : 20 * D]]
    rows_g = jnp.concatenate(rows_g + [small[:, 32 : 32 + PIN], small[:, 64 : 64 + PIN]], axis=1)
    down_g = jnp.concatenate([blk[:, up:] for blk in (f_enc, f_side, f_dec)], axis=1)
    tables_g = jnp.concatenate([small[:, : PIN + 1], tone, klass], axis=1)
    results = adam(tables_w, tables_m, tables_v, factor * tables_g.astype(F32))

    def own(val):
        size = val.shape[1] // nd
        return lax.dynamic_slice_in_dim(val, me_d * size, size, 1)

    results += adam(own(rows_w), own(rows_m), own(rows_v), factor * own(rows_g).astype(F32))
    results += adam(own(down_w), own(down_m), own(down_v), factor * own(down_g).astype(F32))
    return tuple([loss_out, grad_norm] + results)


def solution(mesh):
    lat = P(None, ("dp", "fsdp"), None)
    num = P(None, ("dp", "fsdp"))
    row = P("fsdp", None)
    both = P("fsdp", "dp")
    return jax.shard_map(
        on_device,
        mesh=mesh,
        in_specs=(lat, lat, num, num, lat, num, P()) + (row,) * 9,
        out_specs=(P(), P()) + (row,) * 3 + (both,) * 6,
        check_vma=False,
    )
```
